32 devices in a mesh: ctx: 8 (over y, x, core), tp: 4 (over z).
Axes of the slice: x: 2, y: 2, z: 4, core: 2. Of those that a mesh axis runs over, the one named last changes fastest.
Arguments:
- queries: float32 [2048, 2048], P('ctx', 'tp'), may hold values from -6 to 6
- key_vectors: float32 [2048, 2048], P('ctx', 'tp'), may hold values from -6 to 6
- values: float32 [2048, 4096], P('ctx', 'tp'), may hold values from -6 to 6
- decays: float32 [32, 2048], P('tp', 'ctx'), may hold values from 0.5 to 0.99995
- strengths: float32 [32, 2048], P('tp', 'ctx'), may hold values from 0.0001 to 0.95
- out_gate: float32 [2048, 4096], P('ctx', 'tp'), may hold values from -6 to 6
- norm_gain: float32 [128], replicated, may hold values from 0.5 to 1.5
- out_weight: float32 [4096, 2048], P('tp'), may hold values from -0.09375 to 0.09375
Outputs:
- layer_out: float32 [2048, 2048], P(('ctx', 'tp'))
The draws below stay inside these ranges and needn't reach their ends.
All inputs are finite; a program needn't handle non-finite values.
Results may differ from the reference program's by a relative error of at most 0.0003.
Values sent between devices are 32-bit elements; how exact they have to be, the bound alone decides.
No kernel may reach another device: no remote copies, remote signals or barrier semaphores. Data moves between devices by JAX's collectives and lax.ppermute only.
A program may use at most 128 MiB of HBM per device.

```python
import math
import jax
import jax.numpy as jnp
from jax import lax

D = 2048
HK = 16
OUTPUT_HEAD_NUM = 32
DK = 128
DV = 128
GROUP = 64
TOK_DEV = 256
SEQUENCE_LENGTH = 2048


def slow_heads(key, share):
    return jax.random.uniform(jax.random.fold_in(key, 17), (OUTPUT_HEAD_NUM,)) < share


def rough_factor(key, shape_now):
    return jnp.exp(jax.random.uniform(key, shape_now, jnp.float32, -math.log(2.0), math.log(2.0)))


def draw_decays(key, part):
    slow = slow_heads(key, 0.5)
    key = jax.random.fold_in(key, 1)
    first, second, middle_multiplier, last_multiplier = jax.random.split(key, 4)
    rough = rough_factor(first, (OUTPUT_HEAD_NUM, SEQUENCE_LENGTH))
    device_factor = jnp.exp(jax.random.uniform(second, (OUTPUT_HEAD_NUM, SEQUENCE_LENGTH // TOK_DEV, 1), jnp.float32, -math.log(2.0), math.log(2.0)))
    device_factor = jnp.broadcast_to(device_factor, (OUTPUT_HEAD_NUM, SEQUENCE_LENGTH // TOK_DEV, TOK_DEV)).reshape(OUTPUT_HEAD_NUM, SEQUENCE_LENGTH)
    rate = rough * device_factor
    slow_value = jnp.minimum(jnp.exp(-0.5 * rate / SEQUENCE_LENGTH), 0.99995)
    fast_value = jnp.exp(-rate / 40.0)
    forget_coefficients = jnp.where(slow[:, None], slow_value, fast_value)
    trajectory_segment = jax.random.uniform(middle_multiplier, (OUTPUT_HEAD_NUM, SEQUENCE_LENGTH)) < 2.0 / SEQUENCE_LENGTH
    segment_target_matrix = jax.random.uniform(last_multiplier, (OUTPUT_HEAD_NUM, SEQUENCE_LENGTH), jnp.float32, 0.5, 0.8)
    return jnp.where(trajectory_segment, jnp.minimum(forget_coefficients, segment_target_matrix), forget_coefficients).astype(jnp.float32)


def draw_strengths(key, part):
    slow = slow_heads(key, 0.5)
    key = jax.random.fold_in(key, 2)
    rough = rough_factor(key, (OUTPUT_HEAD_NUM, SEQUENCE_LENGTH))
    slow_value = 0.3 * rough * DK / SEQUENCE_LENGTH
    fast_value = jnp.minimum(0.45 * rough, 0.95)
    return jnp.where(slow[:, None], slow_value, fast_value).astype(jnp.float32)


def levels(own_key, shape, pieces, smallest, top_value):
    loudness = 1.0
    for dim, parts in pieces:
        draws = jax.random.uniform(jax.random.fold_in(jax.random.fold_in(own_key, 6), dim), (parts,), jnp.float32, smallest / len(pieces), top_value / len(pieces))
        loudness = loudness * jnp.repeat(jnp.exp(draws), shape[dim] // parts).reshape((-1,) + (1,) * (len(shape) - 1 - dim))
    return loudness


def normal_values(key, dims, deviation, limit, cuts=(), kind=jnp.bfloat16):
    level = levels(key, dims, cuts, -0.22, 0.18) if cuts else 1.0
    result = jax.random.normal(key, dims, jnp.float32) * deviation * level
    return jnp.minimum(jnp.maximum(result, -limit), limit).astype(kind)


def setup_inputs(seed: int = 0) -> dict:
    keys = jax.random.split(jax.random.key(seed), 9)
    return {
        "queries": normal_values(keys[0], (SEQUENCE_LENGTH, HK * DK), 1.0, 6.0, ((0, 8), (1, 4)), jnp.float32),
        "key_vectors": normal_values(keys[1], (SEQUENCE_LENGTH, HK * DK), 1.0, 6.0, ((0, 8), (1, 4)), jnp.float32),
        "values": normal_values(keys[2], (SEQUENCE_LENGTH, OUTPUT_HEAD_NUM * DV), 1.0, 6.0, ((0, 8), (1, 4)), jnp.float32),
        "decays": draw_decays(jax.random.fold_in(keys[8], 71), 0),
        "strengths": draw_strengths(jax.random.fold_in(keys[8], 71), 0),
        "out_gate": normal_values(keys[5], (SEQUENCE_LENGTH, OUTPUT_HEAD_NUM * DV), 1.0, 6.0, ((0, 8), (1, 4)), jnp.float32),
        "norm_gain": jnp.clip(1.0 + 0.1 * jax.random.normal(keys[6], (DV,), jnp.float32), 0.5, 1.5),
        "out_weight": normal_values(keys[7], (OUTPUT_HEAD_NUM * DV, D), (OUTPUT_HEAD_NUM * DV) ** -0.5, 0.09375, ((0, 4),), jnp.float32),
    }


TOP_PRECISION = lax.Precision.HIGHEST

def unit_heads(matrix, nheads, hwidth):
    shaped = matrix.reshape(matrix.shape[0], nheads, hwidth)
    return shaped * lax.rsqrt(lax.optimization_barrier(jnp.sum(shaped * shaped, axis=-1, keepdims=True)) + 1e-06)

def group_pieces(q_unit, k_unit, value_rows, decay_rows, strength_rows, block_len):
    tokens_here, key_heads, key_width = k_unit.shape
    value_heads = value_rows.shape[1]
    value_width = value_rows.shape[2]
    repeat = value_heads // key_heads
    blocks = tokens_here // block_len

    def by_head(tensor, width_now):
        return tensor.transpose(1, 0, 2).reshape(tensor.shape[1], blocks, block_len, width_now)
    queries_h = jnp.repeat(by_head(q_unit, key_width), repeat, axis=0) * key_width ** (-0.5)
    keys_h = jnp.repeat(by_head(k_unit, key_width), repeat, axis=0)
    values_h = by_head(value_rows, value_width)
    cumlog = jnp.cumsum(jnp.log(decay_rows).reshape(value_heads, blocks, block_len), axis=-1)
    weights_b = strength_rows.reshape(value_heads, blocks, block_len)
    row_index = lax.broadcasted_iota(jnp.int32, (block_len, block_len), 0)
    col_index = lax.broadcasted_iota(jnp.int32, (block_len, block_len), 1)
    strict = row_index > col_index
    inclusive = row_index >= col_index
    spread = cumlog[..., :, None] - cumlog[..., None, :]
    damp_strict = jnp.where(strict, jnp.exp(jnp.where(strict, spread, 0.0)), 0.0)
    damp_incl = jnp.where(inclusive, jnp.exp(jnp.where(inclusive, spread, 0.0)), 0.0)
    gram = jnp.einsum('hnid,hnjd->hnij', keys_h, keys_h, precision=TOP_PRECISION)
    lower = weights_b[..., :, None] * gram * damp_strict
    identity = jnp.eye(block_len, dtype=jnp.float32)
    inverse = identity - lower
    power = lower
    for level in range(block_len.bit_length() - 2):
        power = jnp.einsum('hnij,hnjk->hnik', power, power, precision=TOP_PRECISION)
        inverse = jnp.einsum('hnij,hnjk->hnik', inverse, identity + power, precision=TOP_PRECISION)
    scaled_keys = (weights_b * jnp.exp(cumlog))[..., None] * keys_h
    w_fac = jnp.einsum('hnij,hnjd->hnid', inverse, scaled_keys, precision=TOP_PRECISION)
    update_factor = jnp.einsum('hnij,hnjd->hnid', inverse, weights_b[..., None] * values_h, precision=TOP_PRECISION)
    scores = jnp.einsum('hnid,hnjd->hnij', queries_h, keys_h, precision=TOP_PRECISION) * damp_incl
    q_decayed = jnp.exp(cumlog)[..., None] * queries_h
    k_ending = jnp.exp(cumlog[..., -1:] - cumlog)[..., None] * keys_h
    end_decay = jnp.exp(cumlog[..., -1])
    return (w_fac, update_factor, scores, q_decayed, k_ending, end_decay)

def block_outputs(states, w_fac, update_factor, scores, q_decayed):
    fresh = update_factor - jnp.einsum('hnid,hnde->hnie', w_fac, states, precision=TOP_PRECISION)
    core = jnp.einsum('hnid,hnde->hnie', q_decayed, states, precision=TOP_PRECISION)
    core = core + jnp.einsum('hnij,hnje->hnie', scores, fresh, precision=TOP_PRECISION)
    return (core, fresh)

def gated_norm(core, out_gate, norm_gain):
    scaled = core * lax.rsqrt(lax.optimization_barrier(jnp.mean(core * core, axis=-1, keepdims=True)) + 1e-06) * norm_gain
    return scaled.reshape(core.shape[0], -1) * jax.nn.silu(out_gate)

def reference(queries, key_vectors, values, decays, strengths, out_gate, norm_gain, out_weight):
    q_unit = unit_heads(queries, HK, DK)
    k_unit = unit_heads(key_vectors, HK, DK)
    value_rows = values.reshape(SEQUENCE_LENGTH, OUTPUT_HEAD_NUM, DV)
    blocks = SEQUENCE_LENGTH // GROUP

    def advance(state, index):
        begin = (index * GROUP).astype(jnp.int32)
        w_fac, update_factor, scores, q_dec, key_final, end_decay = group_pieces(lax.dynamic_slice_in_dim(q_unit, begin, GROUP, 0), lax.dynamic_slice_in_dim(k_unit, begin, GROUP, 0), lax.dynamic_slice_in_dim(value_rows, begin, GROUP, 0), lax.dynamic_slice_in_dim(decays, begin, GROUP, 1), lax.dynamic_slice_in_dim(strengths, begin, GROUP, 1), GROUP)
        core, fresh = block_outputs(state[:, None], w_fac, update_factor, scores, q_dec)
        new_state = end_decay[:, 0, None, None] * state
        new_state = new_state + jnp.einsum('hjd,hje->hde', key_final[:, 0], fresh[:, 0], precision=TOP_PRECISION)
        return (new_state, core[:, 0])
    initial = jnp.zeros((OUTPUT_HEAD_NUM, DK, DV), jnp.float32)
    final_state, cores = lax.scan(advance, initial, jnp.arange(blocks, dtype=jnp.int32))
    core = cores.transpose(1, 0, 2, 3).reshape(OUTPUT_HEAD_NUM, SEQUENCE_LENGTH, DV).transpose(1, 0, 2)
    normed = gated_norm(core, out_gate, norm_gain)
    return jnp.dot(normed, out_weight, precision=TOP_PRECISION, preferred_element_type=jnp.float32)
```

```python
import functools
import typing

import jax
import jax.numpy as jnp
from jax import lax
from jax.experimental import pallas as pl
from jax.experimental.pallas import tpu as pltpu
from jax.sharding import PartitionSpec as P

DK = 128
DV = 128
BLOCK = 128
SMALL = 32
BAND = 256
WEIGHT_ROWS = 128
MOST_VMEM = 56
SCAN_VMEM = 51
WEIGHT_VMEM = 40
FIRST_VMEM = 24
LATER_VMEM = 24
HEADS_AT_ONCE = 4
EPS = 1e-06


HBM = pl.BlockSpec(memory_space=pltpu.HBM)
VMEM = pl.BlockSpec(memory_space=pltpu.VMEM)


def dot(left, right):
    return jnp.dot(left, right, precision=lax.Precision.HIGH, preferred_element_type=jnp.float32)


def dot_transposed(left, right):
    return lax.dot_general(
        left,
        right,
        (((1,), (1,)), ((), ())),
        precision=lax.Precision.HIGH,
        preferred_element_type=jnp.float32,
    )


def iota(shape, dim):
    return lax.broadcasted_iota(jnp.int32, shape, dim)


def unit(rows):
    return rows * lax.rsqrt(jnp.sum(rows * rows, axis=-1, keepdims=True) + EPS)


def cumulative_logs(decays):
    tokens = decays.shape[1]
    upto = jnp.where(iota((tokens, tokens), 0) <= iota((tokens, tokens), 1), 1.0, 0.0)
    rows = jnp.dot(
        jnp.log(decays), upto, precision=lax.Precision.HIGHEST, preferred_element_type=jnp.float32
    )
    return rows, rows.T


def spread_diagonal(packed):
    size = packed.shape[0]
    place = iota(packed.shape, 1) // size
    return jnp.concatenate(
        [jnp.where(place == block, packed, 0.0) for block in range(BLOCK // size)], axis=0
    )


def lower_inverses(lowers):
    row = iota((SMALL, BLOCK), 0)
    lane = iota((SMALL, BLOCK), 1)
    column = lane % SMALL
    place = lane // SMALL
    eye = jnp.where(row == column, 1.0, 0.0)
    in_8 = row // 8 == column // 8
    in_16 = row // 16 == column // 16
    packed = []
    for lower in lowers:
        blocks = jnp.zeros((SMALL, BLOCK), jnp.float32)
        for block in range(BLOCK // SMALL):
            blocks = jnp.where(place == block, lower[block * SMALL : (block + 1) * SMALL], blocks)
        packed.append(blocks)
    nil = [jnp.where(in_8, blocks, 0.0) for blocks in packed]
    nil_2 = [dot(n, spread_diagonal(n)) for n in nil]
    wide_2 = [spread_diagonal(n) for n in nil_2]
    start = [eye - n for n in nil]
    nil_4 = [dot(n, w) for n, w in zip(nil_2, wide_2)]
    start = [s + dot(s, w) for s, w in zip(start, wide_2)]
    inv = [s + dot(s, spread_diagonal(n)) for s, n in zip(start, nil_4)]
    step_16 = [spread_diagonal(jnp.where(in_16 & ~in_8, blocks, 0.0)) for blocks in packed]
    half = [jnp.concatenate([d[8:16], d[24:32]], axis=0) for d in inv]
    half = [dot(h, w) for h, w in zip(half, step_16)]
    half = [dot(h, spread_diagonal(d)) for h, d in zip(half, inv)]
    inv = [
        jnp.concatenate([d[:8], d[8:16] - h[:8], d[16:24], d[24:] - h[8:]], axis=0)
        for d, h in zip(inv, half)
    ]
    step_32 = [spread_diagonal(jnp.where(in_16, 0.0, blocks)) for blocks in packed]
    half = [dot(d[16:], w) for d, w in zip(inv, step_32)]
    half = [dot(h, spread_diagonal(d)) for h, d in zip(half, inv)]
    inv = [jnp.concatenate([d[:16], d[16:] - h], axis=0) for d, h in zip(inv, half)]
    odd = place % 2 == 1
    zeros = jnp.zeros((SMALL, BLOCK), jnp.float32)
    low = [jnp.where(odd, d, 0.0) for d in inv]
    wide = [
        spread_diagonal(jnp.concatenate([jnp.where(odd, 0.0, d), l], axis=0)) for d, l in zip(inv, low)
    ]
    step_64 = [
        spread_diagonal(
            jnp.concatenate(
                [
                    zeros,
                    jnp.where(
                        place == 0, lower[32:64], jnp.where(place == 2, lower[96:128], 0.0)
                    ),
                ],
                axis=0,
            )
        )
        for lower in lowers
    ]
    half = [dot(l, w) for l, w in zip(low, step_64)]
    half = [dot(h, w) for h, w in zip(half, wide)]
    inv = [
        jnp.concatenate([jnp.where(odd, 0.0, d), l - h], axis=0) for d, l, h in zip(inv, low, half)
    ]
    left = iota((64, BLOCK), 1) < 64
    low = [jnp.where(left, 0.0, d) for d in inv]
    wide = [jnp.concatenate([jnp.where(left, d, 0.0), l], axis=0) for d, l in zip(inv, low)]
    step_128 = [
        jnp.concatenate(
            [jnp.zeros((64, BLOCK), jnp.float32), jnp.where(left, lower[64:], 0.0)], axis=0
        )
        for lower in lowers
    ]
    half = [dot(l, w) for l, w in zip(low, step_128)]
    half = [dot(h, w) for h, w in zip(half, wide)]
    return [jnp.concatenate([w[:64], w[64:] - h], axis=0) for w, h in zip(wide, half)]


def block(index):
    return slice(index * BLOCK, (index + 1) * BLOCK)


def fetch(pairs, sems):
    copies = [pltpu.make_async_copy(src, dst, sems.at[i]) for i, (src, dst) in enumerate(pairs)]
    for copy in copies:
        copy.start()
    return copies


def partner(place, swap):
    return lax.axis_index("ctx") ^ place if swap else place


def summary_kernel(decay_hbm, strength_hbm, k_hbm, v_hbm, factor_hbm, *rest, swap):
    *summaries, decay_ref, strength_ref, k_ref, v_ref, sems, factor_ref, summary_ref, out_sems = rest
    copies = fetch(
        [(decay_hbm, decay_ref), (strength_hbm, strength_ref), (k_hbm, k_ref), (v_hbm, v_ref)], sems
    )
    for copy in copies[:3]:
        copy.wait()
    tokens = k_ref.shape[0]
    key_heads = k_ref.shape[1] // DK
    value_heads = v_ref.shape[1] // DV
    repeat = value_heads // key_heads
    blocks = tokens // BLOCK
    rows, columns = cumulative_logs(decay_ref[...])
    strengths = strength_ref[...].T
    strict = iota((BLOCK, BLOCK), 0) > iota((BLOCK, BLOCK), 1)
    eye = jnp.where(iota((BLOCK, DK + DV), 0) == iota((BLOCK, DK + DV), 1), 1.0, 0.0)
    leaving = []
    for first in range(0, value_heads, HEADS_AT_ONCE):
        heads = range(first, min(first + HEADS_AT_ONCE, value_heads))
        keys = {}
        gram = {}
        for key_head in sorted({head // repeat for head in heads}):
            unit_rows = unit(k_ref[:, key_head * DK : (key_head + 1) * DK])
            keys[key_head] = [unit_rows[block(p)] for p in range(blocks)]
            gram[key_head] = {
                (p, r): dot_transposed(keys[key_head][p], keys[key_head][r])
                for p in range(blocks)
                for r in range(p + 1)
            }
        lower = {}
        for head in heads:
            for p in range(blocks):
                at = columns[block(p), head : head + 1]
                weight = strengths[block(p), head : head + 1]
                for r in range(p + 1):
                    spread = at - rows[head : head + 1, block(r)]
                    if p == r:
                        damp = jnp.where(strict, jnp.exp(jnp.where(strict, spread, 0.0)), 0.0)
                    else:
                        damp = jnp.exp(spread)
                    lower[head, p, r] = weight * gram[head // repeat][p, r] * damp
        inverse = lower_inverses([lower[head, p, p] for head in heads for p in range(blocks)])
        inverse = {
            (head, p): inverse[i * blocks + p] for i, head in enumerate(heads) for p in range(blocks)
        }
        if first == 0:
            copies[3].wait()
        factors = {}
        for p in range(blocks):
            for head in heads:
                at = columns[block(p), head : head + 1]
                weight = strengths[block(p), head : head + 1]
                right = jnp.concatenate(
                    [
                        keys[head // repeat][p] * (-weight * jnp.exp(at)),
                        v_ref[block(p), head * DV : (head + 1) * DV] * weight,
                    ],
                    axis=1,
                )
                for r in range(p):
                    right = right - dot(lower[head, p, r], factors[head, r])
                factors[head, p] = dot(inverse[head, p], right)
                factor_ref[head, block(p), :] = factors[head, p]
        flipped = {key_head: [k.T for k in keys[key_head]] for key_head in keys}
        for head in heads:
            last = rows[head : head + 1, tokens - 1 : tokens]
            total = jnp.exp(last) * eye
            for p in range(blocks):
                ending = jnp.exp(last - columns[block(p), head : head + 1])
                total = total + dot(flipped[head // repeat][p], factors[head, p] * ending)
            summary_ref[head] = total
        group = pl.ds(first, len(heads))
        leaving.append(
            pltpu.make_async_copy(
                factor_ref.at[group], factor_hbm.at[group], out_sems.at[len(leaving)]
            )
        )
        leaving[-1].start()
    for place, out_ref in enumerate(summaries):
        out_ref[...] = summary_ref[partner(place, swap)]
    for copy in leaving:
        copy.wait()


def output_kernel(
    decay_hbm,
    q_hbm,
    k_hbm,
    factor_hbm,
    map_hbm,
    decay_ref,
    q_ref,
    k_ref,
    factor_ref,
    sems,
    map_ref,
    out_sems,
):
    copies = fetch(
        [(decay_hbm, decay_ref), (q_hbm, q_ref), (k_hbm, k_ref), (factor_hbm, factor_ref)], sems
    )
    leaving = []
    for copy in copies[:3]:
        copy.wait()
    tokens = q_ref.shape[0]
    key_heads = q_ref.shape[1] // DK
    value_heads = factor_ref.shape[0]
    repeat = value_heads // key_heads
    blocks = tokens // BLOCK
    rows, columns = cumulative_logs(decay_ref[...])
    inclusive = iota((BLOCK, BLOCK), 0) >= iota((BLOCK, BLOCK), 1)
    for key_head in range(key_heads):
        lanes = slice(key_head * DK, (key_head + 1) * DK)
        queries = unit(q_ref[:, lanes]) * DK**-0.5
        keys = unit(k_ref[:, lanes])
        for p in range(blocks):
            scores = [dot_transposed(queries[block(p)], keys[block(r)]) for r in range(p + 1)]
            if key_head == 0 and p == 0:
                copies[3].wait()
            for head in range(key_head * repeat, (key_head + 1) * repeat):
                at = columns[block(p), head : head + 1]
                total = jnp.concatenate(
                    [queries[block(p)] * jnp.exp(at), jnp.zeros((BLOCK, DV), jnp.float32)], axis=1
                )
                for r in range(p + 1):
                    spread = at - rows[head : head + 1, block(r)]
                    if p == r:
                        damp = jnp.where(inclusive, jnp.exp(jnp.where(inclusive, spread, 0.0)), 0.0)
                    else:
                        damp = jnp.exp(spread)
                    total = total + dot(scores[r] * damp, factor_ref[head, block(r), :])
                map_ref[head, block(p), :] = total
        group = pl.ds(key_head * repeat, repeat)
        leaving.append(
            pltpu.make_async_copy(map_ref.at[group], map_hbm.at[group], out_sems.at[key_head])
        )
        leaving[-1].start()
    for copy in leaving:
        copy.wait()


def scan_kernel(held_ref, entry_ref):
    count, held, key_width, width = entry_ref.shape
    for head in range(held):
        state = jnp.zeros((key_width, width), jnp.float32)
        entry_ref[0, head] = state
        for source in range(count - 1):
            added = held_ref[source, head, :, key_width:]
            if source:
                added = added + dot(held_ref[source, head, :, :key_width], state)
            state = added
            entry_ref[source + 1, head] = state


def ordered_scan_kernel(own_hbm, *rest):
    *arrays, held_ref, entry_ref, sems = rest
    count = entry_ref.shape[0]
    held, own_entry_hbm, entries = arrays[: count - 1], arrays[count - 1], arrays[count:]
    here = partner(0, True)
    own = pltpu.make_async_copy(own_hbm, held_ref.at[here], sems.at[0])
    own.start()
    for i, summary in enumerate(held):
        held_ref[partner(i + 1, True)] = summary[...]
    own.wait()
    state = jnp.zeros(entry_ref.shape[1:], jnp.float32)
    entry_ref[0] = state
    for source in range(count - 1):
        added = held_ref[source, :, DK:]
        if source:
            added = added + dot(held_ref[source, :, :DK], state)
        state = added
        entry_ref[source + 1] = state
    own = pltpu.make_async_copy(entry_ref.at[here], own_entry_hbm, sems.at[1])
    own.start()
    for i, entry in enumerate(entries):
        entry[...] = entry_ref[partner(i + 1, True)]
    own.wait()


def split(value):
    high = value.astype(jnp.bfloat16)
    return high, (value - high.astype(jnp.float32)).astype(jnp.bfloat16)


def weight_kernel(weight_ref, parts_ref):
    parts_ref[0], parts_ref[1] = split(weight_ref[...])


def projection_kernel(map_hbm, gate_hbm, gain_ref, parts_ref, own_hbm, *rest, pieces, swap):
    *arrays, map_ref, gate_ref, state_ref, high_ref, low_ref, gate_sems, map_sems, state_sems = rest
    outs = arrays[-len(pieces) :]
    states = arrays[: -len(pieces)]
    heads = state_ref.shape[0]
    rows = outs[0].shape[0]
    blocks = sorted({index for index, _ in pieces})
    own = fetch([(own_hbm, state_ref.at[partner(0, swap.heads)])], state_sems)
    places = []
    for i, index in enumerate(blocks):
        start = (lax.axis_index("tp") ^ index) * rows if swap.rows else index * rows
        places.append((pl.ds(pl.multiple_of(start, rows), rows), pl.ds(i * rows, rows)))
    gates = fetch([(gate_hbm.at[s, :], gate_ref.at[t, :]) for s, t in places], gate_sems)
    maps = fetch(
        [
            (map_hbm.at[head, s, :], map_ref.at[head, t, :])
            for head in range(heads)
            for s, t in places
        ],
        map_sems,
    )
    for i, state in enumerate(states):
        state_ref[partner(i + 1, swap.heads)] = state[...]
    for copy in own + gates:
        copy.wait()
    gain = gain_ref[...]
    for head in range(heads):
        lanes = slice(head * DV, (head + 1) * DV)
        gate = gate_ref[:, lanes]
        factor = gate / (1.0 + jnp.exp(-gate)) * gain
        for copy in maps[head * len(blocks) : (head + 1) * len(blocks)]:
            copy.wait()
        core = map_ref[head, :, DK:] + dot(map_ref[head, :, :DK], state_ref[head])
        scale = lax.rsqrt(jnp.mean(core * core, axis=-1, keepdims=True) + EPS)
        high_ref[:, lanes], low_ref[:, lanes] = split(core * scale * factor)
    total = len(blocks) * rows
    for band in range(0, parts_ref.shape[2], BAND):
        lanes = slice(band, band + BAND)
        both = jnp.concatenate([high_ref[...], low_ref[...]], axis=0)
        sums = jnp.dot(both, parts_ref[0, :, lanes], preferred_element_type=jnp.float32)
        last = jnp.dot(high_ref[...], parts_ref[1, :, lanes], preferred_element_type=jnp.float32)
        result = sums[:total] + (sums[total:] + last)
        for (index, start), out_ref in zip(pieces, outs):
            if start <= band < start + out_ref.shape[1]:
                at = blocks.index(index) * rows
                out_ref[:, band - start : band - start + BAND] = result[at : at + rows]


def shape(*dims):
    return jax.ShapeDtypeStruct(dims, jnp.float32)


def params(mebibytes):
    return pltpu.CompilerParams(vmem_limit_bytes=mebibytes * 1024 * 1024)


def cost(flops, *arrays):
    return pl.CostEstimate(
        flops=flops, bytes_accessed=4 * sum(a.size for a in arrays), transcendentals=0
    )


def partners_swap(arrays, axis):
    count = len(arrays)
    away = [
        lax.ppermute(arrays[i], axis, [(d, d ^ i) for d in range(count)])
        for i in range(count - 1, 0, -1)
    ]
    return [arrays[0]] + away[::-1]


class Swap(typing.NamedTuple):
    heads: bool
    rows: bool


def swap_is_possible(heads, count):
    return heads == count and count & (count - 1) == 0 and count <= 8


def entering_states(summaries, swap, beside, after):
    heads = len(summaries)
    count = lax.axis_size("ctx")
    if swap:
        held = partners_swap(summaries, "ctx")
        held, beside = lax.optimization_barrier((held, beside))
        entry = shape(DK, DV)
        entries = pl.pallas_call(
            ordered_scan_kernel,
            in_specs=[HBM] + [VMEM] * (count - 1),
            out_specs=[HBM] + [VMEM] * (count - 1),
            out_shape=[entry] * count,
            scratch_shapes=[
                pltpu.VMEM((count, DK, DK + DV), jnp.float32),
                pltpu.VMEM((count, DK, DV), jnp.float32),
                pltpu.SemaphoreType.DMA((2,)),
            ],
            compiler_params=params(SCAN_VMEM),
            name="state_scan",
        )(*held)
        entries, after = lax.optimization_barrier((entries, after))
        return partners_swap(entries, "ctx"), beside, after
    parts = max(1, count // heads)
    per_owner = max(1, heads // count)
    width = DV // parts
    groups = heads // per_owner
    summary = jnp.stack(summaries)
    maps = summary[:, :, :DK].reshape(groups, 1, per_owner, DK, DK)
    maps = jnp.broadcast_to(maps, (groups, parts, per_owner, DK, DK))
    adds = summary[:, :, DK:].reshape(groups, per_owner, DK, parts, width)
    payload = jnp.concatenate([maps, adds.transpose(0, 3, 1, 2, 4)], axis=-1)
    payload = payload.reshape(count, per_owner, DK, DK + width)
    held = lax.all_to_all(payload, "ctx", split_axis=0, concat_axis=0, tiled=True)
    entries = pl.pallas_call(
        scan_kernel,
        out_shape=shape(count, per_owner, DK, width),
        compiler_params=params(32),
        name="state_scan",
    )(held)
    back = lax.all_to_all(entries, "ctx", split_axis=0, concat_axis=0, tiled=True)
    back = back.reshape(groups, parts, per_owner, DK, width).transpose(0, 2, 3, 1, 4)
    back = back.reshape(heads, DK, DV)
    return [back[head] for head in range(heads)], beside, after


def project_and_sum(project, columns, axis):
    count = lax.axis_size(axis)
    if count != 4:
        whole = jnp.concatenate(project([(i, 0, columns) for i in range(count)], LATER_VMEM), axis=0)
        return lax.psum_scatter(whole, axis, scatter_dimension=0, tiled=True)
    half = columns // 2
    halves = [(0, half), (half, half)]
    *first, opposite = project([(3, *h) for h in halves] + [(3, 0, columns)], FIRST_VMEM)
    from_end = [lax.ppermute(piece, axis, [(0, 1), (3, 2)]) for piece in first]
    from_inner = lax.ppermute(opposite, axis, [(1, 2), (2, 1)])
    *across, near, own = project(
        [(2, *h) for h in halves] + [(1, 0, columns), (0, 0, columns)], LATER_VMEM
    )
    from_end[1], near = lax.optimization_barrier((from_end[1], near))
    from_across = [
        lax.ppermute(piece + came, axis, [(i, i ^ 2) for i in range(4)])
        for piece, came in zip(across, from_end)
    ]
    from_near = lax.ppermute(near, axis, [(i, i ^ 1) for i in range(4)])
    return (own + from_inner) + (from_near + jnp.concatenate(from_across, axis=1))


def per_device(queries, key_vectors, values, decays, strengths, out_gate, norm_gain, out_weight):
    tokens = queries.shape[0]
    heads = values.shape[1] // DV
    depth, columns = out_weight.shape
    rows = tokens // lax.axis_size("tp")
    gain = norm_gain.reshape(1, DV)
    swap = Swap(
        heads=swap_is_possible(heads, lax.axis_size("ctx")), rows=lax.axis_size("tp") == 4
    )

    def buffers(*arrays):
        return [pltpu.VMEM(a.shape, a.dtype) for a in arrays] + [
            pltpu.SemaphoreType.DMA((len(arrays),))
        ]

    factor_shape = shape(heads, tokens, DK + DV)
    groups = pl.cdiv(heads, HEADS_AT_ONCE)
    factors, *summaries = pl.pallas_call(
        functools.partial(summary_kernel, swap=swap.heads),
        in_specs=[HBM] * 4,
        out_specs=[HBM] + [VMEM] * heads,
        out_shape=[factor_shape] + [shape(DK, DK + DV)] * heads,
        scratch_shapes=buffers(decays, strengths, key_vectors, values)
        + [pltpu.VMEM(factor_shape.shape, jnp.float32), pltpu.VMEM((heads, DK, DK + DV), jnp.float32)]
        + [pltpu.SemaphoreType.DMA((groups,))],
        compiler_params=params(MOST_VMEM),
        name="state_summary",
    )(decays, strengths, key_vectors, values)
    maps = pl.pallas_call(
        output_kernel,
        in_specs=[HBM] * 4,
        out_specs=HBM,
        out_shape=factor_shape,
        scratch_shapes=buffers(decays, queries, key_vectors, factors)
        + [pltpu.VMEM(factor_shape.shape, jnp.float32)]
        + [pltpu.SemaphoreType.DMA((queries.shape[1] // DK,))],
        compiler_params=params(MOST_VMEM),
        cost_estimate=cost(3 * 2 * heads * tokens * tokens * 384, factors, factors, queries),
        name="output_maps",
    )(decays, queries, key_vectors, factors)
    states, maps, weights = entering_states(summaries, swap.heads, maps, out_weight)
    parts = pl.pallas_call(
        weight_kernel,
        grid=(depth // WEIGHT_ROWS,),
        in_specs=[pl.BlockSpec((WEIGHT_ROWS, columns), lambda i: (i, 0))],
        out_specs=pl.BlockSpec((2, WEIGHT_ROWS, columns), lambda i: (0, i, 0)),
        out_shape=jax.ShapeDtypeStruct((2, depth, columns), jnp.bfloat16),
        compiler_params=params(WEIGHT_VMEM),
        cost_estimate=cost(6 * weights.size, weights, weights),
        name="weight_parts",
    )(weights)

    def project(pieces, vmem):
        total = len({piece[0] for piece in pieces}) * rows
        normed = pltpu.VMEM((total, depth), jnp.bfloat16)
        counts = (total // rows, heads * total // rows, 1)
        return pl.pallas_call(
            functools.partial(
                projection_kernel, pieces=[(index, start) for index, start, _ in pieces], swap=swap
            ),
            in_specs=[HBM] * 2 + [VMEM] * 2 + [HBM] + [VMEM] * (heads - 1),
            out_shape=[shape(rows, width) for _, _, width in pieces],
            scratch_shapes=[
                pltpu.VMEM((heads, total, DK + DV), jnp.float32),
                pltpu.VMEM((total, heads * DV), jnp.float32),
                pltpu.VMEM((heads, DK, DV), jnp.float32),
                normed,
                normed,
            ]
            + [pltpu.SemaphoreType.DMA((n,)) for n in counts],
            compiler_params=params(vmem),
            cost_estimate=cost(3 * 2 * total * depth * columns, out_weight),
            name="projection",
        )(maps, out_gate, gain, parts, *states)

    return project_and_sum(project, columns, "tp")


def solution(mesh):
    return jax.shard_map(
        per_device,
        mesh=mesh,
        in_specs=(
            P("ctx", "tp"),
            P("ctx", "tp"),
            P("ctx", "tp"),
            P("tp", "ctx"),
            P("tp", "ctx"),
            P("ctx", "tp"),
            P(),
            P("tp", None),
        ),
        out_specs=P(("ctx", "tp"), None),
        check_vma=False,
    )
```

```python
import functools
import typing

import jax
import jax.numpy as jnp
from jax import lax
from jax.experimental import pallas as pl
from jax.experimental.pallas import tpu as pltpu
from jax.sharding import PartitionSpec as P

DK = 128
DV = 128
BLOCK = 128
SMALL = 32
BAND = 256
WEIGHT_ROWS = 128
MOST_VMEM = 56
SCAN_VMEM = 52.25
WEIGHT_VMEM = 40
FIRST_VMEM = 24
LATER_VMEM = 24
HEADS_AT_ONCE = 8
EPS = 1e-06


HBM = pl.BlockSpec(memory_space=pltpu.HBM)
VMEM = pl.BlockSpec(memory_space=pltpu.VMEM)


def dot(left, right):
    return jnp.dot(left, right, precision=lax.Precision.HIGH, preferred_element_type=jnp.float32)


def dot_transposed(left, right):
    return lax.dot_general(
        left,
        right,
        (((1,), (1,)), ((), ())),
        precision=lax.Precision.HIGH,
        preferred_element_type=jnp.float32,
    )


def iota(shape, dim):
    return lax.broadcasted_iota(jnp.int32, shape, dim)


def unit(rows):
    return rows * lax.rsqrt(jnp.sum(rows * rows, axis=-1, keepdims=True) + EPS)


def cumulative_logs(decays):
    tokens = decays.shape[1]
    upto = jnp.where(iota((tokens, tokens), 0) <= iota((tokens, tokens), 1), 1.0, 0.0)
    rows = jnp.dot(
        jnp.log(decays), upto, precision=lax.Precision.HIGHEST, preferred_element_type=jnp.float32
    )
    return rows, rows.T


def spread_diagonal(packed):
    size = packed.shape[0]
    place = iota(packed.shape, 1) // size
    return jnp.concatenate(
        [jnp.where(place == block, packed, 0.0) for block in range(BLOCK // size)], axis=0
    )


def lower_inverses(lowers):
    row = iota((SMALL, BLOCK), 0)
    lane = iota((SMALL, BLOCK), 1)
    column = lane % SMALL
    place = lane // SMALL
    eye = jnp.where(row == column, 1.0, 0.0)
    in_8 = row // 8 == column // 8
    in_16 = row // 16 == column // 16
    packed = []
    for lower in lowers:
        blocks = jnp.zeros((SMALL, BLOCK), jnp.float32)
        for block in range(BLOCK // SMALL):
            blocks = jnp.where(place == block, lower[block * SMALL : (block + 1) * SMALL], blocks)
        packed.append(blocks)
    nil = [jnp.where(in_8, blocks, 0.0) for blocks in packed]
    nil_2 = [dot(n, spread_diagonal(n)) for n in nil]
    wide_2 = [spread_diagonal(n) for n in nil_2]
    start = [eye - n for n in nil]
    nil_4 = [dot(n, w) for n, w in zip(nil_2, wide_2)]
    start = [s + dot(s, w) for s, w in zip(start, wide_2)]
    inv = [s + dot(s, spread_diagonal(n)) for s, n in zip(start, nil_4)]
    step_16 = [spread_diagonal(jnp.where(in_16 & ~in_8, blocks, 0.0)) for blocks in packed]
    half = [jnp.concatenate([d[8:16], d[24:32]], axis=0) for d in inv]
    half = [dot(h, w) for h, w in zip(half, step_16)]
    half = [dot(h, spread_diagonal(d)) for h, d in zip(half, inv)]
    inv = [
        jnp.concatenate([d[:8], d[8:16] - h[:8], d[16:24], d[24:] - h[8:]], axis=0)
        for d, h in zip(inv, half)
    ]
    step_32 = [spread_diagonal(jnp.where(in_16, 0.0, blocks)) for blocks in packed]
    half = [dot(d[16:], w) for d, w in zip(inv, step_32)]
    half = [dot(h, spread_diagonal(d)) for h, d in zip(half, inv)]
    inv = [jnp.concatenate([d[:16], d[16:] - h], axis=0) for d, h in zip(inv, half)]
    odd = place % 2 == 1
    zeros = jnp.zeros((SMALL, BLOCK), jnp.float32)
    low = [jnp.where(odd, d, 0.0) for d in inv]
    wide = [
        spread_diagonal(jnp.concatenate([jnp.where(odd, 0.0, d), l], axis=0)) for d, l in zip(inv, low)
    ]
    step_64 = [
        spread_diagonal(
            jnp.concatenate(
                [
                    zeros,
                    jnp.where(
                        place == 0, lower[32:64], jnp.where(place == 2, lower[96:128], 0.0)
                    ),
                ],
                axis=0,
            )
        )
        for lower in lowers
    ]
    half = [dot(l, w) for l, w in zip(low, step_64)]
    half = [dot(h, w) for h, w in zip(half, wide)]
    inv = [
        jnp.concatenate([jnp.where(odd, 0.0, d), l - h], axis=0) for d, l, h in zip(inv, low, half)
    ]
    left = iota((64, BLOCK), 1) < 64
    low = [jnp.where(left, 0.0, d) for d in inv]
    wide = [jnp.concatenate([jnp.where(left, d, 0.0), l], axis=0) for d, l in zip(inv, low)]
    step_128 = [
        jnp.concatenate(
            [jnp.zeros((64, BLOCK), jnp.float32), jnp.where(left, lower[64:], 0.0)], axis=0
        )
        for lower in lowers
    ]
    half = [dot(l, w) for l, w in zip(low, step_128)]
    half = [dot(h, w) for h, w in zip(half, wide)]
    return [jnp.concatenate([w[:64], w[64:] - h], axis=0) for w, h in zip(wide, half)]


def block(index):
    return slice(index * BLOCK, (index + 1) * BLOCK)


def fetch(pairs, sems):
    copies = [pltpu.make_async_copy(src, dst, sems.at[i]) for i, (src, dst) in enumerate(pairs)]
    for copy in copies:
        copy.start()
    return copies


def partner(place, swap):
    return lax.axis_index("ctx") ^ place if swap else place


def summary_kernel(decay_hbm, strength_hbm, k_hbm, v_hbm, factor_hbm, *rest, swap):
    *summaries, decay_ref, strength_ref, k_ref, v_ref, sems, factor_ref, summary_ref, out_sems = rest
    copies = fetch(
        [(decay_hbm, decay_ref), (strength_hbm, strength_ref), (k_hbm, k_ref), (v_hbm, v_ref)], sems
    )
    for copy in copies[:3]:
        copy.wait()
    tokens = k_ref.shape[0]
    key_heads = k_ref.shape[1] // DK
    value_heads = v_ref.shape[1] // DV
    repeat = value_heads // key_heads
    blocks = tokens // BLOCK
    rows, columns = cumulative_logs(decay_ref[...])
    strengths = strength_ref[...].T
    strict = iota((BLOCK, BLOCK), 0) > iota((BLOCK, BLOCK), 1)
    eye = jnp.where(iota((BLOCK, DK + DV), 0) == iota((BLOCK, DK + DV), 1), 1.0, 0.0)
    leaving = []
    for first in range(0, value_heads, HEADS_AT_ONCE):
        heads = range(first, min(first + HEADS_AT_ONCE, value_heads))
        keys = {}
        gram = {}
        for key_head in sorted({head // repeat for head in heads}):
            unit_rows = unit(k_ref[:, key_head * DK : (key_head + 1) * DK])
            keys[key_head] = [unit_rows[block(p)] for p in range(blocks)]
            gram[key_head] = {
                (p, r): dot_transposed(keys[key_head][p], keys[key_head][r])
                for p in range(blocks)
                for r in range(p + 1)
            }
        lower = {}
        for head in heads:
            for p in range(blocks):
                at = columns[block(p), head : head + 1]
                weight = strengths[block(p), head : head + 1]
                for r in range(p + 1):
                    spread = at - rows[head : head + 1, block(r)]
                    if p == r:
                        damp = jnp.where(strict, jnp.exp(jnp.where(strict, spread, 0.0)), 0.0)
                    else:
                        damp = jnp.exp(spread)
                    lower[head, p, r] = weight * gram[head // repeat][p, r] * damp
        inverse = lower_inverses([lower[head, p, p] for head in heads for p in range(blocks)])
        inverse = {
            (head, p): inverse[i * blocks + p] for i, head in enumerate(heads) for p in range(blocks)
        }
        if first == 0:
            copies[3].wait()
        factors = {}
        for p in range(blocks):
            for head in heads:
                at = columns[block(p), head : head + 1]
                weight = strengths[block(p), head : head + 1]
                right = jnp.concatenate(
                    [
                        keys[head // repeat][p] * (-weight * jnp.exp(at)),
                        v_ref[block(p), head * DV : (head + 1) * DV] * weight,
                    ],
                    axis=1,
                )
                for r in range(p):
                    right = right - dot(lower[head, p, r], factors[head, r])
                factors[head, p] = dot(inverse[head, p], right)
                factor_ref[head, block(p), :] = factors[head, p]
        flipped = {key_head: [k.T for k in keys[key_head]] for key_head in keys}
        for head in heads:
            last = rows[head : head + 1, tokens - 1 : tokens]
            total = jnp.exp(last) * eye
            for p in range(blocks):
                ending = jnp.exp(last - columns[block(p), head : head + 1])
                total = total + dot(flipped[head // repeat][p], factors[head, p] * ending)
            summary_ref[head] = total
        group = pl.ds(first, len(heads))
        leaving.append(
            pltpu.make_async_copy(
                factor_ref.at[group], factor_hbm.at[group], out_sems.at[len(leaving)]
            )
        )
        leaving[-1].start()
    for place, out_ref in enumerate(summaries):
        out_ref[...] = summary_ref[partner(place, swap)]
    for copy in leaving:
        copy.wait()


def output_kernel(
    decay_hbm,
    q_hbm,
    k_hbm,
    factor_hbm,
    map_hbm,
    decay_ref,
    q_ref,
    k_ref,
    factor_ref,
    sems,
    map_ref,
    out_sems,
):
    copies = fetch(
        [(decay_hbm, decay_ref), (q_hbm, q_ref), (k_hbm, k_ref), (factor_hbm, factor_ref)], sems
    )
    leaving = []
    for copy in copies[:3]:
        copy.wait()
    tokens = q_ref.shape[0]
    key_heads = q_ref.shape[1] // DK
    value_heads = factor_ref.shape[0]
    repeat = value_heads // key_heads
    blocks = tokens // BLOCK
    rows, columns = cumulative_logs(decay_ref[...])
    inclusive = iota((BLOCK, BLOCK), 0) >= iota((BLOCK, BLOCK), 1)
    for key_head in range(key_heads):
        lanes = slice(key_head * DK, (key_head + 1) * DK)
        queries = unit(q_ref[:, lanes]) * DK**-0.5
        keys = unit(k_ref[:, lanes])
        for p in range(blocks):
            scores = [dot_transposed(queries[block(p)], keys[block(r)]) for r in range(p + 1)]
            if key_head == 0 and p == 0:
                copies[3].wait()
            for head in range(key_head * repeat, (key_head + 1) * repeat):
                at = columns[block(p), head : head + 1]
                total = jnp.concatenate(
                    [queries[block(p)] * jnp.exp(at), jnp.zeros((BLOCK, DV), jnp.float32)], axis=1
                )
                for r in range(p + 1):
                    spread = at - rows[head : head + 1, block(r)]
                    if p == r:
                        damp = jnp.where(inclusive, jnp.exp(jnp.where(inclusive, spread, 0.0)), 0.0)
                    else:
                        damp = jnp.exp(spread)
                    total = total + dot(scores[r] * damp, factor_ref[head, block(r), :])
                map_ref[head, block(p), :] = total
        group = pl.ds(key_head * repeat, repeat)
        leaving.append(
            pltpu.make_async_copy(map_ref.at[group], map_hbm.at[group], out_sems.at[key_head])
        )
        leaving[-1].start()
    for copy in leaving:
        copy.wait()


def scan_kernel(held_ref, entry_ref):
    count, held, key_width, width = entry_ref.shape
    for head in range(held):
        state = jnp.zeros((key_width, width), jnp.float32)
        entry_ref[0, head] = state
        for source in range(count - 1):
            added = held_ref[source, head, :, key_width:]
            if source:
                added = added + dot(held_ref[source, head, :, :key_width], state)
            state = added
            entry_ref[source + 1, head] = state


def ordered_scan_kernel(own_hbm, *rest):
    *arrays, held_ref, entry_ref, sems = rest
    count = entry_ref.shape[0]
    held, own_entry_hbm, entries = arrays[: count - 1], arrays[count - 1], arrays[count:]
    here = partner(0, True)
    own = pltpu.make_async_copy(own_hbm, held_ref.at[here], sems.at[0])
    own.start()
    for i, summary in enumerate(held):
        held_ref[partner(i + 1, True)] = summary[...]
    own.wait()
    state = jnp.zeros(entry_ref.shape[1:], jnp.float32)
    entry_ref[0] = state
    for source in range(count - 1):
        added = held_ref[source, :, DK:]
        if source:
            added = added + dot(held_ref[source, :, :DK], state)
        state = added
        entry_ref[source + 1] = state
    own = pltpu.make_async_copy(entry_ref.at[here], own_entry_hbm, sems.at[1])
    own.start()
    for i, entry in enumerate(entries):
        entry[...] = entry_ref[partner(i + 1, True)]
    own.wait()


def split(value):
    high = value.astype(jnp.bfloat16)
    return high, (value - high.astype(jnp.float32)).astype(jnp.bfloat16)


def weight_kernel(weight_hbm, parts_ref, weight_ref, sems):
    bands = [pl.ds(row, WEIGHT_ROWS) for row in range(0, weight_ref.shape[0], WEIGHT_ROWS)]
    copies = fetch([(weight_hbm.at[band, :], weight_ref.at[band, :]) for band in bands], sems)
    for copy, band in zip(copies, bands):
        copy.wait()
        parts_ref[0, band, :], parts_ref[1, band, :] = split(weight_ref[band, :])


def projection_kernel(map_hbm, gate_hbm, gain_ref, parts_ref, own_hbm, *rest, pieces, swap):
    *arrays, map_ref, gate_ref, state_ref, high_ref, low_ref, gate_sems, map_sems, state_sems = rest
    outs = arrays[-len(pieces) :]
    states = arrays[: -len(pieces)]
    heads = state_ref.shape[0]
    rows = outs[0].shape[0]
    blocks = sorted({index for index, _ in pieces})
    own = fetch([(own_hbm, state_ref.at[partner(0, swap.heads)])], state_sems)
    places = []
    for i, index in enumerate(blocks):
        start = (lax.axis_index("tp") ^ index) * rows if swap.rows else index * rows
        places.append((pl.ds(pl.multiple_of(start, rows), rows), pl.ds(i * rows, rows)))
    gates = fetch([(gate_hbm.at[s, :], gate_ref.at[t, :]) for s, t in places], gate_sems)
    maps = fetch(
        [
            (map_hbm.at[head, s, :], map_ref.at[head, t, :])
            for head in range(heads)
            for s, t in places
        ],
        map_sems,
    )
    for i, state in enumerate(states):
        state_ref[partner(i + 1, swap.heads)] = state[...]
    for copy in own + gates:
        copy.wait()
    gain = gain_ref[...]
    for head in range(heads):
        lanes = slice(head * DV, (head + 1) * DV)
        gate = gate_ref[:, lanes]
        factor = gate / (1.0 + jnp.exp(-gate)) * gain
        for copy in maps[head * len(blocks) : (head + 1) * len(blocks)]:
            copy.wait()
        core = map_ref[head, :, DK:] + dot(map_ref[head, :, :DK], state_ref[head])
        scale = lax.rsqrt(jnp.mean(core * core, axis=-1, keepdims=True) + EPS)
        high_ref[:, lanes], low_ref[:, lanes] = split(core * scale * factor)
    total = len(blocks) * rows
    for band in range(0, parts_ref.shape[2], BAND):
        lanes = slice(band, band + BAND)
        both = jnp.concatenate([high_ref[...], low_ref[...]], axis=0)
        sums = jnp.dot(both, parts_ref[0, :, lanes], preferred_element_type=jnp.float32)
        last = jnp.dot(high_ref[...], parts_ref[1, :, lanes], preferred_element_type=jnp.float32)
        result = sums[:total] + (sums[total:] + last)
        for (index, start), out_ref in zip(pieces, outs):
            if start <= band < start + out_ref.shape[1]:
                at = blocks.index(index) * rows
                out_ref[:, band - start : band - start + BAND] = result[at : at + rows]


def shape(*dims):
    return jax.ShapeDtypeStruct(dims, jnp.float32)


def params(mebibytes):
    return pltpu.CompilerParams(vmem_limit_bytes=int(mebibytes * 1024 * 1024))


def cost(flops, *arrays):
    return pl.CostEstimate(
        flops=flops, bytes_accessed=4 * sum(a.size for a in arrays), transcendentals=0
    )


def partners_swap(arrays, axis):
    count = len(arrays)
    away = [
        lax.ppermute(arrays[i], axis, [(d, d ^ i) for d in range(count)])
        for i in range(count - 1, 0, -1)
    ]
    return [arrays[0]] + away[::-1]


class Swap(typing.NamedTuple):
    heads: bool
    rows: bool


def swap_is_possible(heads, count):
    return heads == count and count & (count - 1) == 0 and count <= 8


def entering_states(summaries, swap, beside, after):
    heads = len(summaries)
    count = lax.axis_size("ctx")
    if swap:
        held = partners_swap(summaries, "ctx")
        held, beside = lax.optimization_barrier((held, beside))
        entry = shape(DK, DV)
        entries = pl.pallas_call(
            ordered_scan_kernel,
            in_specs=[HBM] + [VMEM] * (count - 1),
            out_specs=[HBM] + [VMEM] * (count - 1),
            out_shape=[entry] * count,
            scratch_shapes=[
                pltpu.VMEM((count, DK, DK + DV), jnp.float32),
                pltpu.VMEM((count, DK, DV), jnp.float32),
                pltpu.SemaphoreType.DMA((2,)),
            ],
            compiler_params=params(SCAN_VMEM),
            name="state_scan",
        )(*held)
        entries, after = lax.optimization_barrier((entries, after))
        return partners_swap(entries, "ctx"), beside, after
    parts = max(1, count // heads)
    per_owner = max(1, heads // count)
    width = DV // parts
    groups = heads // per_owner
    summary = jnp.stack(summaries)
    maps = summary[:, :, :DK].reshape(groups, 1, per_owner, DK, DK)
    maps = jnp.broadcast_to(maps, (groups, parts, per_owner, DK, DK))
    adds = summary[:, :, DK:].reshape(groups, per_owner, DK, parts, width)
    payload = jnp.concatenate([maps, adds.transpose(0, 3, 1, 2, 4)], axis=-1)
    payload = payload.reshape(count, per_owner, DK, DK + width)
    held = lax.all_to_all(payload, "ctx", split_axis=0, concat_axis=0, tiled=True)
    entries = pl.pallas_call(
        scan_kernel,
        out_shape=shape(count, per_owner, DK, width),
        compiler_params=params(32),
        name="state_scan",
    )(held)
    back = lax.all_to_all(entries, "ctx", split_axis=0, concat_axis=0, tiled=True)
    back = back.reshape(groups, parts, per_owner, DK, width).transpose(0, 2, 3, 1, 4)
    back = back.reshape(heads, DK, DV)
    return [back[head] for head in range(heads)], beside, after


def project_and_sum(project, columns, axis):
    count = lax.axis_size(axis)
    if count != 4:
        whole = jnp.concatenate(project([(i, 0, columns) for i in range(count)], LATER_VMEM), axis=0)
        return lax.psum_scatter(whole, axis, scatter_dimension=0, tiled=True)
    half = columns // 2
    halves = [(0, half), (half, half)]
    outward = lax.axis_index(axis) == 1
    opposite = project([(3, *h) for h in halves], FIRST_VMEM)
    steps = [
        (lax.ppermute(piece, axis, [(0, 1), (1, 2)]), lax.ppermute(piece, axis, [(3, 2), (2, 1)]))
        for piece in opposite
    ]
    *across, near, own = project(
        [(2, *h) for h in halves] + [(1, 0, columns), (0, 0, columns)], LATER_VMEM
    )
    from_end = [jnp.where(outward, up, down) for up, down in steps]
    from_inner = [jnp.where(outward, down, up) for up, down in steps]
    going = [piece + came for piece, came in zip(across, from_end)]
    going[1], near = lax.optimization_barrier((going[1], near))
    from_across = [lax.ppermute(piece, axis, [(i, i ^ 2) for i in range(4)]) for piece in going]
    from_near = lax.ppermute(near, axis, [(i, i ^ 1) for i in range(4)])
    rest = [inner + far for inner, far in zip(from_inner, from_across)]
    return (own + from_near) + jnp.concatenate(rest, axis=1)


def per_device(queries, key_vectors, values, decays, strengths, out_gate, norm_gain, out_weight):
    tokens = queries.shape[0]
    heads = values.shape[1] // DV
    depth, columns = out_weight.shape
    rows = tokens // lax.axis_size("tp")
    gain = norm_gain.reshape(1, DV)
    swap = Swap(
        heads=swap_is_possible(heads, lax.axis_size("ctx")), rows=lax.axis_size("tp") == 4
    )

    def buffers(*arrays):
        return [pltpu.VMEM(a.shape, a.dtype) for a in arrays] + [
            pltpu.SemaphoreType.DMA((len(arrays),))
        ]

    factor_shape = shape(heads, tokens, DK + DV)
    groups = pl.cdiv(heads, HEADS_AT_ONCE)
    factors, *summaries = pl.pallas_call(
        functools.partial(summary_kernel, swap=swap.heads),
        in_specs=[HBM] * 4,
        out_specs=[HBM] + [VMEM] * heads,
        out_shape=[factor_shape] + [shape(DK, DK + DV)] * heads,
        scratch_shapes=buffers(decays, strengths, key_vectors, values)
        + [pltpu.VMEM(factor_shape.shape, jnp.float32), pltpu.VMEM((heads, DK, DK + DV), jnp.float32)]
        + [pltpu.SemaphoreType.DMA((groups,))],
        compiler_params=params(MOST_VMEM),
        name="state_summary",
    )(decays, strengths, key_vectors, values)
    maps = pl.pallas_call(
        output_kernel,
        in_specs=[HBM] * 4,
        out_specs=HBM,
        out_shape=factor_shape,
        scratch_shapes=buffers(decays, queries, key_vectors, factors)
        + [pltpu.VMEM(factor_shape.shape, jnp.float32)]
        + [pltpu.SemaphoreType.DMA((queries.shape[1] // DK,))],
        compiler_params=params(MOST_VMEM),
        cost_estimate=cost(3 * 2 * heads * tokens * tokens * 384, factors, factors, queries),
        name="output_maps",
    )(decays, queries, key_vectors, factors)
    states, maps, weights = entering_states(summaries, swap.heads, maps, out_weight)
    parts = pl.pallas_call(
        weight_kernel,
        in_specs=[HBM],
        out_shape=jax.ShapeDtypeStruct((2, depth, columns), jnp.bfloat16),
        scratch_shapes=[
            pltpu.VMEM(out_weight.shape, jnp.float32),
            pltpu.SemaphoreType.DMA((depth // WEIGHT_ROWS,)),
        ],
        compiler_params=params(WEIGHT_VMEM),
        cost_estimate=cost(6 * weights.size, weights, weights),
        name="weight_parts",
    )(weights)

    def project(pieces, vmem):
        total = len({piece[0] for piece in pieces}) * rows
        normed = pltpu.VMEM((total, depth), jnp.bfloat16)
        counts = (total // rows, heads * total // rows, 1)
        return pl.pallas_call(
            functools.partial(
                projection_kernel, pieces=[(index, start) for index, start, _ in pieces], swap=swap
            ),
            in_specs=[HBM] * 2 + [VMEM] * 2 + [HBM] + [VMEM] * (heads - 1),
            out_shape=[shape(rows, width) for _, _, width in pieces],
            scratch_shapes=[
                pltpu.VMEM((heads, total, DK + DV), jnp.float32),
                pltpu.VMEM((total, heads * DV), jnp.float32),
                pltpu.VMEM((heads, DK, DV), jnp.float32),
                normed,
                normed,
            ]
            + [pltpu.SemaphoreType.DMA((n,)) for n in counts],
            compiler_params=params(vmem),
            cost_estimate=cost(3 * 2 * total * depth * columns, out_weight),
            name="projection",
        )(maps, out_gate, gain, parts, *states)

    return project_and_sum(project, columns, "tp")


def solution(mesh):
    return jax.shard_map(
        per_device,
        mesh=mesh,
        in_specs=(
            P("ctx", "tp"),
            P("ctx", "tp"),
            P("ctx", "tp"),
            P("tp", "ctx"),
            P("tp", "ctx"),
            P("ctx", "tp"),
            P(),
            P("tp", None),
        ),
        out_specs=P(("ctx", "tp"), None),
        check_vma=False,
    )
```

```python
import functools
import typing

import jax
import jax.numpy as jnp
from jax import lax
from jax.experimental import pallas as pl
from jax.experimental.pallas import tpu as pltpu
from jax.sharding import PartitionSpec as P

DK = 128
DV = 128
BLOCK = 128
SMALL = 32
BAND = 256
SWAP_ORDER = (7, 6, 3, 5, 2, 4, 1)
WEIGHT_ROWS = 128
MOST_VMEM = 56
SCAN_VMEM = 52.25
WEIGHT_VMEM = 40
FIRST_VMEM = 24
LATER_VMEM = 24
HEADS_AT_ONCE = 8
EPS = 1e-06


HBM = pl.BlockSpec(memory_space=pltpu.HBM)
VMEM = pl.BlockSpec(memory_space=pltpu.VMEM)


def dot(left, right):
    return jnp.dot(left, right, precision=lax.Precision.HIGH, preferred_element_type=jnp.float32)


def dot_transposed(left, right):
    return lax.dot_general(
        left,
        right,
        (((1,), (1,)), ((), ())),
        precision=lax.Precision.HIGH,
        preferred_element_type=jnp.float32,
    )


def iota(shape, dim):
    return lax.broadcasted_iota(jnp.int32, shape, dim)


def unit(rows):
    return rows * lax.rsqrt(jnp.sum(rows * rows, axis=-1, keepdims=True) + EPS)


def cumulative_logs(decays):
    tokens = decays.shape[1]
    upto = jnp.where(iota((tokens, tokens), 0) <= iota((tokens, tokens), 1), 1.0, 0.0)
    rows = jnp.dot(
        jnp.log(decays), upto, precision=lax.Precision.HIGHEST, preferred_element_type=jnp.float32
    )
    return rows, rows.T


def spread_diagonal(packed):
    size = packed.shape[0]
    place = iota(packed.shape, 1) // size
    return jnp.concatenate(
        [jnp.where(place == block, packed, 0.0) for block in range(BLOCK // size)], axis=0
    )


def lower_inverses(lowers):
    row = iota((SMALL, BLOCK), 0)
    lane = iota((SMALL, BLOCK), 1)
    column = lane % SMALL
    place = lane // SMALL
    eye = jnp.where(row == column, 1.0, 0.0)
    in_8 = row // 8 == column // 8
    in_16 = row // 16 == column // 16
    packed = []
    for lower in lowers:
        blocks = jnp.zeros((SMALL, BLOCK), jnp.float32)
        for block in range(BLOCK // SMALL):
            blocks = jnp.where(place == block, lower[block * SMALL : (block + 1) * SMALL], blocks)
        packed.append(blocks)
    nil = [jnp.where(in_8, blocks, 0.0) for blocks in packed]
    nil_2 = [dot(n, spread_diagonal(n)) for n in nil]
    wide_2 = [spread_diagonal(n) for n in nil_2]
    start = [eye - n for n in nil]
    nil_4 = [dot(n, w) for n, w in zip(nil_2, wide_2)]
    start = [s + dot(s, w) for s, w in zip(start, wide_2)]
    inv = [s + dot(s, spread_diagonal(n)) for s, n in zip(start, nil_4)]
    step_16 = [spread_diagonal(jnp.where(in_16 & ~in_8, blocks, 0.0)) for blocks in packed]
    half = [jnp.concatenate([d[8:16], d[24:32]], axis=0) for d in inv]
    half = [dot(h, w) for h, w in zip(half, step_16)]
    half = [dot(h, spread_diagonal(d)) for h, d in zip(half, inv)]
    inv = [
        jnp.concatenate([d[:8], d[8:16] - h[:8], d[16:24], d[24:] - h[8:]], axis=0)
        for d, h in zip(inv, half)
    ]
    step_32 = [spread_diagonal(jnp.where(in_16, 0.0, blocks)) for blocks in packed]
    half = [dot(d[16:], w) for d, w in zip(inv, step_32)]
    half = [dot(h, spread_diagonal(d)) for h, d in zip(half, inv)]
    inv = [jnp.concatenate([d[:16], d[16:] - h], axis=0) for d, h in zip(inv, half)]
    odd = place % 2 == 1
    zeros = jnp.zeros((SMALL, BLOCK), jnp.float32)
    low = [jnp.where(odd, d, 0.0) for d in inv]
    wide = [
        spread_diagonal(jnp.concatenate([jnp.where(odd, 0.0, d), l], axis=0)) for d, l in zip(inv, low)
    ]
    step_64 = [
        spread_diagonal(
            jnp.concatenate(
                [
                    zeros,
                    jnp.where(
                        place == 0, lower[32:64], jnp.where(place == 2, lower[96:128], 0.0)
                    ),
                ],
                axis=0,
            )
        )
        for lower in lowers
    ]
    half = [dot(l, w) for l, w in zip(low, step_64)]
    half = [dot(h, w) for h, w in zip(half, wide)]
    inv = [
        jnp.concatenate([jnp.where(odd, 0.0, d), l - h], axis=0) for d, l, h in zip(inv, low, half)
    ]
    left = iota((64, BLOCK), 1) < 64
    low = [jnp.where(left, 0.0, d) for d in inv]
    wide = [jnp.concatenate([jnp.where(left, d, 0.0), l], axis=0) for d, l in zip(inv, low)]
    step_128 = [
        jnp.concatenate(
            [jnp.zeros((64, BLOCK), jnp.float32), jnp.where(left, lower[64:], 0.0)], axis=0
        )
        for lower in lowers
    ]
    half = [dot(l, w) for l, w in zip(low, step_128)]
    half = [dot(h, w) for h, w in zip(half, wide)]
    return [jnp.concatenate([w[:64], w[64:] - h], axis=0) for w, h in zip(wide, half)]


def block(index):
    return slice(index * BLOCK, (index + 1) * BLOCK)


def fetch(pairs, sems):
    copies = [pltpu.make_async_copy(src, dst, sems.at[i]) for i, (src, dst) in enumerate(pairs)]
    for copy in copies:
        copy.start()
    return copies


def partner(place, swap):
    return lax.axis_index("ctx") ^ place if swap else place


def summary_kernel(decay_hbm, strength_hbm, k_hbm, v_hbm, factor_hbm, *rest, swap):
    *summaries, decay_ref, strength_ref, k_ref, v_ref, sems, factor_ref, summary_ref, out_sems = rest
    copies = fetch(
        [(decay_hbm, decay_ref), (strength_hbm, strength_ref), (k_hbm, k_ref), (v_hbm, v_ref)], sems
    )
    for copy in copies[:3]:
        copy.wait()
    tokens = k_ref.shape[0]
    key_heads = k_ref.shape[1] // DK
    value_heads = v_ref.shape[1] // DV
    repeat = value_heads // key_heads
    blocks = tokens // BLOCK
    rows, columns = cumulative_logs(decay_ref[...])
    strengths = strength_ref[...].T
    strict = iota((BLOCK, BLOCK), 0) > iota((BLOCK, BLOCK), 1)
    eye = jnp.where(iota((BLOCK, DK + DV), 0) == iota((BLOCK, DK + DV), 1), 1.0, 0.0)
    leaving = []
    for first in range(0, value_heads, HEADS_AT_ONCE):
        heads = range(first, min(first + HEADS_AT_ONCE, value_heads))
        keys = {}
        gram = {}
        for key_head in sorted({head // repeat for head in heads}):
            unit_rows = unit(k_ref[:, key_head * DK : (key_head + 1) * DK])
            keys[key_head] = [unit_rows[block(p)] for p in range(blocks)]
            gram[key_head] = {
                (p, r): dot_transposed(keys[key_head][p], keys[key_head][r])
                for p in range(blocks)
                for r in range(p + 1)
            }
        lower = {}
        for head in heads:
            for p in range(blocks):
                at = columns[block(p), head : head + 1]
                weight = strengths[block(p), head : head + 1]
                for r in range(p + 1):
                    spread = at - rows[head : head + 1, block(r)]
                    if p == r:
                        damp = jnp.where(strict, jnp.exp(jnp.where(strict, spread, 0.0)), 0.0)
                    else:
                        damp = jnp.exp(spread)
                    lower[head, p, r] = weight * gram[head // repeat][p, r] * damp
        inverse = lower_inverses([lower[head, p, p] for head in heads for p in range(blocks)])
        inverse = {
            (head, p): inverse[i * blocks + p] for i, head in enumerate(heads) for p in range(blocks)
        }
        if first == 0:
            copies[3].wait()
        factors = {}
        for p in range(blocks):
            for head in heads:
                at = columns[block(p), head : head + 1]
                weight = strengths[block(p), head : head + 1]
                right = jnp.concatenate(
                    [
                        keys[head // repeat][p] * (-weight * jnp.exp(at)),
                        v_ref[block(p), head * DV : (head + 1) * DV] * weight,
                    ],
                    axis=1,
                )
                for r in range(p):
                    right = right - dot(lower[head, p, r], factors[head, r])
                factors[head, p] = dot(inverse[head, p], right)
                factor_ref[head, block(p), :] = factors[head, p]
        flipped = {key_head: [k.T for k in keys[key_head]] for key_head in keys}
        for head in heads:
            last = rows[head : head + 1, tokens - 1 : tokens]
            total = jnp.exp(last) * eye
            for p in range(blocks):
                ending = jnp.exp(last - columns[block(p), head : head + 1])
                total = total + dot(flipped[head // repeat][p], factors[head, p] * ending)
            summary_ref[head] = total
        group = pl.ds(first, len(heads))
        leaving.append(
            pltpu.make_async_copy(
                factor_ref.at[group], factor_hbm.at[group], out_sems.at[len(leaving)]
            )
        )
        leaving[-1].start()
    if swap:
        target = factor_hbm.at[value_heads, pl.ds(0, DK)]
        leaving.append(
            pltpu.make_async_copy(summary_ref.at[partner(0, swap)], target, out_sems.at[len(leaving)])
        )
        leaving[-1].start()
    for place, out_ref in enumerate(summaries):
        out_ref[...] = summary_ref[partner(place + 1 if swap else place, swap)]
    for copy in leaving:
        copy.wait()


def output_kernel(
    decay_hbm,
    q_hbm,
    k_hbm,
    factor_hbm,
    map_hbm,
    decay_ref,
    q_ref,
    k_ref,
    factor_ref,
    sems,
    map_ref,
    out_sems,
):
    repeat = factor_ref.shape[0] // (k_hbm.shape[1] // DK)
    groups = [pl.ds(head, repeat) for head in range(0, factor_ref.shape[0], repeat)]
    copies = fetch(
        [(decay_hbm, decay_ref), (q_hbm, q_ref), (k_hbm, k_ref)]
        + [(factor_hbm.at[group], factor_ref.at[group]) for group in groups],
        sems,
    )
    leaving = []
    for copy in copies[:3]:
        copy.wait()
    tokens = q_ref.shape[0]
    key_heads = q_ref.shape[1] // DK
    value_heads = factor_ref.shape[0]
    repeat = value_heads // key_heads
    blocks = tokens // BLOCK
    rows, columns = cumulative_logs(decay_ref[...])
    inclusive = iota((BLOCK, BLOCK), 0) >= iota((BLOCK, BLOCK), 1)
    for key_head in range(key_heads):
        lanes = slice(key_head * DK, (key_head + 1) * DK)
        queries = unit(q_ref[:, lanes]) * DK**-0.5
        keys = unit(k_ref[:, lanes])
        for p in range(blocks):
            scores = [dot_transposed(queries[block(p)], keys[block(r)]) for r in range(p + 1)]
            if p == 0:
                copies[3 + key_head].wait()
            for head in range(key_head * repeat, (key_head + 1) * repeat):
                at = columns[block(p), head : head + 1]
                total = jnp.concatenate(
                    [queries[block(p)] * jnp.exp(at), jnp.zeros((BLOCK, DV), jnp.float32)], axis=1
                )
                for r in range(p + 1):
                    spread = at - rows[head : head + 1, block(r)]
                    if p == r:
                        damp = jnp.where(inclusive, jnp.exp(jnp.where(inclusive, spread, 0.0)), 0.0)
                    else:
                        damp = jnp.exp(spread)
                    total = total + dot(scores[r] * damp, factor_ref[head, block(r), :])
                map_ref[head, block(p), :] = total
        group = groups[key_head]
        leaving.append(
            pltpu.make_async_copy(map_ref.at[group], map_hbm.at[group], out_sems.at[key_head])
        )
        leaving[-1].start()
    for copy in leaving:
        copy.wait()


def scan_kernel(held_ref, entry_ref):
    count, held, key_width, width = entry_ref.shape
    for head in range(held):
        state = jnp.zeros((key_width, width), jnp.float32)
        entry_ref[0, head] = state
        for source in range(count - 1):
            added = held_ref[source, head, :, key_width:]
            if source:
                added = added + dot(held_ref[source, head, :, :key_width], state)
            state = added
            entry_ref[source + 1, head] = state


def ordered_scan_kernel(factor_hbm, *rest):
    *arrays, held_ref, entry_ref, sems = rest
    count = entry_ref.shape[0]
    held, own_entry_hbm, entries = arrays[: count - 1], arrays[count - 1], arrays[count:]
    here = partner(0, True)
    own_summary = factor_hbm.at[factor_hbm.shape[0] - 1, pl.ds(0, DK)]
    own = pltpu.make_async_copy(own_summary, held_ref.at[here], sems.at[0])
    own.start()
    for i, summary in enumerate(held):
        held_ref[partner(i + 1, True)] = summary[...]
    own.wait()
    state = jnp.zeros(entry_ref.shape[1:], jnp.float32)
    entry_ref[0] = state
    for source in range(count - 1):
        added = held_ref[source, :, DK:]
        if source:
            added = added + dot(held_ref[source, :, :DK], state)
        state = added
        entry_ref[source + 1] = state
    own = pltpu.make_async_copy(entry_ref.at[here], own_entry_hbm, sems.at[1])
    own.start()
    for i, entry in enumerate(entries):
        entry[...] = entry_ref[partner(i + 1, True)]
    own.wait()


def split(value):
    high = value.astype(jnp.bfloat16)
    return high, (value - high.astype(jnp.float32)).astype(jnp.bfloat16)


def weight_kernel(weight_hbm, parts_ref, weight_ref, sems):
    bands = [pl.ds(row, WEIGHT_ROWS) for row in range(0, weight_ref.shape[0], WEIGHT_ROWS)]
    copies = fetch([(weight_hbm.at[band, :], weight_ref.at[band, :]) for band in bands], sems)
    for copy, band in zip(copies, bands):
        copy.wait()
        parts_ref[0, band, :], parts_ref[1, band, :] = split(weight_ref[band, :])


def projection_kernel(map_hbm, gate_hbm, gain_ref, parts_ref, own_hbm, *rest, pieces, swap):
    *arrays, map_ref, gate_ref, state_ref, high_ref, low_ref, gate_sems, map_sems, state_sems = rest
    outs = arrays[-len(pieces) :]
    states = arrays[: -len(pieces)]
    heads = state_ref.shape[0]
    rows = outs[0].shape[0]
    blocks = sorted({index for index, _ in pieces})
    own = fetch([(own_hbm, state_ref.at[partner(0, swap.heads)])], state_sems)
    places = []
    for i, index in enumerate(blocks):
        start = (lax.axis_index("tp") ^ index) * rows if swap.rows else index * rows
        places.append((pl.ds(pl.multiple_of(start, rows), rows), pl.ds(i * rows, rows)))
    gates = fetch([(gate_hbm.at[s, :], gate_ref.at[t, :]) for s, t in places], gate_sems)
    maps = fetch(
        [
            (map_hbm.at[head, s, :], map_ref.at[head, t, :])
            for head in range(heads)
            for s, t in places
        ],
        map_sems,
    )
    for i, state in enumerate(states):
        state_ref[partner(i + 1, swap.heads)] = state[...]
    for copy in own + gates:
        copy.wait()
    gain = gain_ref[...]
    for head in range(heads):
        lanes = slice(head * DV, (head + 1) * DV)
        gate = gate_ref[:, lanes]
        factor = gate / (1.0 + jnp.exp(-gate)) * gain
        for copy in maps[head * len(blocks) : (head + 1) * len(blocks)]:
            copy.wait()
        core = map_ref[head, :, DK:] + dot(map_ref[head, :, :DK], state_ref[head])
        scale = lax.rsqrt(jnp.mean(core * core, axis=-1, keepdims=True) + EPS)
        high_ref[:, lanes], low_ref[:, lanes] = split(core * scale * factor)
    total = len(blocks) * rows
    for band in range(0, parts_ref.shape[2], BAND):
        lanes = slice(band, band + BAND)
        both = jnp.concatenate([high_ref[...], low_ref[...]], axis=0)
        sums = jnp.dot(both, parts_ref[0, :, lanes], preferred_element_type=jnp.float32)
        last = jnp.dot(high_ref[...], parts_ref[1, :, lanes], preferred_element_type=jnp.float32)
        result = sums[:total] + (sums[total:] + last)
        for (index, start), out_ref in zip(pieces, outs):
            if start <= band < start + out_ref.shape[1]:
                at = blocks.index(index) * rows
                out_ref[:, band - start : band - start + BAND] = result[at : at + rows]


def forward_kernel(across_ref, own_ref, up_ref, down_ref, going_ref, staying_ref):
    outward = lax.axis_index("tp") == 1
    up, down = up_ref[...], down_ref[...]
    going_ref[...] = across_ref[...] + jnp.where(outward, up, down)
    staying_ref[...] = own_ref[...] + jnp.where(outward, down, up)


def shape(*dims):
    return jax.ShapeDtypeStruct(dims, jnp.float32)


def params(mebibytes):
    return pltpu.CompilerParams(vmem_limit_bytes=int(mebibytes * 1024 * 1024))


def cost(flops, *arrays):
    return pl.CostEstimate(
        flops=flops, bytes_accessed=4 * sum(a.size for a in arrays), transcendentals=0
    )


def partners_swap(arrays, axis):
    count = len(arrays)
    arrays = list(arrays)
    for i in [i for i in SWAP_ORDER if i < count]:
        arrays[i] = lax.ppermute(arrays[i], axis, [(d, d ^ i) for d in range(count)])
    return arrays


class Swap(typing.NamedTuple):
    heads: bool
    rows: bool


def swap_is_possible(heads, count):
    return heads == count and count & (count - 1) == 0 and count <= 8


def entering_states(factors, summaries, swap, beside, after):
    heads = factors.shape[0] - 1
    count = lax.axis_size("ctx")
    if swap:
        held = partners_swap([factors, *summaries], "ctx")
        held, beside = lax.optimization_barrier((held, beside))
        entry = shape(DK, DV)
        entries = pl.pallas_call(
            ordered_scan_kernel,
            in_specs=[HBM] + [VMEM] * (count - 1),
            out_specs=[HBM] + [VMEM] * (count - 1),
            out_shape=[entry] * count,
            scratch_shapes=[
                pltpu.VMEM((count, DK, DK + DV), jnp.float32),
                pltpu.VMEM((count, DK, DV), jnp.float32),
                pltpu.SemaphoreType.DMA((2,)),
            ],
            compiler_params=params(SCAN_VMEM),
            name="state_scan",
        )(*held)
        entries, after = lax.optimization_barrier((entries, after))
        return partners_swap(entries, "ctx"), beside, after
    parts = max(1, count // heads)
    per_owner = max(1, heads // count)
    width = DV // parts
    groups = heads // per_owner
    summary = jnp.stack(summaries)
    maps = summary[:, :, :DK].reshape(groups, 1, per_owner, DK, DK)
    maps = jnp.broadcast_to(maps, (groups, parts, per_owner, DK, DK))
    adds = summary[:, :, DK:].reshape(groups, per_owner, DK, parts, width)
    payload = jnp.concatenate([maps, adds.transpose(0, 3, 1, 2, 4)], axis=-1)
    payload = payload.reshape(count, per_owner, DK, DK + width)
    held = lax.all_to_all(payload, "ctx", split_axis=0, concat_axis=0, tiled=True)
    entries = pl.pallas_call(
        scan_kernel,
        out_shape=shape(count, per_owner, DK, width),
        compiler_params=params(32),
        name="state_scan",
    )(held)
    back = lax.all_to_all(entries, "ctx", split_axis=0, concat_axis=0, tiled=True)
    back = back.reshape(groups, parts, per_owner, DK, width).transpose(0, 2, 3, 1, 4)
    back = back.reshape(heads, DK, DV)
    return [back[head] for head in range(heads)], beside, after


def project_and_sum(project, columns, axis):
    count = lax.axis_size(axis)
    if count != 4:
        whole = jnp.concatenate(project([(i, 0, columns) for i in range(count)], LATER_VMEM), axis=0)
        return lax.psum_scatter(whole, axis, scatter_dimension=0, tiled=True)
    half = columns // 2
    halves = [(0, half), (half, half)]
    opposite = project([(3, *h) for h in halves], FIRST_VMEM)
    steps = [
        (lax.ppermute(piece, axis, [(0, 1), (1, 2)]), lax.ppermute(piece, axis, [(3, 2), (2, 1)]))
        for piece in opposite
    ]
    *pieces, near = project(
        [(2, *h) for h in halves] + [(0, *h) for h in halves] + [(1, 0, columns)], LATER_VMEM
    )
    from_near = lax.ppermute(near, axis, [(i, i ^ 1) for i in range(4)])
    sums = []
    for across, own, step in zip(pieces[:2], pieces[2:], steps):
        going, staying = pl.pallas_call(
            forward_kernel,
            out_shape=[shape(*own.shape)] * 2,
            compiler_params=params(LATER_VMEM),
            name="forward",
        )(across, own, *step)
        sums.append(staying + lax.ppermute(going, axis, [(i, i ^ 2) for i in range(4)]))
    return from_near + jnp.concatenate(sums, axis=1)


def per_device(queries, key_vectors, values, decays, strengths, out_gate, norm_gain, out_weight):
    tokens = queries.shape[0]
    heads = values.shape[1] // DV
    key_heads = queries.shape[1] // DK
    depth, columns = out_weight.shape
    rows = tokens // lax.axis_size("tp")
    gain = norm_gain.reshape(1, DV)
    swap = Swap(
        heads=swap_is_possible(heads, lax.axis_size("ctx")), rows=lax.axis_size("tp") == 4
    )

    def buffers(*arrays):
        return [pltpu.VMEM(a.shape, a.dtype) for a in arrays] + [
            pltpu.SemaphoreType.DMA((len(arrays),))
        ]

    factor_shape = shape(heads, tokens, DK + DV)
    groups = pl.cdiv(heads, HEADS_AT_ONCE)
    sent = heads - 1 if swap.heads else heads
    factors, *summaries = pl.pallas_call(
        functools.partial(summary_kernel, swap=swap.heads),
        in_specs=[HBM] * 4,
        out_specs=[HBM] + [VMEM] * sent,
        out_shape=[shape(heads + 1, tokens, DK + DV)] + [shape(DK, DK + DV)] * sent,
        scratch_shapes=buffers(decays, strengths, key_vectors, values)
        + [pltpu.VMEM(factor_shape.shape, jnp.float32), pltpu.VMEM((heads, DK, DK + DV), jnp.float32)]
        + [pltpu.SemaphoreType.DMA((groups + 1,))],
        compiler_params=params(MOST_VMEM),
        name="state_summary",
    )(decays, strengths, key_vectors, values)
    maps = pl.pallas_call(
        output_kernel,
        in_specs=[HBM] * 4,
        out_specs=HBM,
        out_shape=factor_shape,
        scratch_shapes=[pltpu.VMEM(a.shape, jnp.float32) for a in (decays, queries, key_vectors)]
        + [pltpu.VMEM(factor_shape.shape, jnp.float32), pltpu.SemaphoreType.DMA((3 + key_heads,))]
        + [pltpu.VMEM(factor_shape.shape, jnp.float32), pltpu.SemaphoreType.DMA((key_heads,))],
        compiler_params=params(MOST_VMEM),
        cost_estimate=cost(3 * 2 * heads * tokens * tokens * 384, factors, factors, queries),
        name="output_maps",
    )(decays, queries, key_vectors, factors)
    states, maps, weights = entering_states(factors, summaries, swap.heads, maps, out_weight)
    parts = pl.pallas_call(
        weight_kernel,
        in_specs=[HBM],
        out_shape=jax.ShapeDtypeStruct((2, depth, columns), jnp.bfloat16),
        scratch_shapes=[
            pltpu.VMEM(out_weight.shape, jnp.float32),
            pltpu.SemaphoreType.DMA((depth // WEIGHT_ROWS,)),
        ],
        compiler_params=params(WEIGHT_VMEM),
        cost_estimate=cost(6 * weights.size, weights, weights),
        name="weight_parts",
    )(weights)

    def project(pieces, vmem):
        total = len({piece[0] for piece in pieces}) * rows
        normed = pltpu.VMEM((total, depth), jnp.bfloat16)
        counts = (total // rows, heads * total // rows, 1)
        return pl.pallas_call(
            functools.partial(
                projection_kernel, pieces=[(index, start) for index, start, _ in pieces], swap=swap
            ),
            in_specs=[HBM] * 2 + [VMEM] * 2 + [HBM] + [VMEM] * (heads - 1),
            out_shape=[shape(rows, width) for _, _, width in pieces],
            scratch_shapes=[
                pltpu.VMEM((heads, total, DK + DV), jnp.float32),
                pltpu.VMEM((total, heads * DV), jnp.float32),
                pltpu.VMEM((heads, DK, DV), jnp.float32),
                normed,
                normed,
            ]
            + [pltpu.SemaphoreType.DMA((n,)) for n in counts],
            compiler_params=params(vmem),
            cost_estimate=cost(3 * 2 * total * depth * columns, out_weight),
            name="projection",
        )(maps, out_gate, gain, parts, *states)

    return project_and_sum(project, columns, "tp")


def solution(mesh):
    return jax.shard_map(
        per_device,
        mesh=mesh,
        in_specs=(
            P("ctx", "tp"),
            P("ctx", "tp"),
            P("ctx", "tp"),
            P("tp", "ctx"),
            P("tp", "ctx"),
            P("ctx", "tp"),
            P(),
            P("tp", None),
        ),
        out_specs=P(("ctx", "tp"), None),
        check_vma=False,
    )
```

```python
import functools
import typing

import jax
import jax.numpy as jnp
from jax import lax
from jax.experimental import pallas as pl
from jax.experimental.pallas import tpu as pltpu
from jax.sharding import PartitionSpec as P

DK = 128
DV = 128
BLOCK = 128
SMALL = 32
BAND = 256
SWAP_ORDER = (7, 6, 3, 5, 2, 4, 1)
WEIGHT_ROWS = 128
MOST_VMEM = 56
SCAN_VMEM = 52.25
WEIGHT_VMEM = 40
FIRST_VMEM = 24
LATER_VMEM = 24
HEADS_AT_ONCE = 8
EPS = 1e-06


HBM = pl.BlockSpec(memory_space=pltpu.HBM)
VMEM = pl.BlockSpec(memory_space=pltpu.VMEM)


def dot(left, right):
    return jnp.dot(left, right, precision=lax.Precision.HIGH, preferred_element_type=jnp.float32)


def dot_transposed(left, right):
    return lax.dot_general(
        left,
        right,
        (((1,), (1,)), ((), ())),
        precision=lax.Precision.HIGH,
        preferred_element_type=jnp.float32,
    )


def iota(shape, dim):
    return lax.broadcasted_iota(jnp.int32, shape, dim)


def unit(rows):
    return rows * lax.rsqrt(jnp.sum(rows * rows, axis=-1, keepdims=True) + EPS)


def cumulative_logs(decays):
    tokens = decays.shape[1]
    upto = jnp.where(iota((tokens, tokens), 0) <= iota((tokens, tokens), 1), 1.0, 0.0)
    rows = jnp.dot(
        jnp.log(decays), upto, precision=lax.Precision.HIGHEST, preferred_element_type=jnp.float32
    )
    return rows, rows.T


def spread_diagonal(packed):
    size = packed.shape[0]
    place = iota(packed.shape, 1) // size
    return jnp.concatenate(
        [jnp.where(place == block, packed, 0.0) for block in range(BLOCK // size)], axis=0
    )


def lower_inverses(lowers):
    row = iota((SMALL, BLOCK), 0)
    lane = iota((SMALL, BLOCK), 1)
    column = lane % SMALL
    place = lane // SMALL
    eye = jnp.where(row == column, 1.0, 0.0)
    in_8 = row // 8 == column // 8
    in_16 = row // 16 == column // 16
    packed = []
    for lower in lowers:
        blocks = jnp.zeros((SMALL, BLOCK), jnp.float32)
        for block in range(BLOCK // SMALL):
            blocks = jnp.where(place == block, lower[block * SMALL : (block + 1) * SMALL], blocks)
        packed.append(blocks)
    nil = [jnp.where(in_8, blocks, 0.0) for blocks in packed]
    nil_2 = [dot(n, spread_diagonal(n)) for n in nil]
    wide_2 = [spread_diagonal(n) for n in nil_2]
    start = [eye - n for n in nil]
    nil_4 = [dot(n, w) for n, w in zip(nil_2, wide_2)]
    start = [s + dot(s, w) for s, w in zip(start, wide_2)]
    inv = [s + dot(s, spread_diagonal(n)) for s, n in zip(start, nil_4)]
    step_16 = [spread_diagonal(jnp.where(in_16 & ~in_8, blocks, 0.0)) for blocks in packed]
    half = [jnp.concatenate([d[8:16], d[24:32]], axis=0) for d in inv]
    half = [dot(h, w) for h, w in zip(half, step_16)]
    half = [dot(h, spread_diagonal(d)) for h, d in zip(half, inv)]
    inv = [
        jnp.concatenate([d[:8], d[8:16] - h[:8], d[16:24], d[24:] - h[8:]], axis=0)
        for d, h in zip(inv, half)
    ]
    step_32 = [spread_diagonal(jnp.where(in_16, 0.0, blocks)) for blocks in packed]
    half = [dot(d[16:], w) for d, w in zip(inv, step_32)]
    half = [dot(h, spread_diagonal(d)) for h, d in zip(half, inv)]
    inv = [jnp.concatenate([d[:16], d[16:] - h], axis=0) for d, h in zip(inv, half)]
    odd = place % 2 == 1
    zeros = jnp.zeros((SMALL, BLOCK), jnp.float32)
    low = [jnp.where(odd, d, 0.0) for d in inv]
    wide = [
        spread_diagonal(jnp.concatenate([jnp.where(odd, 0.0, d), l], axis=0)) for d, l in zip(inv, low)
    ]
    step_64 = [
        spread_diagonal(
            jnp.concatenate(
                [
                    zeros,
                    jnp.where(
                        place == 0, lower[32:64], jnp.where(place == 2, lower[96:128], 0.0)
                    ),
                ],
                axis=0,
            )
        )
        for lower in lowers
    ]
    half = [dot(l, w) for l, w in zip(low, step_64)]
    half = [dot(h, w) for h, w in zip(half, wide)]
    inv = [
        jnp.concatenate([jnp.where(odd, 0.0, d), l - h], axis=0) for d, l, h in zip(inv, low, half)
    ]
    left = iota((64, BLOCK), 1) < 64
    low = [jnp.where(left, 0.0, d) for d in inv]
    wide = [jnp.concatenate([jnp.where(left, d, 0.0), l], axis=0) for d, l in zip(inv, low)]
    step_128 = [
        jnp.concatenate(
            [jnp.zeros((64, BLOCK), jnp.float32), jnp.where(left, lower[64:], 0.0)], axis=0
        )
        for lower in lowers
    ]
    half = [dot(l, w) for l, w in zip(low, step_128)]
    half = [dot(h, w) for h, w in zip(half, wide)]
    return [jnp.concatenate([w[:64], w[64:] - h], axis=0) for w, h in zip(wide, half)]


def block(index):
    return slice(index * BLOCK, (index + 1) * BLOCK)


def fetch(pairs, sems):
    copies = [pltpu.make_async_copy(src, dst, sems.at[i]) for i, (src, dst) in enumerate(pairs)]
    for copy in copies:
        copy.start()
    return copies


def partner(place, swap):
    return lax.axis_index("ctx") ^ place if swap else place


def summary_kernel(decay_hbm, strength_hbm, k_hbm, v_hbm, factor_hbm, *rest, swap):
    *summaries, decay_ref, strength_ref, k_ref, v_ref, sems, factor_ref, summary_ref, out_sems = rest
    copies = fetch(
        [(decay_hbm, decay_ref), (strength_hbm, strength_ref), (k_hbm, k_ref), (v_hbm, v_ref)], sems
    )
    for copy in copies[:3]:
        copy.wait()
    tokens = k_ref.shape[0]
    key_heads = k_ref.shape[1] // DK
    value_heads = v_ref.shape[1] // DV
    repeat = value_heads // key_heads
    blocks = tokens // BLOCK
    rows, columns = cumulative_logs(decay_ref[...])
    strengths = strength_ref[...].T
    strict = iota((BLOCK, BLOCK), 0) > iota((BLOCK, BLOCK), 1)
    eye = jnp.where(iota((BLOCK, DK + DV), 0) == iota((BLOCK, DK + DV), 1), 1.0, 0.0)
    leaving = []
    for first in range(0, value_heads, HEADS_AT_ONCE):
        heads = range(first, min(first + HEADS_AT_ONCE, value_heads))
        keys = {}
        gram = {}
        for key_head in sorted({head // repeat for head in heads}):
            unit_rows = unit(k_ref[:, key_head * DK : (key_head + 1) * DK])
            keys[key_head] = [unit_rows[block(p)] for p in range(blocks)]
            gram[key_head] = {
                (p, r): dot_transposed(keys[key_head][p], keys[key_head][r])
                for p in range(blocks)
                for r in range(p + 1)
            }
        lower = {}
        for head in heads:
            for p in range(blocks):
                at = columns[block(p), head : head + 1]
                weight = strengths[block(p), head : head + 1]
                for r in range(p + 1):
                    spread = at - rows[head : head + 1, block(r)]
                    if p == r:
                        damp = jnp.where(strict, jnp.exp(jnp.where(strict, spread, 0.0)), 0.0)
                    else:
                        damp = jnp.exp(spread)
                    lower[head, p, r] = weight * gram[head // repeat][p, r] * damp
        inverse = lower_inverses([lower[head, p, p] for head in heads for p in range(blocks)])
        inverse = {
            (head, p): inverse[i * blocks + p] for i, head in enumerate(heads) for p in range(blocks)
        }
        if first == 0:
            copies[3].wait()
        factors = {}
        for p in range(blocks):
            for head in heads:
                at = columns[block(p), head : head + 1]
                weight = strengths[block(p), head : head + 1]
                right = jnp.concatenate(
                    [
                        keys[head // repeat][p] * (-weight * jnp.exp(at)),
                        v_ref[block(p), head * DV : (head + 1) * DV] * weight,
                    ],
                    axis=1,
                )
                for r in range(p):
                    right = right - dot(lower[head, p, r], factors[head, r])
                factors[head, p] = dot(inverse[head, p], right)
                factor_ref[head, block(p), :] = factors[head, p]
        flipped = {key_head: [k.T for k in keys[key_head]] for key_head in keys}
        for head in heads:
            last = rows[head : head + 1, tokens - 1 : tokens]
            total = jnp.exp(last) * eye
            for p in range(blocks):
                ending = jnp.exp(last - columns[block(p), head : head + 1])
                total = total + dot(flipped[head // repeat][p], factors[head, p] * ending)
            summary_ref[head] = total
        group = pl.ds(first, len(heads))
        leaving.append(
            pltpu.make_async_copy(
                factor_ref.at[group], factor_hbm.at[group], out_sems.at[len(leaving)]
            )
        )
        leaving[-1].start()
    if swap:
        target = factor_hbm.at[value_heads, pl.ds(0, DK)]
        leaving.append(
            pltpu.make_async_copy(summary_ref.at[partner(0, swap)], target, out_sems.at[len(leaving)])
        )
        leaving[-1].start()
    for place, out_ref in enumerate(summaries):
        out_ref[...] = summary_ref[partner(place + 1 if swap else place, swap)]
    for copy in leaving:
        copy.wait()


def output_kernel(
    decay_hbm,
    q_hbm,
    k_hbm,
    factor_hbm,
    map_hbm,
    decay_ref,
    q_ref,
    k_ref,
    factor_ref,
    sems,
    map_ref,
    out_sems,
):
    repeat = factor_ref.shape[0] // (k_hbm.shape[1] // DK)
    groups = [pl.ds(head, repeat) for head in range(0, factor_ref.shape[0], repeat)]
    copies = fetch(
        [(decay_hbm, decay_ref), (q_hbm, q_ref), (k_hbm, k_ref)]
        + [(factor_hbm.at[group], factor_ref.at[group]) for group in groups],
        sems,
    )
    leaving = []
    for copy in copies[:3]:
        copy.wait()
    tokens = q_ref.shape[0]
    key_heads = q_ref.shape[1] // DK
    value_heads = factor_ref.shape[0]
    repeat = value_heads // key_heads
    blocks = tokens // BLOCK
    rows, columns = cumulative_logs(decay_ref[...])
    inclusive = iota((BLOCK, BLOCK), 0) >= iota((BLOCK, BLOCK), 1)
    for key_head in range(key_heads):
        lanes = slice(key_head * DK, (key_head + 1) * DK)
        queries = unit(q_ref[:, lanes]) * DK**-0.5
        keys = unit(k_ref[:, lanes])
        for p in range(blocks):
            scores = [dot_transposed(queries[block(p)], keys[block(r)]) for r in range(p + 1)]
            if p == 0:
                copies[3 + key_head].wait()
            for head in range(key_head * repeat, (key_head + 1) * repeat):
                at = columns[block(p), head : head + 1]
                total = jnp.concatenate(
                    [queries[block(p)] * jnp.exp(at), jnp.zeros((BLOCK, DV), jnp.float32)], axis=1
                )
                for r in range(p + 1):
                    spread = at - rows[head : head + 1, block(r)]
                    if p == r:
                        damp = jnp.where(inclusive, jnp.exp(jnp.where(inclusive, spread, 0.0)), 0.0)
                    else:
                        damp = jnp.exp(spread)
                    total = total + dot(scores[r] * damp, factor_ref[head, block(r), :])
                map_ref[head, block(p), :] = total
        group = groups[key_head]
        leaving.append(
            pltpu.make_async_copy(map_ref.at[group], map_hbm.at[group], out_sems.at[key_head])
        )
        leaving[-1].start()
    for copy in leaving:
        copy.wait()


def scan_kernel(held_ref, entry_ref):
    count, held, key_width, width = entry_ref.shape
    for head in range(held):
        state = jnp.zeros((key_width, width), jnp.float32)
        entry_ref[0, head] = state
        for source in range(count - 1):
            added = held_ref[source, head, :, key_width:]
            if source:
                added = added + dot(held_ref[source, head, :, :key_width], state)
            state = added
            entry_ref[source + 1, head] = state


def ordered_scan_kernel(factor_hbm, *rest):
    *arrays, held_ref, entry_ref, sems = rest
    count = entry_ref.shape[0]
    held, own_entry_hbm, entries = arrays[: count - 1], arrays[count - 1], arrays[count:]
    here = partner(0, True)
    own_summary = factor_hbm.at[factor_hbm.shape[0] - 1, pl.ds(0, DK)]
    own = pltpu.make_async_copy(own_summary, held_ref.at[here], sems.at[0])
    own.start()
    for i, summary in enumerate(held):
        held_ref[partner(i + 1, True)] = summary[...]
    own.wait()
    state = jnp.zeros(entry_ref.shape[1:], jnp.float32)
    entry_ref[0] = state
    for source in range(count - 1):
        added = held_ref[source, :, DK:]
        if source:
            added = added + dot(held_ref[source, :, :DK], state)
        state = added
        entry_ref[source + 1] = state
    own = pltpu.make_async_copy(entry_ref.at[here], own_entry_hbm, sems.at[1])
    own.start()
    for i, entry in enumerate(entries):
        entry[...] = entry_ref[partner(i + 1, True)]
    own.wait()


def split(value):
    high = value.astype(jnp.bfloat16)
    return high, (value - high.astype(jnp.float32)).astype(jnp.bfloat16)


def weight_kernel(weight_hbm, parts_ref, weight_ref, sems):
    bands = [pl.ds(row, WEIGHT_ROWS) for row in range(0, weight_ref.shape[0], WEIGHT_ROWS)]
    copies = fetch([(weight_hbm.at[band, :], weight_ref.at[band, :]) for band in bands], sems)
    for copy, band in zip(copies, bands):
        copy.wait()
        parts_ref[0, band, :], parts_ref[1, band, :] = split(weight_ref[band, :])


def projection_kernel(map_hbm, gate_hbm, gain_ref, parts_ref, own_hbm, *rest, pieces, swap):
    *arrays, map_ref, gate_ref, state_ref, high_ref, low_ref, gate_sems, map_sems, state_sems = rest
    outs = arrays[-len(pieces) :]
    states = arrays[: -len(pieces)]
    heads = state_ref.shape[0]
    rows = outs[0].shape[0]
    blocks = sorted({index for index, _ in pieces})
    own = fetch([(own_hbm, state_ref.at[partner(0, swap.heads)])], state_sems)
    places = []
    for i, index in enumerate(blocks):
        start = (lax.axis_index("tp") ^ index) * rows if swap.rows else index * rows
        places.append((pl.ds(pl.multiple_of(start, rows), rows), pl.ds(i * rows, rows)))
    gates = fetch([(gate_hbm.at[s, :], gate_ref.at[t, :]) for s, t in places], gate_sems)
    maps = fetch(
        [
            (map_hbm.at[head, s, :], map_ref.at[head, t, :])
            for head in range(heads)
            for s, t in places
        ],
        map_sems,
    )
    for i, state in enumerate(states):
        state_ref[partner(i + 1, swap.heads)] = state[...]
    for copy in own + gates:
        copy.wait()
    gain = gain_ref[...]
    for head in range(heads):
        lanes = slice(head * DV, (head + 1) * DV)
        gate = gate_ref[:, lanes]
        factor = gate / (1.0 + jnp.exp(-gate)) * gain
        for copy in maps[head * len(blocks) : (head + 1) * len(blocks)]:
            copy.wait()
        core = map_ref[head, :, DK:] + dot(map_ref[head, :, :DK], state_ref[head])
        scale = lax.rsqrt(jnp.mean(core * core, axis=-1, keepdims=True) + EPS)
        high_ref[:, lanes], low_ref[:, lanes] = split(core * scale * factor)
    total = len(blocks) * rows
    for band in range(0, parts_ref.shape[2], BAND):
        lanes = slice(band, band + BAND)
        both = jnp.concatenate([high_ref[...], low_ref[...]], axis=0)
        sums = jnp.dot(both, parts_ref[0, :, lanes], preferred_element_type=jnp.float32)
        last = jnp.dot(high_ref[...], parts_ref[1, :, lanes], preferred_element_type=jnp.float32)
        result = sums[:total] + (sums[total:] + last)
        for (index, start), out_ref in zip(pieces, outs):
            if start <= band < start + out_ref.shape[1]:
                at = blocks.index(index) * rows
                out_ref[:, band - start : band - start + BAND] = result[at : at + rows]


def forward_kernel(across_ref, own_ref, up_ref, down_ref, going_ref, staying_ref):
    outward = lax.axis_index("tp") == 1
    up, down = up_ref[...], down_ref[...]
    going_ref[...] = across_ref[...] + jnp.where(outward, up, down)
    staying_ref[...] = own_ref[...] + jnp.where(outward, down, up)


def shape(*dims):
    return jax.ShapeDtypeStruct(dims, jnp.float32)


def params(mebibytes):
    return pltpu.CompilerParams(vmem_limit_bytes=int(mebibytes * 1024 * 1024))


def cost(flops, *arrays):
    return pl.CostEstimate(
        flops=flops, bytes_accessed=4 * sum(a.size for a in arrays), transcendentals=0
    )


def partners_swap(arrays, axis):
    count = len(arrays)
    arrays = list(arrays)
    for i in [i for i in SWAP_ORDER if i < count]:
        arrays[i] = lax.ppermute(arrays[i], axis, [(d, d ^ i) for d in range(count)])
    return arrays


class Swap(typing.NamedTuple):
    heads: bool
    rows: bool


def swap_is_possible(heads, count):
    return heads == count and count & (count - 1) == 0 and count <= 8


def entering_states(factors, summaries, swap, beside, after):
    heads = factors.shape[0] - 1
    count = lax.axis_size("ctx")
    if swap:
        held = partners_swap([factors, *summaries], "ctx")
        held, beside = lax.optimization_barrier((held, beside))
        entry = shape(DK, DV)
        entries = pl.pallas_call(
            ordered_scan_kernel,
            in_specs=[HBM] + [VMEM] * (count - 1),
            out_specs=[HBM] + [VMEM] * (count - 1),
            out_shape=[entry] * count,
            scratch_shapes=[
                pltpu.VMEM((count, DK, DK + DV), jnp.float32),
                pltpu.VMEM((count, DK, DV), jnp.float32),
                pltpu.SemaphoreType.DMA((2,)),
            ],
            compiler_params=params(SCAN_VMEM),
            name="state_scan",
        )(*held)
        entries, after = lax.optimization_barrier((entries, after))
        return partners_swap(entries, "ctx"), beside, after
    parts = max(1, count // heads)
    per_owner = max(1, heads // count)
    width = DV // parts
    groups = heads // per_owner
    summary = jnp.stack(summaries)
    maps = summary[:, :, :DK].reshape(groups, 1, per_owner, DK, DK)
    maps = jnp.broadcast_to(maps, (groups, parts, per_owner, DK, DK))
    adds = summary[:, :, DK:].reshape(groups, per_owner, DK, parts, width)
    payload = jnp.concatenate([maps, adds.transpose(0, 3, 1, 2, 4)], axis=-1)
    payload = payload.reshape(count, per_owner, DK, DK + width)
    held = lax.all_to_all(payload, "ctx", split_axis=0, concat_axis=0, tiled=True)
    entries = pl.pallas_call(
        scan_kernel,
        out_shape=shape(count, per_owner, DK, width),
        compiler_params=params(32),
        name="state_scan",
    )(held)
    back = lax.all_to_all(entries, "ctx", split_axis=0, concat_axis=0, tiled=True)
    back = back.reshape(groups, parts, per_owner, DK, width).transpose(0, 2, 3, 1, 4)
    back = back.reshape(heads, DK, DV)
    return [back[head] for head in range(heads)], beside, after


def project_and_sum(project, columns, axis):
    count = lax.axis_size(axis)
    if count != 4:
        whole = jnp.concatenate(project([(i, 0, columns) for i in range(count)], LATER_VMEM), axis=0)
        return lax.psum_scatter(whole, axis, scatter_dimension=0, tiled=True)
    (opposite,) = project([(3, 0, columns)], FIRST_VMEM)
    up = lax.ppermute(opposite, axis, [(0, 1), (1, 2)])
    down = lax.ppermute(opposite, axis, [(3, 2), (2, 1)])
    across, own, near = project([(i, 0, columns) for i in (2, 0, 1)], LATER_VMEM)
    from_near = lax.ppermute(near, axis, [(i, i ^ 1) for i in range(4)])
    going, staying = pl.pallas_call(
        forward_kernel,
        out_shape=[shape(*own.shape)] * 2,
        compiler_params=params(LATER_VMEM),
        name="forward",
    )(across, own, up, down)
    from_across = lax.ppermute(going, axis, [(i, i ^ 2) for i in range(4)])
    return (staying + from_near) + from_across


def per_device(queries, key_vectors, values, decays, strengths, out_gate, norm_gain, out_weight):
    tokens = queries.shape[0]
    heads = values.shape[1] // DV
    key_heads = queries.shape[1] // DK
    depth, columns = out_weight.shape
    rows = tokens // lax.axis_size("tp")
    gain = norm_gain.reshape(1, DV)
    swap = Swap(
        heads=swap_is_possible(heads, lax.axis_size("ctx")), rows=lax.axis_size("tp") == 4
    )

    def buffers(*arrays):
        return [pltpu.VMEM(a.shape, a.dtype) for a in arrays] + [
            pltpu.SemaphoreType.DMA((len(arrays),))
        ]

    factor_shape = shape(heads, tokens, DK + DV)
    groups = pl.cdiv(heads, HEADS_AT_ONCE)
    sent = heads - 1 if swap.heads else heads
    factors, *summaries = pl.pallas_call(
        functools.partial(summary_kernel, swap=swap.heads),
        in_specs=[HBM] * 4,
        out_specs=[HBM] + [VMEM] * sent,
        out_shape=[shape(heads + 1, tokens, DK + DV)] + [shape(DK, DK + DV)] * sent,
        scratch_shapes=buffers(decays, strengths, key_vectors, values)
        + [pltpu.VMEM(factor_shape.shape, jnp.float32), pltpu.VMEM((heads, DK, DK + DV), jnp.float32)]
        + [pltpu.SemaphoreType.DMA((groups + 1,))],
        compiler_params=params(MOST_VMEM),
        name="state_summary",
    )(decays, strengths, key_vectors, values)
    maps = pl.pallas_call(
        output_kernel,
        in_specs=[HBM] * 4,
        out_specs=HBM,
        out_shape=factor_shape,
        scratch_shapes=[pltpu.VMEM(a.shape, jnp.float32) for a in (decays, queries, key_vectors)]
        + [pltpu.VMEM(factor_shape.shape, jnp.float32), pltpu.SemaphoreType.DMA((3 + key_heads,))]
        + [pltpu.VMEM(factor_shape.shape, jnp.float32), pltpu.SemaphoreType.DMA((key_heads,))],
        compiler_params=params(MOST_VMEM),
        cost_estimate=cost(3 * 2 * heads * tokens * tokens * 384, factors, factors, queries),
        name="output_maps",
    )(decays, queries, key_vectors, factors)
    states, maps, weights = entering_states(factors, summaries, swap.heads, maps, out_weight)
    parts = pl.pallas_call(
        weight_kernel,
        in_specs=[HBM],
        out_shape=jax.ShapeDtypeStruct((2, depth, columns), jnp.bfloat16),
        scratch_shapes=[
            pltpu.VMEM(out_weight.shape, jnp.float32),
            pltpu.SemaphoreType.DMA((depth // WEIGHT_ROWS,)),
        ],
        compiler_params=params(WEIGHT_VMEM),
        cost_estimate=cost(6 * weights.size, weights, weights),
        name="weight_parts",
    )(weights)

    def project(pieces, vmem):
        total = len({piece[0] for piece in pieces}) * rows
        normed = pltpu.VMEM((total, depth), jnp.bfloat16)
        counts = (total // rows, heads * total // rows, 1)
        return pl.pallas_call(
            functools.partial(
                projection_kernel, pieces=[(index, start) for index, start, _ in pieces], swap=swap
            ),
            in_specs=[HBM] * 2 + [VMEM] * 2 + [HBM] + [VMEM] * (heads - 1),
            out_shape=[shape(rows, width) for _, _, width in pieces],
            scratch_shapes=[
                pltpu.VMEM((heads, total, DK + DV), jnp.float32),
                pltpu.VMEM((total, heads * DV), jnp.float32),
                pltpu.VMEM((heads, DK, DV), jnp.float32),
                normed,
                normed,
            ]
            + [pltpu.SemaphoreType.DMA((n,)) for n in counts],
            compiler_params=params(vmem),
            cost_estimate=cost(3 * 2 * total * depth * columns, out_weight),
            name="projection",
        )(maps, out_gate, gain, parts, *states)

    return project_and_sum(project, columns, "tp")


def solution(mesh):
    return jax.shard_map(
        per_device,
        mesh=mesh,
        in_specs=(
            P("ctx", "tp"),
            P("ctx", "tp"),
            P("ctx", "tp"),
            P("tp", "ctx"),
            P("tp", "ctx"),
            P("ctx", "tp"),
            P(),
            P("tp", None),
        ),
        out_specs=P(("ctx", "tp"), None),
        check_vma=False,
    )
```

```python
import functools
import typing

import jax
import jax.numpy as jnp
from jax import lax
from jax.experimental import pallas as pl
from jax.experimental.pallas import tpu as pltpu
from jax.sharding import PartitionSpec as P

DK = 128
DV = 128
BLOCK = 128
SMALL = 32
BAND = 256
SWAP_ORDER = (7, 6, 3, 5, 2, 4, 1)
WEIGHT_ROWS = 128
MOST_VMEM = 56
SCAN_VMEM = 52.25
WEIGHT_VMEM = 40
FIRST_VMEM = 24
LATER_VMEM = 24
HEADS_AT_ONCE = 8
EPS = 1e-06


HBM = pl.BlockSpec(memory_space=pltpu.HBM)
VMEM = pl.BlockSpec(memory_space=pltpu.VMEM)


def dot(left, right):
    return jnp.dot(left, right, precision=lax.Precision.HIGH, preferred_element_type=jnp.float32)


def dot_transposed(left, right):
    return lax.dot_general(
        left,
        right,
        (((1,), (1,)), ((), ())),
        precision=lax.Precision.HIGH,
        preferred_element_type=jnp.float32,
    )


def iota(shape, dim):
    return lax.broadcasted_iota(jnp.int32, shape, dim)


def unit(rows):
    return rows * lax.rsqrt(jnp.sum(rows * rows, axis=-1, keepdims=True) + EPS)


def cumulative_logs(decays):
    tokens = decays.shape[1]
    upto = jnp.where(iota((tokens, tokens), 0) <= iota((tokens, tokens), 1), 1.0, 0.0)
    rows = jnp.dot(
        jnp.log(decays), upto, precision=lax.Precision.HIGHEST, preferred_element_type=jnp.float32
    )
    return rows, rows.T


def split(value):
    high = value.astype(jnp.bfloat16)
    return high, (value - high.astype(jnp.float32)).astype(jnp.bfloat16)


def dot_parts(left, right):
    rows = left[0].shape[0]
    both = jnp.concatenate(left, axis=0)
    sums = jnp.dot(both, right[0], preferred_element_type=jnp.float32)
    rest = jnp.dot(left[0], right[1], preferred_element_type=jnp.float32)
    return sums[:rows] + (sums[rows:] + rest)


def stack_parts(*values):
    return tuple(jnp.concatenate(pieces, axis=0) for pieces in zip(*values))


def spread_parts(parts, masks):
    return tuple(jnp.concatenate([part * mask for mask in masks], axis=0) for part in parts)


def lower_inverses(lowers):
    row = iota((SMALL, BLOCK), 0)
    lane = iota((SMALL, BLOCK), 1)
    column = lane % SMALL
    place = lane // SMALL
    eye = jnp.where(row == column, 1.0, 0.0)
    in_8 = row // 8 == column // 8
    in_16 = row // 16 == column // 16
    odd = place % 2 == 1
    masks = [
        jnp.where(place == index, 1.0, 0.0).astype(jnp.bfloat16) for index in range(BLOCK // SMALL)
    ]
    packed = []
    for lower in lowers:
        blocks = jnp.zeros((SMALL, BLOCK), jnp.float32)
        for index in range(BLOCK // SMALL):
            blocks = jnp.where(place == index, lower[index * SMALL : (index + 1) * SMALL], blocks)
        packed.append(blocks)
    nil = [jnp.where(in_8, blocks, 0.0) for blocks in packed]
    parts = [split(n) for n in nil]
    nil_2 = [split(dot_parts(n, spread_parts(n, masks))) for n in parts]
    start = [eye - n for n in nil]
    pairs = [
        dot_parts(stack_parts(n, split(s)), spread_parts(n, masks)) for n, s in zip(nil_2, start)
    ]
    start = [s + pair[SMALL:] for s, pair in zip(start, pairs)]
    nil_4 = [spread_parts(split(pair[:SMALL]), masks) for pair in pairs]
    inv = [s + dot_parts(split(s), n) for s, n in zip(start, nil_4)]
    step_16 = [
        spread_parts(split(jnp.where(in_16 & ~in_8, blocks, 0.0)), masks) for blocks in packed
    ]
    half = [jnp.concatenate([d[8:16], d[24:32]], axis=0) for d in inv]
    half = [dot_parts(split(h), w) for h, w in zip(half, step_16)]
    half = [dot_parts(split(h), spread_parts(split(d), masks)) for h, d in zip(half, inv)]
    inv = [
        jnp.concatenate([d[:8], d[8:16] - h[:8], d[16:24], d[24:] - h[8:]], axis=0)
        for d, h in zip(inv, half)
    ]
    step_32 = [spread_parts(split(jnp.where(in_16, 0.0, blocks)), masks) for blocks in packed]
    half = [dot_parts(split(d[16:]), w) for d, w in zip(inv, step_32)]
    half = [dot_parts(split(h), spread_parts(split(d), masks)) for h, d in zip(half, inv)]
    inv = [jnp.concatenate([d[:16], d[16:] - h], axis=0) for d, h in zip(inv, half)]
    wide = [spread_parts(split(d), masks) for d in inv]
    low = [jnp.where(odd, d, 0.0) for d in inv]
    zeros = jnp.zeros((SMALL, BLOCK), jnp.bfloat16)
    step_64 = []
    for lower in lowers:
        below = jnp.where(place == 0, lower[32:64], jnp.where(place == 2, lower[96:128], 0.0))
        step_64.append(
            tuple(
                jnp.concatenate([zeros, part * masks[0], zeros, part * masks[2]], axis=0)
                for part in split(below)
            )
        )
    half = [dot_parts(split(l), w) for l, w in zip(low, step_64)]
    half = [dot_parts(split(h), w) for h, w in zip(half, wide)]
    inv = [
        jnp.concatenate([jnp.where(odd, 0.0, d), l - h], axis=0) for d, l, h in zip(inv, low, half)
    ]
    left = iota((64, BLOCK), 1) < 64
    low = [jnp.where(left, 0.0, d) for d in inv]
    wide = [jnp.concatenate([jnp.where(left, d, 0.0), l], axis=0) for d, l in zip(inv, low)]
    wide_parts = [split(w) for w in wide]
    zeros = jnp.zeros((64, BLOCK), jnp.bfloat16)
    step_128 = [
        tuple(
            jnp.concatenate([zeros, part], axis=0) for part in split(jnp.where(left, lower[64:], 0.0))
        )
        for lower in lowers
    ]
    half = [dot_parts(tuple(part[64:] for part in l), w) for l, w in zip(wide_parts, step_128)]
    half = [dot_parts(split(h), w) for h, w in zip(half, wide_parts)]
    return [
        tuple(
            jnp.concatenate([high, low], axis=0)
            for high, low in zip((part[:64] for part in parts), split(w[64:] - h))
        )
        for parts, w, h in zip(wide_parts, wide, half)
    ]


def block(index):
    return slice(index * BLOCK, (index + 1) * BLOCK)


def fetch(pairs, sems):
    copies = [pltpu.make_async_copy(src, dst, sems.at[i]) for i, (src, dst) in enumerate(pairs)]
    for copy in copies:
        copy.start()
    return copies


def partner(place, swap):
    return lax.axis_index("ctx") ^ place if swap else place


def summary_kernel(decay_hbm, strength_hbm, k_hbm, v_hbm, factor_hbm, *rest, swap):
    *summaries, decay_ref, strength_ref, k_ref, v_ref, sems, factor_ref, summary_ref, out_sems = rest
    copies = fetch(
        [(decay_hbm, decay_ref), (strength_hbm, strength_ref), (k_hbm, k_ref), (v_hbm, v_ref)], sems
    )
    for copy in copies[:3]:
        copy.wait()
    tokens = k_ref.shape[0]
    key_heads = k_ref.shape[1] // DK
    value_heads = v_ref.shape[1] // DV
    repeat = value_heads // key_heads
    blocks = tokens // BLOCK
    rows, columns = cumulative_logs(decay_ref[...])
    strengths = strength_ref[...].T
    strict = iota((BLOCK, BLOCK), 0) > iota((BLOCK, BLOCK), 1)
    eye = jnp.where(iota((BLOCK, DK + DV), 0) == iota((BLOCK, DK + DV), 1), 1.0, 0.0)
    leaving = []
    for first in range(0, value_heads, HEADS_AT_ONCE):
        heads = range(first, min(first + HEADS_AT_ONCE, value_heads))
        keys = {}
        gram = {}
        for key_head in sorted({head // repeat for head in heads}):
            unit_rows = unit(k_ref[:, key_head * DK : (key_head + 1) * DK])
            keys[key_head] = [unit_rows[block(p)] for p in range(blocks)]
            gram[key_head] = {
                (p, r): dot_transposed(keys[key_head][p], keys[key_head][r])
                for p in range(blocks)
                for r in range(p + 1)
            }
        lower = {}
        for head in heads:
            for p in range(blocks):
                at = columns[block(p), head : head + 1]
                weight = strengths[block(p), head : head + 1]
                for r in range(p + 1):
                    spread = at - rows[head : head + 1, block(r)]
                    if p == r:
                        damp = jnp.where(strict, jnp.exp(jnp.where(strict, spread, 0.0)), 0.0)
                    else:
                        damp = jnp.exp(spread)
                    lower[head, p, r] = weight * gram[head // repeat][p, r] * damp
        inverse = lower_inverses([lower[head, p, p] for head in heads for p in range(blocks)])
        inverse = {
            (head, p): inverse[i * blocks + p] for i, head in enumerate(heads) for p in range(blocks)
        }
        if first == 0:
            copies[3].wait()
        factors = {}
        for p in range(blocks):
            for head in heads:
                at = columns[block(p), head : head + 1]
                weight = strengths[block(p), head : head + 1]
                right = jnp.concatenate(
                    [
                        keys[head // repeat][p] * (-weight * jnp.exp(at)),
                        v_ref[block(p), head * DV : (head + 1) * DV] * weight,
                    ],
                    axis=1,
                )
                for r in range(p):
                    right = right - dot_parts(split(lower[head, p, r]), split(factors[head, r]))
                factors[head, p] = dot_parts(inverse[head, p], split(right))
                factor_ref[head, block(p), :] = factors[head, p]
        flipped = {key_head: [split(k.T) for k in keys[key_head]] for key_head in keys}
        for head in heads:
            last = rows[head : head + 1, tokens - 1 : tokens]
            total = jnp.exp(last) * eye
            for p in range(blocks):
                ending = jnp.exp(last - columns[block(p), head : head + 1])
                total = total + dot_parts(flipped[head // repeat][p], split(factors[head, p] * ending))
            summary_ref[head] = total
        group = pl.ds(first, len(heads))
        leaving.append(
            pltpu.make_async_copy(
                factor_ref.at[group], factor_hbm.at[group], out_sems.at[len(leaving)]
            )
        )
        leaving[-1].start()
    if swap:
        target = factor_hbm.at[value_heads, pl.ds(0, DK)]
        leaving.append(
            pltpu.make_async_copy(summary_ref.at[partner(0, swap)], target, out_sems.at[len(leaving)])
        )
        leaving[-1].start()
    for place, out_ref in enumerate(summaries):
        out_ref[...] = summary_ref[partner(place + 1 if swap else place, swap)]
    for copy in leaving:
        copy.wait()


def output_kernel(
    decay_hbm,
    q_hbm,
    k_hbm,
    factor_hbm,
    map_hbm,
    decay_ref,
    q_ref,
    k_ref,
    factor_ref,
    sems,
    map_ref,
    out_sems,
):
    repeat = factor_ref.shape[0] // (k_hbm.shape[1] // DK)
    groups = [pl.ds(head, repeat) for head in range(0, factor_ref.shape[0], repeat)]
    copies = fetch(
        [(decay_hbm, decay_ref), (q_hbm, q_ref), (k_hbm, k_ref)]
        + [(factor_hbm.at[group], factor_ref.at[group]) for group in groups],
        sems,
    )
    leaving = []
    for copy in copies[:3]:
        copy.wait()
    tokens = q_ref.shape[0]
    key_heads = q_ref.shape[1] // DK
    value_heads = factor_ref.shape[0]
    repeat = value_heads // key_heads
    blocks = tokens // BLOCK
    rows, columns = cumulative_logs(decay_ref[...])
    inclusive = iota((BLOCK, BLOCK), 0) >= iota((BLOCK, BLOCK), 1)
    for key_head in range(key_heads):
        lanes = slice(key_head * DK, (key_head + 1) * DK)
        queries = unit(q_ref[:, lanes]) * DK**-0.5
        keys = unit(k_ref[:, lanes])
        for p in range(blocks):
            scores = [dot_transposed(queries[block(p)], keys[block(r)]) for r in range(p + 1)]
            if p == 0:
                copies[3 + key_head].wait()
            for head in range(key_head * repeat, (key_head + 1) * repeat):
                at = columns[block(p), head : head + 1]
                total = jnp.concatenate(
                    [queries[block(p)] * jnp.exp(at), jnp.zeros((BLOCK, DV), jnp.float32)], axis=1
                )
                for r in range(p + 1):
                    spread = at - rows[head : head + 1, block(r)]
                    if p == r:
                        damp = jnp.where(inclusive, jnp.exp(jnp.where(inclusive, spread, 0.0)), 0.0)
                    else:
                        damp = jnp.exp(spread)
                    total = total + dot(scores[r] * damp, factor_ref[head, block(r), :])
                map_ref[head, block(p), :] = total
        group = groups[key_head]
        leaving.append(
            pltpu.make_async_copy(map_ref.at[group], map_hbm.at[group], out_sems.at[key_head])
        )
        leaving[-1].start()
    for copy in leaving:
        copy.wait()


def scan_kernel(held_ref, entry_ref):
    count, held, key_width, width = entry_ref.shape
    for head in range(held):
        state = jnp.zeros((key_width, width), jnp.float32)
        entry_ref[0, head] = state
        for source in range(count - 1):
            added = held_ref[source, head, :, key_width:]
            if source:
                added = added + dot(held_ref[source, head, :, :key_width], state)
            state = added
            entry_ref[source + 1, head] = state


def ordered_scan_kernel(factor_hbm, *rest):
    *arrays, held_ref, entry_ref, sems = rest
    count = entry_ref.shape[0]
    held, entries = arrays[: count - 1], arrays[count - 1 :]
    here = partner(0, True)
    own_summary = factor_hbm.at[factor_hbm.shape[0] - 1, pl.ds(0, DK)]
    own = pltpu.make_async_copy(own_summary, held_ref.at[here], sems.at[0])
    own.start()
    for i, summary in enumerate(held):
        held_ref[partner(i + 1, True)] = summary[...]
    own.wait()
    state = jnp.zeros(entry_ref.shape[1:], jnp.float32)
    entry_ref[0] = state
    for source in range(count - 1):
        added = held_ref[source, :, DK:]
        if source:
            added = added + dot(held_ref[source, :, :DK], state)
        state = added
        entry_ref[source + 1] = state
    for i, entry in enumerate(entries):
        entry[...] = entry_ref[partner(i, True)]


def weight_kernel(weight_hbm, parts_ref, weight_ref, sems):
    bands = [pl.ds(row, WEIGHT_ROWS) for row in range(0, weight_ref.shape[0], WEIGHT_ROWS)]
    copies = fetch([(weight_hbm.at[band, :], weight_ref.at[band, :]) for band in bands], sems)
    for copy, band in zip(copies, bands):
        copy.wait()
        parts_ref[0, band, :], parts_ref[1, band, :] = split(weight_ref[band, :])


def projection_kernel(map_hbm, gate_hbm, gain_ref, parts_ref, *rest, pieces, swap):
    *arrays, map_ref, gate_ref, state_ref, high_ref, low_ref, gate_sems, map_sems = rest
    outs = arrays[-len(pieces) :]
    states = arrays[: -len(pieces)]
    heads = state_ref.shape[0]
    rows = outs[0].shape[0]
    blocks = sorted({index for index, _ in pieces})
    places = []
    for i, index in enumerate(blocks):
        start = (lax.axis_index("tp") ^ index) * rows if swap.rows else index * rows
        places.append((pl.ds(pl.multiple_of(start, rows), rows), pl.ds(i * rows, rows)))
    gates = fetch([(gate_hbm.at[s, :], gate_ref.at[t, :]) for s, t in places], gate_sems)
    maps = fetch(
        [
            (map_hbm.at[head, s, :], map_ref.at[head, t, :])
            for head in range(heads)
            for s, t in places
        ],
        map_sems,
    )
    for i, state in enumerate(states):
        state_ref[partner(i, swap.heads)] = state[...]
    for copy in gates:
        copy.wait()
    gain = gain_ref[...]
    for head in range(heads):
        lanes = slice(head * DV, (head + 1) * DV)
        gate = gate_ref[:, lanes]
        factor = gate / (1.0 + jnp.exp(-gate)) * gain
        for copy in maps[head * len(blocks) : (head + 1) * len(blocks)]:
            copy.wait()
        core = map_ref[head, :, DK:] + dot(map_ref[head, :, :DK], state_ref[head])
        scale = lax.rsqrt(jnp.mean(core * core, axis=-1, keepdims=True) + EPS)
        high_ref[:, lanes], low_ref[:, lanes] = split(core * scale * factor)
    total = len(blocks) * rows
    for band in range(0, parts_ref.shape[2], BAND):
        lanes = slice(band, band + BAND)
        both = jnp.concatenate([high_ref[...], low_ref[...]], axis=0)
        sums = jnp.dot(both, parts_ref[0, :, lanes], preferred_element_type=jnp.float32)
        last = jnp.dot(high_ref[...], parts_ref[1, :, lanes], preferred_element_type=jnp.float32)
        result = sums[:total] + (sums[total:] + last)
        for (index, start), out_ref in zip(pieces, outs):
            if start <= band < start + out_ref.shape[1]:
                at = blocks.index(index) * rows
                out_ref[:, band - start : band - start + BAND] = result[at : at + rows]


def forward_kernel(across_ref, own_ref, up_ref, down_ref, _, going_ref, staying_ref, __):
    outward = lax.axis_index("tp") == 1
    up, down = up_ref[...], down_ref[...]
    going_ref[...] = across_ref[...] + jnp.where(outward, up, down)
    staying_ref[...] = own_ref[...] + jnp.where(outward, down, up)


def shape(*dims):
    return jax.ShapeDtypeStruct(dims, jnp.float32)


def params(mebibytes):
    return pltpu.CompilerParams(vmem_limit_bytes=int(mebibytes * 1024 * 1024))


def cost(flops, *arrays):
    return pl.CostEstimate(
        flops=flops, bytes_accessed=4 * sum(a.size for a in arrays), transcendentals=0
    )


def partners_swap(arrays, axis):
    count = len(arrays)
    arrays = list(arrays)
    for i in [i for i in SWAP_ORDER if i < count]:
        arrays[i] = lax.ppermute(arrays[i], axis, [(d, d ^ i) for d in range(count)])
    return arrays


class Swap(typing.NamedTuple):
    heads: bool
    rows: bool


def swap_is_possible(heads, count):
    return heads == count and count & (count - 1) == 0 and count <= 8


def entering_states(factors, summaries, swap, beside, after):
    heads = factors.shape[0] - 1
    count = lax.axis_size("ctx")
    if swap:
        held = partners_swap([factors, *summaries], "ctx")
        held, beside = lax.optimization_barrier((held, beside))
        entry = shape(DK, DV)
        entries = pl.pallas_call(
            ordered_scan_kernel,
            in_specs=[HBM] + [VMEM] * (count - 1),
            out_specs=[VMEM] * count,
            out_shape=[entry] * count,
            scratch_shapes=[
                pltpu.VMEM((count, DK, DK + DV), jnp.float32),
                pltpu.VMEM((count, DK, DV), jnp.float32),
                pltpu.SemaphoreType.DMA((1,)),
            ],
            compiler_params=params(SCAN_VMEM),
            name="state_scan",
        )(*held)
        entries, after = lax.optimization_barrier((entries, after))
        return partners_swap(entries, "ctx"), beside, after
    parts = max(1, count // heads)
    per_owner = max(1, heads // count)
    width = DV // parts
    groups = heads // per_owner
    summary = jnp.stack(summaries)
    maps = summary[:, :, :DK].reshape(groups, 1, per_owner, DK, DK)
    maps = jnp.broadcast_to(maps, (groups, parts, per_owner, DK, DK))
    adds = summary[:, :, DK:].reshape(groups, per_owner, DK, parts, width)
    payload = jnp.concatenate([maps, adds.transpose(0, 3, 1, 2, 4)], axis=-1)
    payload = payload.reshape(count, per_owner, DK, DK + width)
    held = lax.all_to_all(payload, "ctx", split_axis=0, concat_axis=0, tiled=True)
    entries = pl.pallas_call(
        scan_kernel,
        out_shape=shape(count, per_owner, DK, width),
        compiler_params=params(32),
        name="state_scan",
    )(held)
    back = lax.all_to_all(entries, "ctx", split_axis=0, concat_axis=0, tiled=True)
    back = back.reshape(groups, parts, per_owner, DK, width).transpose(0, 2, 3, 1, 4)
    back = back.reshape(heads, DK, DV)
    return [back[head] for head in range(heads)], beside, after


def project_and_sum(project, columns, axis):
    count = lax.axis_size(axis)
    if count != 4:
        whole = jnp.concatenate(project([(i, 0, columns) for i in range(count)], LATER_VMEM), axis=0)
        return lax.psum_scatter(whole, axis, scatter_dimension=0, tiled=True)
    (opposite,) = project([(3, 0, columns)], FIRST_VMEM)
    up = lax.ppermute(opposite, axis, [(0, 1), (1, 2)])
    down = lax.ppermute(opposite, axis, [(3, 2), (2, 1)])
    across, own, near = project([(i, 0, columns) for i in (2, 0, 1)], LATER_VMEM)
    anywhere = pl.BlockSpec(memory_space=pl.ANY)
    going, staying, near = pl.pallas_call(
        forward_kernel,
        in_specs=[VMEM] * 4 + [anywhere],
        out_specs=[VMEM] * 2 + [anywhere],
        out_shape=[shape(*own.shape)] * 3,
        input_output_aliases={4: 2},
        compiler_params=params(LATER_VMEM),
        name="forward",
    )(across, own, up, down, near)
    from_across = lax.ppermute(going, axis, [(i, i ^ 2) for i in range(4)])
    from_near = lax.ppermute(near, axis, [(i, i ^ 1) for i in range(4)])
    return (staying + from_near) + from_across


def per_device(queries, key_vectors, values, decays, strengths, out_gate, norm_gain, out_weight):
    tokens = queries.shape[0]
    heads = values.shape[1] // DV
    key_heads = queries.shape[1] // DK
    depth, columns = out_weight.shape
    rows = tokens // lax.axis_size("tp")
    gain = norm_gain.reshape(1, DV)
    swap = Swap(
        heads=swap_is_possible(heads, lax.axis_size("ctx")), rows=lax.axis_size("tp") == 4
    )

    def buffers(*arrays):
        return [pltpu.VMEM(a.shape, a.dtype) for a in arrays] + [
            pltpu.SemaphoreType.DMA((len(arrays),))
        ]

    factor_shape = shape(heads, tokens, DK + DV)
    groups = pl.cdiv(heads, HEADS_AT_ONCE)
    sent = heads - 1 if swap.heads else heads
    factors, *summaries = pl.pallas_call(
        functools.partial(summary_kernel, swap=swap.heads),
        in_specs=[HBM] * 4,
        out_specs=[HBM] + [VMEM] * sent,
        out_shape=[shape(heads + 1, tokens, DK + DV)] + [shape(DK, DK + DV)] * sent,
        scratch_shapes=buffers(decays, strengths, key_vectors, values)
        + [pltpu.VMEM(factor_shape.shape, jnp.float32), pltpu.VMEM((heads, DK, DK + DV), jnp.float32)]
        + [pltpu.SemaphoreType.DMA((groups + 1,))],
        compiler_params=params(MOST_VMEM),
        name="state_summary",
    )(decays, strengths, key_vectors, values)
    maps = pl.pallas_call(
        output_kernel,
        in_specs=[HBM] * 4,
        out_specs=HBM,
        out_shape=factor_shape,
        scratch_shapes=[pltpu.VMEM(a.shape, jnp.float32) for a in (decays, queries, key_vectors)]
        + [pltpu.VMEM(factor_shape.shape, jnp.float32), pltpu.SemaphoreType.DMA((3 + key_heads,))]
        + [pltpu.VMEM(factor_shape.shape, jnp.float32), pltpu.SemaphoreType.DMA((key_heads,))],
        compiler_params=params(MOST_VMEM),
        cost_estimate=cost(3 * 2 * heads * tokens * tokens * 384, factors, factors, queries),
        name="output_maps",
    )(decays, queries, key_vectors, factors)
    states, maps, weights = entering_states(factors, summaries, swap.heads, maps, out_weight)
    parts = pl.pallas_call(
        weight_kernel,
        in_specs=[HBM],
        out_shape=jax.ShapeDtypeStruct((2, depth, columns), jnp.bfloat16),
        scratch_shapes=[
            pltpu.VMEM(out_weight.shape, jnp.float32),
            pltpu.SemaphoreType.DMA((depth // WEIGHT_ROWS,)),
        ],
        compiler_params=params(WEIGHT_VMEM),
        cost_estimate=cost(6 * weights.size, weights, weights),
        name="weight_parts",
    )(weights)

    def project(pieces, vmem):
        total = len({piece[0] for piece in pieces}) * rows
        normed = pltpu.VMEM((total, depth), jnp.bfloat16)
        counts = (total // rows, heads * total // rows)
        return pl.pallas_call(
            functools.partial(
                projection_kernel, pieces=[(index, start) for index, start, _ in pieces], swap=swap
            ),
            in_specs=[HBM] * 2 + [VMEM] * (2 + heads),
            out_shape=[shape(rows, width) for _, _, width in pieces],
            scratch_shapes=[
                pltpu.VMEM((heads, total, DK + DV), jnp.float32),
                pltpu.VMEM((total, heads * DV), jnp.float32),
                pltpu.VMEM((heads, DK, DV), jnp.float32),
                normed,
                normed,
            ]
            + [pltpu.SemaphoreType.DMA((n,)) for n in counts],
            compiler_params=params(vmem),
            cost_estimate=cost(3 * 2 * total * depth * columns, out_weight),
            name="projection",
        )(maps, out_gate, gain, parts, *states)

    return project_and_sum(project, columns, "tp")


def solution(mesh):
    return jax.shard_map(
        per_device,
        mesh=mesh,
        in_specs=(
            P("ctx", "tp"),
            P("ctx", "tp"),
            P("ctx", "tp"),
            P("tp", "ctx"),
            P("tp", "ctx"),
            P("ctx", "tp"),
            P(),
            P("tp", None),
        ),
        out_specs=P(("ctx", "tp"), None),
        check_vma=False,
    )
```

```python
import functools
import typing

import jax
import jax.numpy as jnp
from jax import lax
from jax.experimental import pallas as pl
from jax.experimental.pallas import tpu as pltpu
from jax.sharding import PartitionSpec as P

DK = 128
DV = 128
BLOCK = 128
SMALL = 32
BAND = 256
SWAP_ORDER = (7, 6, 5, 4, 3, 2, 1)
WEIGHT_ROWS = 128
MOST_VMEM = 56
SCAN_VMEM = 52.25
WEIGHT_VMEM = 40
FIRST_VMEM = 24
LATER_VMEM = 24
HEADS_AT_ONCE = 8
EPS = 1e-06


HBM = pl.BlockSpec(memory_space=pltpu.HBM)
VMEM = pl.BlockSpec(memory_space=pltpu.VMEM)


def dot(left, right):
    return jnp.dot(left, right, precision=lax.Precision.HIGH, preferred_element_type=jnp.float32)


def dot_transposed(left, right):
    return lax.dot_general(
        left,
        right,
        (((1,), (1,)), ((), ())),
        precision=lax.Precision.HIGH,
        preferred_element_type=jnp.float32,
    )


def iota(shape, dim):
    return lax.broadcasted_iota(jnp.int32, shape, dim)


def unit(rows):
    return rows * lax.rsqrt(jnp.sum(rows * rows, axis=-1, keepdims=True) + EPS)


def cumulative_logs(decays):
    tokens = decays.shape[1]
    upto = jnp.where(iota((tokens, tokens), 0) <= iota((tokens, tokens), 1), 1.0, 0.0)
    rows = jnp.dot(
        jnp.log(decays), upto, precision=lax.Precision.HIGHEST, preferred_element_type=jnp.float32
    )
    return rows, rows.T


def split(value):
    high = value.astype(jnp.bfloat16)
    return high, (value - high.astype(jnp.float32)).astype(jnp.bfloat16)


def dot_parts(left, right):
    rows = left[0].shape[0]
    both = jnp.concatenate(left, axis=0)
    sums = jnp.dot(both, right[0], preferred_element_type=jnp.float32)
    rest = jnp.dot(left[0], right[1], preferred_element_type=jnp.float32)
    return sums[:rows] + (sums[rows:] + rest)


def stack_parts(*values):
    return tuple(jnp.concatenate(pieces, axis=0) for pieces in zip(*values))


def spread_parts(parts, masks):
    return tuple(jnp.concatenate([part * mask for mask in masks], axis=0) for part in parts)


def lower_inverses(lowers):
    row = iota((SMALL, BLOCK), 0)
    lane = iota((SMALL, BLOCK), 1)
    column = lane % SMALL
    place = lane // SMALL
    eye = jnp.where(row == column, 1.0, 0.0)
    in_8 = row // 8 == column // 8
    in_16 = row // 16 == column // 16
    odd = place % 2 == 1
    masks = [
        jnp.where(place == index, 1.0, 0.0).astype(jnp.bfloat16) for index in range(BLOCK // SMALL)
    ]
    packed = []
    for lower in lowers:
        blocks = jnp.zeros((SMALL, BLOCK), jnp.float32)
        for index in range(BLOCK // SMALL):
            blocks = jnp.where(place == index, lower[index * SMALL : (index + 1) * SMALL], blocks)
        packed.append(blocks)
    nil = [jnp.where(in_8, blocks, 0.0) for blocks in packed]
    parts = [split(n) for n in nil]
    nil_2 = [split(dot_parts(n, spread_parts(n, masks))) for n in parts]
    start = [eye - n for n in nil]
    pairs = [
        dot_parts(stack_parts(n, split(s)), spread_parts(n, masks)) for n, s in zip(nil_2, start)
    ]
    start = [s + pair[SMALL:] for s, pair in zip(start, pairs)]
    nil_4 = [spread_parts(split(pair[:SMALL]), masks) for pair in pairs]
    inv = [s + dot_parts(split(s), n) for s, n in zip(start, nil_4)]
    step_16 = [
        spread_parts(split(jnp.where(in_16 & ~in_8, blocks, 0.0)), masks) for blocks in packed
    ]
    half = [jnp.concatenate([d[8:16], d[24:32]], axis=0) for d in inv]
    half = [dot_parts(split(h), w) for h, w in zip(half, step_16)]
    half = [dot_parts(split(h), spread_parts(split(d), masks)) for h, d in zip(half, inv)]
    inv = [
        jnp.concatenate([d[:8], d[8:16] - h[:8], d[16:24], d[24:] - h[8:]], axis=0)
        for d, h in zip(inv, half)
    ]
    step_32 = [spread_parts(split(jnp.where(in_16, 0.0, blocks)), masks) for blocks in packed]
    half = [dot_parts(split(d[16:]), w) for d, w in zip(inv, step_32)]
    half = [dot_parts(split(h), spread_parts(split(d), masks)) for h, d in zip(half, inv)]
    inv = [jnp.concatenate([d[:16], d[16:] - h], axis=0) for d, h in zip(inv, half)]
    wide = [spread_parts(split(d), masks) for d in inv]
    low = [jnp.where(odd, d, 0.0) for d in inv]
    zeros = jnp.zeros((SMALL, BLOCK), jnp.bfloat16)
    step_64 = []
    for lower in lowers:
        below = jnp.where(place == 0, lower[32:64], jnp.where(place == 2, lower[96:128], 0.0))
        step_64.append(
            tuple(
                jnp.concatenate([zeros, part * masks[0], zeros, part * masks[2]], axis=0)
                for part in split(below)
            )
        )
    half = [dot_parts(split(l), w) for l, w in zip(low, step_64)]
    half = [dot_parts(split(h), w) for h, w in zip(half, wide)]
    inv = [
        jnp.concatenate([jnp.where(odd, 0.0, d), l - h], axis=0) for d, l, h in zip(inv, low, half)
    ]
    left = iota((64, BLOCK), 1) < 64
    low = [jnp.where(left, 0.0, d) for d in inv]
    wide = [jnp.concatenate([jnp.where(left, d, 0.0), l], axis=0) for d, l in zip(inv, low)]
    wide_parts = [split(w) for w in wide]
    zeros = jnp.zeros((64, BLOCK), jnp.bfloat16)
    step_128 = [
        tuple(
            jnp.concatenate([zeros, part], axis=0) for part in split(jnp.where(left, lower[64:], 0.0))
        )
        for lower in lowers
    ]
    half = [dot_parts(tuple(part[64:] for part in l), w) for l, w in zip(wide_parts, step_128)]
    half = [dot_parts(split(h), w) for h, w in zip(half, wide_parts)]
    return [
        tuple(
            jnp.concatenate([high, low], axis=0)
            for high, low in zip((part[:64] for part in parts), split(w[64:] - h))
        )
        for parts, w, h in zip(wide_parts, wide, half)
    ]


def block(index):
    return slice(index * BLOCK, (index + 1) * BLOCK)


def fetch(pairs, sems):
    copies = [pltpu.make_async_copy(src, dst, sems.at[i]) for i, (src, dst) in enumerate(pairs)]
    for copy in copies:
        copy.start()
    return copies


def partner(place, swap):
    return lax.axis_index("ctx") ^ (0, *SWAP_ORDER)[place] if swap else place


def summary_kernel(decay_hbm, strength_hbm, k_hbm, v_hbm, factor_hbm, *rest, swap):
    *summaries, decay_ref, strength_ref, k_ref, v_ref, sems, factor_ref, summary_ref, out_sems = rest
    copies = fetch(
        [(decay_hbm, decay_ref), (strength_hbm, strength_ref), (k_hbm, k_ref), (v_hbm, v_ref)], sems
    )
    for copy in copies[:3]:
        copy.wait()
    tokens = k_ref.shape[0]
    key_heads = k_ref.shape[1] // DK
    value_heads = v_ref.shape[1] // DV
    repeat = value_heads // key_heads
    blocks = tokens // BLOCK
    rows, columns = cumulative_logs(decay_ref[...])
    strengths = strength_ref[...].T
    strict = iota((BLOCK, BLOCK), 0) > iota((BLOCK, BLOCK), 1)
    eye = jnp.where(iota((BLOCK, DK + DV), 0) == iota((BLOCK, DK + DV), 1), 1.0, 0.0)
    leaving = []
    for first in range(0, value_heads, HEADS_AT_ONCE):
        heads = range(first, min(first + HEADS_AT_ONCE, value_heads))
        keys = {}
        gram = {}
        for key_head in sorted({head // repeat for head in heads}):
            unit_rows = unit(k_ref[:, key_head * DK : (key_head + 1) * DK])
            keys[key_head] = [unit_rows[block(p)] for p in range(blocks)]
            gram[key_head] = {
                (p, r): dot_transposed(keys[key_head][p], keys[key_head][r])
                for p in range(blocks)
                for r in range(p + 1)
            }
        lower = {}
        for head in heads:
            for p in range(blocks):
                at = columns[block(p), head : head + 1]
                weight = strengths[block(p), head : head + 1]
                for r in range(p + 1):
                    spread = at - rows[head : head + 1, block(r)]
                    if p == r:
                        damp = jnp.where(strict, jnp.exp(jnp.where(strict, spread, 0.0)), 0.0)
                    else:
                        damp = jnp.exp(spread)
                    lower[head, p, r] = weight * gram[head // repeat][p, r] * damp
        inverse = lower_inverses([lower[head, p, p] for head in heads for p in range(blocks)])
        inverse = {
            (head, p): inverse[i * blocks + p] for i, head in enumerate(heads) for p in range(blocks)
        }
        if first == 0:
            copies[3].wait()
        factors = {}
        for p in range(blocks):
            for head in heads:
                at = columns[block(p), head : head + 1]
                weight = strengths[block(p), head : head + 1]
                right = jnp.concatenate(
                    [
                        keys[head // repeat][p] * (-weight * jnp.exp(at)),
                        v_ref[block(p), head * DV : (head + 1) * DV] * weight,
                    ],
                    axis=1,
                )
                for r in range(p):
                    right = right - dot_parts(split(lower[head, p, r]), split(factors[head, r]))
                factors[head, p] = dot_parts(inverse[head, p], split(right))
                factor_ref[head, block(p), :] = factors[head, p]
        flipped = {key_head: [split(k.T) for k in keys[key_head]] for key_head in keys}
        for head in heads:
            last = rows[head : head + 1, tokens - 1 : tokens]
            total = jnp.exp(last) * eye
            for p in range(blocks):
                ending = jnp.exp(last - columns[block(p), head : head + 1])
                total = total + dot_parts(flipped[head // repeat][p], split(factors[head, p] * ending))
            summary_ref[head] = total
        group = pl.ds(first, len(heads))
        leaving.append(
            pltpu.make_async_copy(
                factor_ref.at[group], factor_hbm.at[group], out_sems.at[len(leaving)]
            )
        )
        leaving[-1].start()
    if swap:
        target = factor_hbm.at[value_heads, pl.ds(0, DK)]
        leaving.append(
            pltpu.make_async_copy(summary_ref.at[partner(0, swap)], target, out_sems.at[len(leaving)])
        )
        leaving[-1].start()
    for place, out_ref in enumerate(summaries):
        out_ref[...] = summary_ref[partner(place + 1 if swap else place, swap)]
    for copy in leaving:
        copy.wait()


def output_kernel(
    decay_hbm,
    q_hbm,
    k_hbm,
    factor_hbm,
    map_hbm,
    decay_ref,
    q_ref,
    k_ref,
    factor_ref,
    sems,
    map_ref,
    out_sems,
):
    repeat = factor_ref.shape[0] // (k_hbm.shape[1] // DK)
    groups = [pl.ds(head, repeat) for head in range(0, factor_ref.shape[0], repeat)]
    copies = fetch(
        [(decay_hbm, decay_ref), (q_hbm, q_ref), (k_hbm, k_ref)]
        + [(factor_hbm.at[group], factor_ref.at[group]) for group in groups],
        sems,
    )
    leaving = []
    for copy in copies[:3]:
        copy.wait()
    tokens = q_ref.shape[0]
    key_heads = q_ref.shape[1] // DK
    value_heads = factor_ref.shape[0]
    repeat = value_heads // key_heads
    blocks = tokens // BLOCK
    rows, columns = cumulative_logs(decay_ref[...])
    inclusive = iota((BLOCK, BLOCK), 0) >= iota((BLOCK, BLOCK), 1)
    for key_head in range(key_heads):
        lanes = slice(key_head * DK, (key_head + 1) * DK)
        queries = unit(q_ref[:, lanes]) * DK**-0.5
        keys = unit(k_ref[:, lanes])
        for p in range(blocks):
            scores = [dot_transposed(queries[block(p)], keys[block(r)]) for r in range(p + 1)]
            if p == 0:
                copies[3 + key_head].wait()
            for head in range(key_head * repeat, (key_head + 1) * repeat):
                at = columns[block(p), head : head + 1]
                total = jnp.concatenate(
                    [queries[block(p)] * jnp.exp(at), jnp.zeros((BLOCK, DV), jnp.float32)], axis=1
                )
                for r in range(p + 1):
                    spread = at - rows[head : head + 1, block(r)]
                    if p == r:
                        damp = jnp.where(inclusive, jnp.exp(jnp.where(inclusive, spread, 0.0)), 0.0)
                    else:
                        damp = jnp.exp(spread)
                    total = total + dot(scores[r] * damp, factor_ref[head, block(r), :])
                map_ref[head, block(p), :] = total
        group = groups[key_head]
        leaving.append(
            pltpu.make_async_copy(map_ref.at[group], map_hbm.at[group], out_sems.at[key_head])
        )
        leaving[-1].start()
    for copy in leaving:
        copy.wait()


def scan_kernel(held_ref, entry_ref):
    count, held, key_width, width = entry_ref.shape
    for head in range(held):
        state = jnp.zeros((key_width, width), jnp.float32)
        entry_ref[0, head] = state
        for source in range(count - 1):
            added = held_ref[source, head, :, key_width:]
            if source:
                added = added + dot(held_ref[source, head, :, :key_width], state)
            state = added
            entry_ref[source + 1, head] = state


def ordered_scan_kernel(factor_hbm, *rest):
    *arrays, held_ref, entry_ref, sems = rest
    count = entry_ref.shape[0]
    held, entries = arrays[: count - 1], arrays[count - 1 :]
    here = partner(0, True)
    own_summary = factor_hbm.at[factor_hbm.shape[0] - 1, pl.ds(0, DK)]
    own = pltpu.make_async_copy(own_summary, held_ref.at[here], sems.at[0])
    own.start()
    for i, summary in enumerate(held):
        held_ref[partner(i + 1, True)] = summary[...]
    own.wait()
    state = jnp.zeros(entry_ref.shape[1:], jnp.float32)
    entry_ref[0] = state
    for source in range(count - 1):
        added = held_ref[source, :, DK:]
        if source:
            added = added + dot(held_ref[source, :, :DK], state)
        state = added
        entry_ref[source + 1] = state
    for i, entry in enumerate(entries):
        entry[...] = entry_ref[partner(i, True)]


def weight_kernel(weight_hbm, parts_ref, weight_ref, sems):
    bands = [pl.ds(row, WEIGHT_ROWS) for row in range(0, weight_ref.shape[0], WEIGHT_ROWS)]
    copies = fetch([(weight_hbm.at[band, :], weight_ref.at[band, :]) for band in bands], sems)
    for copy, band in zip(copies, bands):
        copy.wait()
        parts_ref[0, band, :], parts_ref[1, band, :] = split(weight_ref[band, :])


def projection_kernel(map_hbm, gate_hbm, gain_ref, parts_ref, *rest, pieces, swap):
    *arrays, map_ref, gate_ref, state_ref, high_ref, low_ref, gate_sems, map_sems = rest
    outs = arrays[-len(pieces) :]
    states = arrays[: -len(pieces)]
    heads = state_ref.shape[0]
    rows = outs[0].shape[0]
    blocks = sorted({index for index, _ in pieces})
    places = []
    for i, index in enumerate(blocks):
        start = (lax.axis_index("tp") ^ index) * rows if swap.rows else index * rows
        places.append((pl.ds(pl.multiple_of(start, rows), rows), pl.ds(i * rows, rows)))
    gates = fetch([(gate_hbm.at[s, :], gate_ref.at[t, :]) for s, t in places], gate_sems)
    maps = fetch(
        [
            (map_hbm.at[head, s, :], map_ref.at[head, t, :])
            for head in range(heads)
            for s, t in places
        ],
        map_sems,
    )
    for i, state in enumerate(states):
        state_ref[partner(i, swap.heads)] = state[...]
    for copy in gates:
        copy.wait()
    gain = gain_ref[...]
    for head in range(heads):
        lanes = slice(head * DV, (head + 1) * DV)
        gate = gate_ref[:, lanes]
        factor = gate / (1.0 + jnp.exp(-gate)) * gain
        for copy in maps[head * len(blocks) : (head + 1) * len(blocks)]:
            copy.wait()
        core = map_ref[head, :, DK:] + dot(map_ref[head, :, :DK], state_ref[head])
        scale = lax.rsqrt(jnp.mean(core * core, axis=-1, keepdims=True) + EPS)
        high_ref[:, lanes], low_ref[:, lanes] = split(core * scale * factor)
    total = len(blocks) * rows
    for band in range(0, parts_ref.shape[2], BAND):
        lanes = slice(band, band + BAND)
        both = jnp.concatenate([high_ref[...], low_ref[...]], axis=0)
        sums = jnp.dot(both, parts_ref[0, :, lanes], preferred_element_type=jnp.float32)
        last = jnp.dot(high_ref[...], parts_ref[1, :, lanes], preferred_element_type=jnp.float32)
        result = sums[:total] + (sums[total:] + last)
        for (index, start), out_ref in zip(pieces, outs):
            if start <= band < start + out_ref.shape[1]:
                at = blocks.index(index) * rows
                out_ref[:, band - start : band - start + BAND] = result[at : at + rows]


def forward_kernel(across_ref, end_ref, going_ref):
    going_ref[...] = across_ref[...] + end_ref[...]


def hand_on_kernel(_, __, ___):
    pass


def shape(*dims):
    return jax.ShapeDtypeStruct(dims, jnp.float32)


def params(mebibytes):
    return pltpu.CompilerParams(vmem_limit_bytes=int(mebibytes * 1024 * 1024))


def cost(flops, *arrays):
    return pl.CostEstimate(
        flops=flops, bytes_accessed=4 * sum(a.size for a in arrays), transcendentals=0
    )


def partners_swap(arrays, axis):
    count = len(arrays)
    return [arrays[0]] + [
        lax.ppermute(array, axis, [(d, d ^ i) for d in range(count)])
        for array, i in zip(arrays[1:], SWAP_ORDER)
    ]


class Swap(typing.NamedTuple):
    heads: bool
    rows: bool


def swap_is_possible(heads, count):
    return heads == count == 1 + len(SWAP_ORDER)


def entering_states(factors, summaries, swap, beside, after):
    heads = factors.shape[0] - 1
    count = lax.axis_size("ctx")
    if swap:
        held = partners_swap([factors, *summaries], "ctx")
        held, beside = lax.optimization_barrier((held, beside))
        entry = shape(DK, DV)
        entries = pl.pallas_call(
            ordered_scan_kernel,
            in_specs=[HBM] + [VMEM] * (count - 1),
            out_specs=[VMEM] * count,
            out_shape=[entry] * count,
            scratch_shapes=[
                pltpu.VMEM((count, DK, DK + DV), jnp.float32),
                pltpu.VMEM((count, DK, DV), jnp.float32),
                pltpu.SemaphoreType.DMA((1,)),
            ],
            compiler_params=params(SCAN_VMEM),
            name="state_scan",
        )(*held)
        entries, after = lax.optimization_barrier((entries, after))
        return partners_swap(entries, "ctx"), beside, after
    parts = max(1, count // heads)
    per_owner = max(1, heads // count)
    width = DV // parts
    groups = heads // per_owner
    summary = jnp.stack(summaries)
    maps = summary[:, :, :DK].reshape(groups, 1, per_owner, DK, DK)
    maps = jnp.broadcast_to(maps, (groups, parts, per_owner, DK, DK))
    adds = summary[:, :, DK:].reshape(groups, per_owner, DK, parts, width)
    payload = jnp.concatenate([maps, adds.transpose(0, 3, 1, 2, 4)], axis=-1)
    payload = payload.reshape(count, per_owner, DK, DK + width)
    held = lax.all_to_all(payload, "ctx", split_axis=0, concat_axis=0, tiled=True)
    entries = pl.pallas_call(
        scan_kernel,
        out_shape=shape(count, per_owner, DK, width),
        compiler_params=params(32),
        name="state_scan",
    )(held)
    back = lax.all_to_all(entries, "ctx", split_axis=0, concat_axis=0, tiled=True)
    back = back.reshape(groups, parts, per_owner, DK, width).transpose(0, 2, 3, 1, 4)
    back = back.reshape(heads, DK, DV)
    return [back[head] for head in range(heads)], beside, after


def project_and_sum(project, columns, axis):
    count = lax.axis_size(axis)
    if count != 4:
        whole = jnp.concatenate(project([(i, 0, columns) for i in range(count)], LATER_VMEM), axis=0)
        return lax.psum_scatter(whole, axis, scatter_dimension=0, tiled=True)
    (opposite,) = project([(3, 0, columns)], FIRST_VMEM)
    from_end = lax.ppermute(opposite, axis, [(0, 1), (3, 2)])
    from_inner = lax.ppermute(opposite, axis, [(1, 2), (2, 1)])
    across, own, near = project([(i, 0, columns) for i in (2, 0, 1)], LATER_VMEM)
    going = pl.pallas_call(
        forward_kernel,
        out_shape=shape(*own.shape),
        compiler_params=params(LATER_VMEM),
        name="forward",
    )(across, from_end)
    anywhere = pl.BlockSpec(memory_space=pl.ANY)
    near = pl.pallas_call(
        hand_on_kernel,
        in_specs=[anywhere] * 2,
        out_specs=anywhere,
        out_shape=shape(*near.shape),
        input_output_aliases={0: 0},
        compiler_params=params(LATER_VMEM),
        name="hand_on",
    )(near, going)
    from_near = lax.ppermute(near, axis, [(i, i ^ 1) for i in range(4)])
    from_across = lax.ppermute(going, axis, [(i, i ^ 2) for i in range(4)])
    return ((own + from_inner) + from_near) + from_across


def per_device(queries, key_vectors, values, decays, strengths, out_gate, norm_gain, out_weight):
    tokens = queries.shape[0]
    heads = values.shape[1] // DV
    key_heads = queries.shape[1] // DK
    depth, columns = out_weight.shape
    rows = tokens // lax.axis_size("tp")
    gain = norm_gain.reshape(1, DV)
    swap = Swap(
        heads=swap_is_possible(heads, lax.axis_size("ctx")), rows=lax.axis_size("tp") == 4
    )

    def buffers(*arrays):
        return [pltpu.VMEM(a.shape, a.dtype) for a in arrays] + [
            pltpu.SemaphoreType.DMA((len(arrays),))
        ]

    factor_shape = shape(heads, tokens, DK + DV)
    groups = pl.cdiv(heads, HEADS_AT_ONCE)
    sent = heads - 1 if swap.heads else heads
    factors, *summaries = pl.pallas_call(
        functools.partial(summary_kernel, swap=swap.heads),
        in_specs=[HBM] * 4,
        out_specs=[HBM] + [VMEM] * sent,
        out_shape=[shape(heads + 1, tokens, DK + DV)] + [shape(DK, DK + DV)] * sent,
        scratch_shapes=buffers(decays, strengths, key_vectors, values)
        + [pltpu.VMEM(factor_shape.shape, jnp.float32), pltpu.VMEM((heads, DK, DK + DV), jnp.float32)]
        + [pltpu.SemaphoreType.DMA((groups + 1,))],
        compiler_params=params(MOST_VMEM),
        name="state_summary",
    )(decays, strengths, key_vectors, values)
    maps = pl.pallas_call(
        output_kernel,
        in_specs=[HBM] * 4,
        out_specs=HBM,
        out_shape=factor_shape,
        scratch_shapes=[pltpu.VMEM(a.shape, jnp.float32) for a in (decays, queries, key_vectors)]
        + [pltpu.VMEM(factor_shape.shape, jnp.float32), pltpu.SemaphoreType.DMA((3 + key_heads,))]
        + [pltpu.VMEM(factor_shape.shape, jnp.float32), pltpu.SemaphoreType.DMA((key_heads,))],
        compiler_params=params(MOST_VMEM),
        cost_estimate=cost(3 * 2 * heads * tokens * tokens * 384, factors, factors, queries),
        name="output_maps",
    )(decays, queries, key_vectors, factors)
    states, maps, weights = entering_states(factors, summaries, swap.heads, maps, out_weight)
    parts = pl.pallas_call(
        weight_kernel,
        in_specs=[HBM],
        out_shape=jax.ShapeDtypeStruct((2, depth, columns), jnp.bfloat16),
        scratch_shapes=[
            pltpu.VMEM(out_weight.shape, jnp.float32),
            pltpu.SemaphoreType.DMA((depth // WEIGHT_ROWS,)),
        ],
        compiler_params=params(WEIGHT_VMEM),
        cost_estimate=cost(6 * weights.size, weights, weights),
        name="weight_parts",
    )(weights)

    def project(pieces, vmem):
        total = len({piece[0] for piece in pieces}) * rows
        normed = pltpu.VMEM((total, depth), jnp.bfloat16)
        counts = (total // rows, heads * total // rows)
        return pl.pallas_call(
            functools.partial(
                projection_kernel, pieces=[(index, start) for index, start, _ in pieces], swap=swap
            ),
            in_specs=[HBM] * 2 + [VMEM] * (2 + heads),
            out_shape=[shape(rows, width) for _, _, width in pieces],
            scratch_shapes=[
                pltpu.VMEM((heads, total, DK + DV), jnp.float32),
                pltpu.VMEM((total, heads * DV), jnp.float32),
                pltpu.VMEM((heads, DK, DV), jnp.float32),
                normed,
                normed,
            ]
            + [pltpu.SemaphoreType.DMA((n,)) for n in counts],
            compiler_params=params(vmem),
            cost_estimate=cost(3 * 2 * total * depth * columns, out_weight),
            name="projection",
        )(maps, out_gate, gain, parts, *states)

    return project_and_sum(project, columns, "tp")


def solution(mesh):
    return jax.shard_map(
        per_device,
        mesh=mesh,
        in_specs=(
            P("ctx", "tp"),
            P("ctx", "tp"),
            P("ctx", "tp"),
            P("tp", "ctx"),
            P("tp", "ctx"),
            P("ctx", "tp"),
            P(),
            P("tp", None),
        ),
        out_specs=P(("ctx", "tp"), None),
        check_vma=False,
    )
```

```python
import functools
import typing

import jax
import jax.numpy as jnp
from jax import lax
from jax.experimental import pallas as pl
from jax.experimental.pallas import tpu as pltpu
from jax.sharding import PartitionSpec as P

DK = 128
DV = 128
BLOCK = 128
SMALL = 32
BAND = 256
SWAP_ORDER = (7, 6, 5, 4, 3, 2, 1)
WEIGHT_ROWS = 256
MOST_VMEM = 56
SCAN_VMEM = 52.25
FIRST_VMEM = 40
LATER_VMEM = 32
HEADS_AT_ONCE = 8
EPS = 1e-06


HBM = pl.BlockSpec(memory_space=pltpu.HBM)
VMEM = pl.BlockSpec(memory_space=pltpu.VMEM)


def dot(left, right):
    return jnp.dot(left, right, precision=lax.Precision.HIGH, preferred_element_type=jnp.float32)


def dot_transposed(left, right):
    return lax.dot_general(
        left,
        right,
        (((1,), (1,)), ((), ())),
        precision=lax.Precision.HIGH,
        preferred_element_type=jnp.float32,
    )


def iota(shape, dim):
    return lax.broadcasted_iota(jnp.int32, shape, dim)


def unit(rows):
    return rows * lax.rsqrt(jnp.sum(rows * rows, axis=-1, keepdims=True) + EPS)


def cumulative_logs(decays):
    tokens = decays.shape[1]
    upto = jnp.where(iota((tokens, tokens), 0) <= iota((tokens, tokens), 1), 1.0, 0.0)
    rows = jnp.dot(
        jnp.log(decays), upto, precision=lax.Precision.HIGHEST, preferred_element_type=jnp.float32
    )
    return rows, rows.T


def split(value):
    high = value.astype(jnp.bfloat16)
    return high, (value - high.astype(jnp.float32)).astype(jnp.bfloat16)


def dot_parts(left, right):
    rows = left[0].shape[0]
    both = jnp.concatenate(left, axis=0)
    sums = jnp.dot(both, right[0], preferred_element_type=jnp.float32)
    rest = jnp.dot(left[0], right[1], preferred_element_type=jnp.float32)
    return sums[:rows] + (sums[rows:] + rest)


def stack_parts(*values):
    return tuple(jnp.concatenate(pieces, axis=0) for pieces in zip(*values))


def spread_parts(parts, masks):
    return tuple(jnp.concatenate([part * mask for mask in masks], axis=0) for part in parts)


def lower_inverses(lowers):
    row = iota((SMALL, BLOCK), 0)
    lane = iota((SMALL, BLOCK), 1)
    column = lane % SMALL
    place = lane // SMALL
    eye = jnp.where(row == column, 1.0, 0.0)
    in_8 = row // 8 == column // 8
    in_16 = row // 16 == column // 16
    odd = place % 2 == 1
    masks = [
        jnp.where(place == index, 1.0, 0.0).astype(jnp.bfloat16) for index in range(BLOCK // SMALL)
    ]
    packed = []
    for lower in lowers:
        blocks = jnp.zeros((SMALL, BLOCK), jnp.float32)
        for index in range(BLOCK // SMALL):
            blocks = jnp.where(place == index, lower[index * SMALL : (index + 1) * SMALL], blocks)
        packed.append(blocks)
    nil = [jnp.where(in_8, blocks, 0.0) for blocks in packed]
    parts = [split(n) for n in nil]
    nil_2 = [split(dot_parts(n, spread_parts(n, masks))) for n in parts]
    start = [eye - n for n in nil]
    pairs = [
        dot_parts(stack_parts(n, split(s)), spread_parts(n, masks)) for n, s in zip(nil_2, start)
    ]
    start = [s + pair[SMALL:] for s, pair in zip(start, pairs)]
    nil_4 = [spread_parts(split(pair[:SMALL]), masks) for pair in pairs]
    inv = [s + dot_parts(split(s), n) for s, n in zip(start, nil_4)]
    step_16 = [
        spread_parts(split(jnp.where(in_16 & ~in_8, blocks, 0.0)), masks) for blocks in packed
    ]
    half = [jnp.concatenate([d[8:16], d[24:32]], axis=0) for d in inv]
    half = [dot_parts(split(h), w) for h, w in zip(half, step_16)]
    half = [dot_parts(split(h), spread_parts(split(d), masks)) for h, d in zip(half, inv)]
    inv = [
        jnp.concatenate([d[:8], d[8:16] - h[:8], d[16:24], d[24:] - h[8:]], axis=0)
        for d, h in zip(inv, half)
    ]
    step_32 = [spread_parts(split(jnp.where(in_16, 0.0, blocks)), masks) for blocks in packed]
    half = [dot_parts(split(d[16:]), w) for d, w in zip(inv, step_32)]
    half = [dot_parts(split(h), spread_parts(split(d), masks)) for h, d in zip(half, inv)]
    inv = [jnp.concatenate([d[:16], d[16:] - h], axis=0) for d, h in zip(inv, half)]
    wide = [spread_parts(split(d), masks) for d in inv]
    low = [jnp.where(odd, d, 0.0) for d in inv]
    zeros = jnp.zeros((SMALL, BLOCK), jnp.bfloat16)
    step_64 = []
    for lower in lowers:
        below = jnp.where(place == 0, lower[32:64], jnp.where(place == 2, lower[96:128], 0.0))
        step_64.append(
            tuple(
                jnp.concatenate([zeros, part * masks[0], zeros, part * masks[2]], axis=0)
                for part in split(below)
            )
        )
    half = [dot_parts(split(l), w) for l, w in zip(low, step_64)]
    half = [dot_parts(split(h), w) for h, w in zip(half, wide)]
    inv = [
        jnp.concatenate([jnp.where(odd, 0.0, d), l - h], axis=0) for d, l, h in zip(inv, low, half)
    ]
    left = iota((64, BLOCK), 1) < 64
    low = [jnp.where(left, 0.0, d) for d in inv]
    wide = [jnp.concatenate([jnp.where(left, d, 0.0), l], axis=0) for d, l in zip(inv, low)]
    wide_parts = [split(w) for w in wide]
    zeros = jnp.zeros((64, BLOCK), jnp.bfloat16)
    step_128 = [
        tuple(
            jnp.concatenate([zeros, part], axis=0) for part in split(jnp.where(left, lower[64:], 0.0))
        )
        for lower in lowers
    ]
    half = [dot_parts(tuple(part[64:] for part in l), w) for l, w in zip(wide_parts, step_128)]
    half = [dot_parts(split(h), w) for h, w in zip(half, wide_parts)]
    return [
        tuple(
            jnp.concatenate([high, low], axis=0)
            for high, low in zip((part[:64] for part in parts), split(w[64:] - h))
        )
        for parts, w, h in zip(wide_parts, wide, half)
    ]


def block(index):
    return slice(index * BLOCK, (index + 1) * BLOCK)


def fetch(pairs, sems):
    copies = [pltpu.make_async_copy(src, dst, sems.at[i]) for i, (src, dst) in enumerate(pairs)]
    for copy in copies:
        copy.start()
    return copies


def partner(place, swap):
    return lax.axis_index("ctx") ^ (0, *SWAP_ORDER)[place] if swap else place


def summary_kernel(decay_hbm, strength_hbm, k_hbm, v_hbm, factor_hbm, *rest, swap):
    *summaries, decay_ref, strength_ref, k_ref, v_ref, sems, factor_ref, summary_ref, out_sems = rest
    copies = fetch(
        [(decay_hbm, decay_ref), (strength_hbm, strength_ref), (k_hbm, k_ref), (v_hbm, v_ref)], sems
    )
    for copy in copies[:3]:
        copy.wait()
    tokens = k_ref.shape[0]
    key_heads = k_ref.shape[1] // DK
    value_heads = v_ref.shape[1] // DV
    repeat = value_heads // key_heads
    blocks = tokens // BLOCK
    rows, columns = cumulative_logs(decay_ref[...])
    strengths = strength_ref[...].T
    strict = iota((BLOCK, BLOCK), 0) > iota((BLOCK, BLOCK), 1)
    eye = jnp.where(iota((BLOCK, DK + DV), 0) == iota((BLOCK, DK + DV), 1), 1.0, 0.0)
    leaving = []
    for first in range(0, value_heads, HEADS_AT_ONCE):
        heads = range(first, min(first + HEADS_AT_ONCE, value_heads))
        keys = {}
        gram = {}
        for key_head in sorted({head // repeat for head in heads}):
            unit_rows = unit(k_ref[:, key_head * DK : (key_head + 1) * DK])
            keys[key_head] = [unit_rows[block(p)] for p in range(blocks)]
            gram[key_head] = {
                (p, r): dot_transposed(keys[key_head][p], keys[key_head][r])
                for p in range(blocks)
                for r in range(p + 1)
            }
        lower = {}
        for head in heads:
            for p in range(blocks):
                at = columns[block(p), head : head + 1]
                weight = strengths[block(p), head : head + 1]
                for r in range(p + 1):
                    spread = at - rows[head : head + 1, block(r)]
                    if p == r:
                        damp = jnp.where(strict, jnp.exp(jnp.where(strict, spread, 0.0)), 0.0)
                    else:
                        damp = jnp.exp(spread)
                    lower[head, p, r] = weight * gram[head // repeat][p, r] * damp
        inverse = lower_inverses([lower[head, p, p] for head in heads for p in range(blocks)])
        inverse = {
            (head, p): inverse[i * blocks + p] for i, head in enumerate(heads) for p in range(blocks)
        }
        if first == 0:
            copies[3].wait()
        factors = {}
        for p in range(blocks):
            for head in heads:
                at = columns[block(p), head : head + 1]
                weight = strengths[block(p), head : head + 1]
                right = jnp.concatenate(
                    [
                        keys[head // repeat][p] * (-weight * jnp.exp(at)),
                        v_ref[block(p), head * DV : (head + 1) * DV] * weight,
                    ],
                    axis=1,
                )
                for r in range(p):
                    right = right - dot_parts(split(lower[head, p, r]), split(factors[head, r]))
                factors[head, p] = dot_parts(inverse[head, p], split(right))
                factor_ref[head, block(p), :] = factors[head, p]
        flipped = {key_head: [split(k.T) for k in keys[key_head]] for key_head in keys}
        for head in heads:
            last = rows[head : head + 1, tokens - 1 : tokens]
            total = jnp.exp(last) * eye
            for p in range(blocks):
                ending = jnp.exp(last - columns[block(p), head : head + 1])
                total = total + dot_parts(flipped[head // repeat][p], split(factors[head, p] * ending))
            summary_ref[head] = total
        group = pl.ds(first, len(heads))
        leaving.append(
            pltpu.make_async_copy(
                factor_ref.at[group], factor_hbm.at[group], out_sems.at[len(leaving)]
            )
        )
        leaving[-1].start()
    if swap:
        target = factor_hbm.at[value_heads, pl.ds(0, DK)]
        leaving.append(
            pltpu.make_async_copy(summary_ref.at[partner(0, swap)], target, out_sems.at[len(leaving)])
        )
        leaving[-1].start()
    for place, out_ref in enumerate(summaries):
        out_ref[...] = summary_ref[partner(place + 1 if swap else place, swap)]
    for copy in leaving:
        copy.wait()


def output_kernel(
    decay_hbm,
    q_hbm,
    k_hbm,
    factor_hbm,
    map_hbm,
    decay_ref,
    q_ref,
    k_ref,
    factor_ref,
    sems,
    map_ref,
    out_sems,
):
    repeat = factor_ref.shape[0] // (k_hbm.shape[1] // DK)
    groups = [pl.ds(head, repeat) for head in range(0, factor_ref.shape[0], repeat)]
    copies = fetch(
        [(decay_hbm, decay_ref), (q_hbm, q_ref), (k_hbm, k_ref)]
        + [(factor_hbm.at[group], factor_ref.at[group]) for group in groups],
        sems,
    )
    leaving = []
    for copy in copies[:3]:
        copy.wait()
    tokens = q_ref.shape[0]
    key_heads = q_ref.shape[1] // DK
    value_heads = factor_ref.shape[0]
    repeat = value_heads // key_heads
    blocks = tokens // BLOCK
    rows, columns = cumulative_logs(decay_ref[...])
    inclusive = iota((BLOCK, BLOCK), 0) >= iota((BLOCK, BLOCK), 1)
    for key_head in range(key_heads):
        lanes = slice(key_head * DK, (key_head + 1) * DK)
        queries = unit(q_ref[:, lanes]) * DK**-0.5
        keys = unit(k_ref[:, lanes])
        for p in range(blocks):
            scores = [dot_transposed(queries[block(p)], keys[block(r)]) for r in range(p + 1)]
            if p == 0:
                copies[3 + key_head].wait()
            for head in range(key_head * repeat, (key_head + 1) * repeat):
                at = columns[block(p), head : head + 1]
                total = jnp.concatenate(
                    [queries[block(p)] * jnp.exp(at), jnp.zeros((BLOCK, DV), jnp.float32)], axis=1
                )
                for r in range(p + 1):
                    spread = at - rows[head : head + 1, block(r)]
                    if p == r:
                        damp = jnp.where(inclusive, jnp.exp(jnp.where(inclusive, spread, 0.0)), 0.0)
                    else:
                        damp = jnp.exp(spread)
                    total = total + dot(scores[r] * damp, factor_ref[head, block(r), :])
                map_ref[head, block(p), :] = total
        group = groups[key_head]
        leaving.append(
            pltpu.make_async_copy(map_ref.at[group], map_hbm.at[group], out_sems.at[key_head])
        )
        leaving[-1].start()
    for copy in leaving:
        copy.wait()


def scan_kernel(held_ref, entry_ref):
    count, held, key_width, width = entry_ref.shape
    for head in range(held):
        state = jnp.zeros((key_width, width), jnp.float32)
        entry_ref[0, head] = state
        for source in range(count - 1):
            added = held_ref[source, head, :, key_width:]
            if source:
                added = added + dot(held_ref[source, head, :, :key_width], state)
            state = added
            entry_ref[source + 1, head] = state


def ordered_scan_kernel(factor_hbm, *rest):
    *arrays, held_ref, entry_ref, sems = rest
    count = entry_ref.shape[0]
    held, entries = arrays[: count - 1], arrays[count - 1 :]
    here = partner(0, True)
    own_summary = factor_hbm.at[factor_hbm.shape[0] - 1, pl.ds(0, DK)]
    own = pltpu.make_async_copy(own_summary, held_ref.at[here], sems.at[0])
    own.start()
    for i, summary in enumerate(held):
        held_ref[partner(i + 1, True)] = summary[...]
    own.wait()
    state = jnp.zeros(entry_ref.shape[1:], jnp.float32)
    entry_ref[0] = state
    for source in range(count - 1):
        added = held_ref[source, :, DK:]
        if source:
            added = added + dot(held_ref[source, :, :DK], state)
        state = added
        entry_ref[source + 1] = state
    for i, entry in enumerate(entries):
        entry[...] = entry_ref[partner(i, True)]


def projection_kernel(map_hbm, gate_hbm, gain_ref, weight_ref, *rest, pieces, split_here, swap):
    if split_here:
        *rest, whole_ref, weight_sems = rest
        parts_ref = rest.pop(-8)
    else:
        parts_ref = weight_ref
    *arrays, map_ref, gate_ref, state_ref, high_ref, low_ref, gate_sems, map_sems = rest
    outs = arrays[-len(pieces) :]
    states = arrays[: -len(pieces)]
    heads = state_ref.shape[0]
    rows = outs[0].shape[0]
    blocks = sorted({index for index, _ in pieces})
    places = []
    for i, index in enumerate(blocks):
        start = (lax.axis_index("tp") ^ index) * rows if swap.rows else index * rows
        places.append((pl.ds(pl.multiple_of(start, rows), rows), pl.ds(i * rows, rows)))
    gates = fetch([(gate_hbm.at[s, :], gate_ref.at[t, :]) for s, t in places], gate_sems)
    maps = fetch(
        [
            (map_hbm.at[head, s, :], map_ref.at[head, t, :])
            for head in range(heads)
            for s, t in places
        ],
        map_sems,
    )
    if split_here:
        bands = [pl.ds(row, WEIGHT_ROWS) for row in range(0, weight_ref.shape[0], WEIGHT_ROWS)]
        weights = fetch(
            [(weight_ref.at[band, :], whole_ref.at[band, :]) for band in bands], weight_sems
        )
    for i, state in enumerate(states):
        state_ref[partner(i, swap.heads)] = state[...]
    for copy in gates:
        copy.wait()
    gain = gain_ref[...]
    for head in range(heads):
        lanes = slice(head * DV, (head + 1) * DV)
        gate = gate_ref[:, lanes]
        factor = gate / (1.0 + jnp.exp(-gate)) * gain
        for copy in maps[head * len(blocks) : (head + 1) * len(blocks)]:
            copy.wait()
        core = map_ref[head, :, DK:] + dot(map_ref[head, :, :DK], state_ref[head])
        scale = lax.rsqrt(jnp.mean(core * core, axis=-1, keepdims=True) + EPS)
        high_ref[:, lanes], low_ref[:, lanes] = split(core * scale * factor)
    total = len(blocks) * rows
    depth, columns = parts_ref.shape[1:]
    step = WEIGHT_ROWS if split_here else depth
    for index, row in enumerate(range(0, depth, step)):
        band = slice(row, row + step)
        if split_here:
            weights[index].wait()
            parts_ref[0, band, :], parts_ref[1, band, :] = split(whole_ref[band, :])
        for column in range(0, columns, BAND):
            lanes = slice(column, column + BAND)
            both = jnp.concatenate([high_ref[:, band], low_ref[:, band]], axis=0)
            sums = jnp.dot(both, parts_ref[0, band, lanes], preferred_element_type=jnp.float32)
            last = jnp.dot(
                high_ref[:, band], parts_ref[1, band, lanes], preferred_element_type=jnp.float32
            )
            result = sums[:total] + (sums[total:] + last)
            for (piece, start), out_ref in zip(pieces, outs):
                if start <= column < start + out_ref.shape[1]:
                    at = blocks.index(piece) * rows
                    target = slice(column - start, column - start + BAND)
                    part = result[at : at + rows]
                    out_ref[:, target] = part if index == 0 else out_ref[:, target] + part


def forward_kernel(across_ref, end_ref, going_ref):
    going_ref[...] = across_ref[...] + end_ref[...]


def hand_on_kernel(_, __, ___):
    pass


def shape(*dims):
    return jax.ShapeDtypeStruct(dims, jnp.float32)


def params(mebibytes):
    return pltpu.CompilerParams(vmem_limit_bytes=int(mebibytes * 1024 * 1024))


def cost(flops, *arrays):
    return pl.CostEstimate(
        flops=flops, bytes_accessed=4 * sum(a.size for a in arrays), transcendentals=0
    )


def partners_swap(arrays, axis):
    count = len(arrays)
    return [arrays[0]] + [
        lax.ppermute(array, axis, [(d, d ^ i) for d in range(count)])
        for array, i in zip(arrays[1:], SWAP_ORDER)
    ]


class Swap(typing.NamedTuple):
    heads: bool
    rows: bool


def swap_is_possible(heads, count):
    return heads == count == 1 + len(SWAP_ORDER)


def entering_states(factors, summaries, swap, beside, after):
    heads = factors.shape[0] - 1
    count = lax.axis_size("ctx")
    if swap:
        held = partners_swap([factors, *summaries], "ctx")
        held, beside = lax.optimization_barrier((held, beside))
        entry = shape(DK, DV)
        entries = pl.pallas_call(
            ordered_scan_kernel,
            in_specs=[HBM] + [VMEM] * (count - 1),
            out_specs=[VMEM] * count,
            out_shape=[entry] * count,
            scratch_shapes=[
                pltpu.VMEM((count, DK, DK + DV), jnp.float32),
                pltpu.VMEM((count, DK, DV), jnp.float32),
                pltpu.SemaphoreType.DMA((1,)),
            ],
            compiler_params=params(SCAN_VMEM),
            name="state_scan",
        )(*held)
        entries, after = lax.optimization_barrier((entries, after))
        return partners_swap(entries, "ctx"), beside, after
    parts = max(1, count // heads)
    per_owner = max(1, heads // count)
    width = DV // parts
    groups = heads // per_owner
    summary = jnp.stack(summaries)
    maps = summary[:, :, :DK].reshape(groups, 1, per_owner, DK, DK)
    maps = jnp.broadcast_to(maps, (groups, parts, per_owner, DK, DK))
    adds = summary[:, :, DK:].reshape(groups, per_owner, DK, parts, width)
    payload = jnp.concatenate([maps, adds.transpose(0, 3, 1, 2, 4)], axis=-1)
    payload = payload.reshape(count, per_owner, DK, DK + width)
    held = lax.all_to_all(payload, "ctx", split_axis=0, concat_axis=0, tiled=True)
    entries = pl.pallas_call(
        scan_kernel,
        out_shape=shape(count, per_owner, DK, width),
        compiler_params=params(32),
        name="state_scan",
    )(held)
    back = lax.all_to_all(entries, "ctx", split_axis=0, concat_axis=0, tiled=True)
    back = back.reshape(groups, parts, per_owner, DK, width).transpose(0, 2, 3, 1, 4)
    back = back.reshape(heads, DK, DV)
    return [back[head] for head in range(heads)], beside, after


def project_and_sum(project, columns, axis):
    count = lax.axis_size(axis)
    if count != 4:
        *pieces, _ = project([(i, 0, columns) for i in range(count)], FIRST_VMEM)
        whole = jnp.concatenate(pieces, axis=0)
        return lax.psum_scatter(whole, axis, scatter_dimension=0, tiled=True)
    opposite, parts = project([(3, 0, columns)], FIRST_VMEM)
    from_end = lax.ppermute(opposite, axis, [(0, 1), (3, 2)])
    from_inner = lax.ppermute(opposite, axis, [(1, 2), (2, 1)])
    across, own, near = project([(i, 0, columns) for i in (2, 0, 1)], LATER_VMEM, parts)
    going = pl.pallas_call(
        forward_kernel,
        out_shape=shape(*own.shape),
        compiler_params=params(LATER_VMEM),
        name="forward",
    )(across, from_end)
    anywhere = pl.BlockSpec(memory_space=pl.ANY)
    near = pl.pallas_call(
        hand_on_kernel,
        in_specs=[anywhere] * 2,
        out_specs=anywhere,
        out_shape=shape(*near.shape),
        input_output_aliases={0: 0},
        compiler_params=params(LATER_VMEM),
        name="hand_on",
    )(near, going)
    from_near = lax.ppermute(near, axis, [(i, i ^ 1) for i in range(4)])
    from_across = lax.ppermute(going, axis, [(i, i ^ 2) for i in range(4)])
    return ((own + from_inner) + from_near) + from_across


def per_device(queries, key_vectors, values, decays, strengths, out_gate, norm_gain, out_weight):
    tokens = queries.shape[0]
    heads = values.shape[1] // DV
    key_heads = queries.shape[1] // DK
    depth, columns = out_weight.shape
    rows = tokens // lax.axis_size("tp")
    gain = norm_gain.reshape(1, DV)
    swap = Swap(
        heads=swap_is_possible(heads, lax.axis_size("ctx")), rows=lax.axis_size("tp") == 4
    )

    def buffers(*arrays):
        return [pltpu.VMEM(a.shape, a.dtype) for a in arrays] + [
            pltpu.SemaphoreType.DMA((len(arrays),))
        ]

    factor_shape = shape(heads, tokens, DK + DV)
    groups = pl.cdiv(heads, HEADS_AT_ONCE)
    sent = heads - 1 if swap.heads else heads
    factors, *summaries = pl.pallas_call(
        functools.partial(summary_kernel, swap=swap.heads),
        in_specs=[HBM] * 4,
        out_specs=[HBM] + [VMEM] * sent,
        out_shape=[shape(heads + 1, tokens, DK + DV)] + [shape(DK, DK + DV)] * sent,
        scratch_shapes=buffers(decays, strengths, key_vectors, values)
        + [pltpu.VMEM(factor_shape.shape, jnp.float32), pltpu.VMEM((heads, DK, DK + DV), jnp.float32)]
        + [pltpu.SemaphoreType.DMA((groups + 1,))],
        compiler_params=params(MOST_VMEM),
        name="state_summary",
    )(decays, strengths, key_vectors, values)
    maps = pl.pallas_call(
        output_kernel,
        in_specs=[HBM] * 4,
        out_specs=HBM,
        out_shape=shape(8 * heads, tokens, DK + DV),
        scratch_shapes=[pltpu.VMEM(a.shape, jnp.float32) for a in (decays, queries, key_vectors)]
        + [pltpu.VMEM(factor_shape.shape, jnp.float32), pltpu.SemaphoreType.DMA((3 + key_heads,))]
        + [pltpu.VMEM(factor_shape.shape, jnp.float32), pltpu.SemaphoreType.DMA((key_heads,))],
        compiler_params=params(MOST_VMEM),
        cost_estimate=cost(3 * 2 * heads * tokens * tokens * 384, factors, factors, queries),
        name="output_maps",
    )(decays, queries, key_vectors, factors)
    states, maps, weights = entering_states(factors, summaries, swap.heads, maps, out_weight)
    parts_shape = jax.ShapeDtypeStruct((2, depth, columns), jnp.bfloat16)

    fetched = [
        pltpu.VMEM(out_weight.shape, jnp.float32),
        pltpu.SemaphoreType.DMA((depth // WEIGHT_ROWS,)),
    ]

    def project(pieces, vmem, parts=None):
        total = len({piece[0] for piece in pieces}) * rows
        normed = pltpu.VMEM((total, depth), jnp.bfloat16)
        counts = (total // rows, heads * total // rows)
        return pl.pallas_call(
            functools.partial(
                projection_kernel,
                pieces=[(index, start) for index, start, _ in pieces],
                split_here=parts is None,
                swap=swap,
            ),
            in_specs=[HBM] * 2 + [VMEM, HBM if parts is None else VMEM] + [VMEM] * heads,
            out_shape=[shape(rows, width) for _, _, width in pieces]
            + [parts_shape] * (parts is None),
            scratch_shapes=[
                pltpu.VMEM((heads, total, DK + DV), jnp.float32),
                pltpu.VMEM((total, heads * DV), jnp.float32),
                pltpu.VMEM((heads, DK, DV), jnp.float32),
                normed,
                normed,
            ]
            + [pltpu.SemaphoreType.DMA((n,)) for n in counts]
            + fetched * (parts is None),
            compiler_params=params(vmem),
            cost_estimate=cost(3 * 2 * total * depth * columns, out_weight),
            name="projection",
        )(maps, out_gate, gain, weights if parts is None else parts, *states)

    return project_and_sum(project, columns, "tp")


def solution(mesh):
    return jax.shard_map(
        per_device,
        mesh=mesh,
        in_specs=(
            P("ctx", "tp"),
            P("ctx", "tp"),
            P("ctx", "tp"),
            P("tp", "ctx"),
            P("tp", "ctx"),
            P("ctx", "tp"),
            P(),
            P("tp", None),
        ),
        out_specs=P(("ctx", "tp"), None),
        check_vma=False,
    )
```

```python
import functools
import typing

import jax
import jax.numpy as jnp
from jax import lax
from jax.experimental import pallas as pl
from jax.experimental.pallas import tpu as pltpu
from jax.sharding import PartitionSpec as P

DK = 128
DV = 128
BLOCK = 128
SMALL = 32
BAND = 256
SWAP_ORDER = (1, 2, 7, 6, 5, 4, 3)
WEIGHT_ROWS = 256
MOST_VMEM = 56
MAP_VMEM = 56
SCAN_VMEM = 52.25
FIRST_VMEM = 40
LATER_VMEM = 32
HEADS_AT_ONCE = 8
EPS = 1e-06


HBM = pl.BlockSpec(memory_space=pltpu.HBM)
VMEM = pl.BlockSpec(memory_space=pltpu.VMEM)


def dot(left, right):
    return jnp.dot(left, right, precision=lax.Precision.HIGH, preferred_element_type=jnp.float32)


def dot_transposed(left, right):
    return lax.dot_general(
        left,
        right,
        (((1,), (1,)), ((), ())),
        precision=lax.Precision.HIGH,
        preferred_element_type=jnp.float32,
    )


def iota(shape, dim):
    return lax.broadcasted_iota(jnp.int32, shape, dim)


def unit(rows):
    return rows * lax.rsqrt(jnp.sum(rows * rows, axis=-1, keepdims=True) + EPS)


def cumulative_logs(decays):
    tokens = decays.shape[1]
    upto = jnp.where(iota((tokens, tokens), 0) <= iota((tokens, tokens), 1), 1.0, 0.0)
    rows = jnp.dot(
        jnp.log(decays), upto, precision=lax.Precision.HIGHEST, preferred_element_type=jnp.float32
    )
    return rows, rows.T


def split(value):
    high = value.astype(jnp.bfloat16)
    return high, (value - high.astype(jnp.float32)).astype(jnp.bfloat16)


def dot_parts(left, right):
    rows = left[0].shape[0]
    both = jnp.concatenate(left, axis=0)
    sums = jnp.dot(both, right[0], preferred_element_type=jnp.float32)
    rest = jnp.dot(left[0], right[1], preferred_element_type=jnp.float32)
    return sums[:rows] + (sums[rows:] + rest)


def dot_parts_transposed(left, right):
    rows = left[0].shape[0]
    dims = (((1,), (1,)), ((), ()))
    both = jnp.concatenate(left, axis=0)
    sums = lax.dot_general(both, right[0], dims, preferred_element_type=jnp.float32)
    rest = lax.dot_general(left[0], right[1], dims, preferred_element_type=jnp.float32)
    return sums[:rows] + (sums[rows:] + rest)


def stack_parts(*values):
    return tuple(jnp.concatenate(pieces, axis=0) for pieces in zip(*values))


def spread_parts(parts, masks):
    return tuple(jnp.concatenate([part * mask for mask in masks], axis=0) for part in parts)


def lower_inverses(lowers):
    row = iota((SMALL, BLOCK), 0)
    lane = iota((SMALL, BLOCK), 1)
    column = lane % SMALL
    place = lane // SMALL
    eye = jnp.where(row == column, 1.0, 0.0)
    in_8 = row // 8 == column // 8
    in_16 = row // 16 == column // 16
    odd = place % 2 == 1
    masks = [
        jnp.where(place == index, 1.0, 0.0).astype(jnp.bfloat16) for index in range(BLOCK // SMALL)
    ]
    packed = []
    for lower in lowers:
        blocks = jnp.zeros((SMALL, BLOCK), jnp.float32)
        for index in range(BLOCK // SMALL):
            blocks = jnp.where(place == index, lower[index * SMALL : (index + 1) * SMALL], blocks)
        packed.append(blocks)
    nil = [jnp.where(in_8, blocks, 0.0) for blocks in packed]
    parts = [split(n) for n in nil]
    nil_2 = [split(dot_parts(n, spread_parts(n, masks))) for n in parts]
    start = [eye - n for n in nil]
    pairs = [
        dot_parts(stack_parts(n, split(s)), spread_parts(n, masks)) for n, s in zip(nil_2, start)
    ]
    start = [s + pair[SMALL:] for s, pair in zip(start, pairs)]
    nil_4 = [spread_parts(split(pair[:SMALL]), masks) for pair in pairs]
    inv = [s + dot_parts(split(s), n) for s, n in zip(start, nil_4)]
    step_16 = [
        spread_parts(split(jnp.where(in_16 & ~in_8, blocks, 0.0)), masks) for blocks in packed
    ]
    half = [jnp.concatenate([d[8:16], d[24:32]], axis=0) for d in inv]
    half = [dot_parts(split(h), w) for h, w in zip(half, step_16)]
    half = [dot_parts(split(h), spread_parts(split(d), masks)) for h, d in zip(half, inv)]
    inv = [
        jnp.concatenate([d[:8], d[8:16] - h[:8], d[16:24], d[24:] - h[8:]], axis=0)
        for d, h in zip(inv, half)
    ]
    step_32 = [spread_parts(split(jnp.where(in_16, 0.0, blocks)), masks) for blocks in packed]
    half = [dot_parts(split(d[16:]), w) for d, w in zip(inv, step_32)]
    half = [dot_parts(split(h), spread_parts(split(d), masks)) for h, d in zip(half, inv)]
    inv = [jnp.concatenate([d[:16], d[16:] - h], axis=0) for d, h in zip(inv, half)]
    wide = [spread_parts(split(d), masks) for d in inv]
    low = [jnp.where(odd, d, 0.0) for d in inv]
    zeros = jnp.zeros((SMALL, BLOCK), jnp.bfloat16)
    step_64 = []
    for lower in lowers:
        below = jnp.where(place == 0, lower[32:64], jnp.where(place == 2, lower[96:128], 0.0))
        step_64.append(
            tuple(
                jnp.concatenate([zeros, part * masks[0], zeros, part * masks[2]], axis=0)
                for part in split(below)
            )
        )
    half = [dot_parts(split(l), w) for l, w in zip(low, step_64)]
    half = [dot_parts(split(h), w) for h, w in zip(half, wide)]
    inv = [
        jnp.concatenate([jnp.where(odd, 0.0, d), l - h], axis=0) for d, l, h in zip(inv, low, half)
    ]
    left = iota((64, BLOCK), 1) < 64
    low = [jnp.where(left, 0.0, d) for d in inv]
    wide = [jnp.concatenate([jnp.where(left, d, 0.0), l], axis=0) for d, l in zip(inv, low)]
    wide_parts = [split(w) for w in wide]
    zeros = jnp.zeros((64, BLOCK), jnp.bfloat16)
    step_128 = [
        tuple(
            jnp.concatenate([zeros, part], axis=0) for part in split(jnp.where(left, lower[64:], 0.0))
        )
        for lower in lowers
    ]
    half = [dot_parts(tuple(part[64:] for part in l), w) for l, w in zip(wide_parts, step_128)]
    half = [dot_parts(split(h), w) for h, w in zip(half, wide_parts)]
    return [
        tuple(
            jnp.concatenate([high, low], axis=0)
            for high, low in zip((part[:64] for part in parts), split(w[64:] - h))
        )
        for parts, w, h in zip(wide_parts, wide, half)
    ]


def block(index):
    return slice(index * BLOCK, (index + 1) * BLOCK)


def fetch(pairs, sems):
    copies = [pltpu.make_async_copy(src, dst, sems.at[i]) for i, (src, dst) in enumerate(pairs)]
    for copy in copies:
        copy.start()
    return copies


def partner(place, swap):
    return lax.axis_index("ctx") ^ (0, *SWAP_ORDER)[place] if swap else place


def summary_kernel(decay_hbm, strength_hbm, k_hbm, v_hbm, factor_hbm, *rest, swap):
    *summaries, decay_ref, strength_ref, k_ref, v_ref, sems, factor_ref, summary_ref, out_sems = rest
    copies = fetch(
        [(decay_hbm, decay_ref), (strength_hbm, strength_ref), (k_hbm, k_ref), (v_hbm, v_ref)], sems
    )
    for copy in copies[:3]:
        copy.wait()
    tokens = k_ref.shape[0]
    key_heads = k_ref.shape[1] // DK
    value_heads = v_ref.shape[1] // DV
    repeat = value_heads // key_heads
    blocks = tokens // BLOCK
    rows, columns = cumulative_logs(decay_ref[...])
    strengths = strength_ref[...].T
    strict = iota((BLOCK, BLOCK), 0) > iota((BLOCK, BLOCK), 1)
    eye = jnp.where(iota((BLOCK, DK + DV), 0) == iota((BLOCK, DK + DV), 1), 1.0, 0.0)
    leaving = []
    for first in range(0, value_heads, HEADS_AT_ONCE):
        heads = range(first, min(first + HEADS_AT_ONCE, value_heads))
        keys = {}
        gram = {}
        for key_head in sorted({head // repeat for head in heads}):
            unit_rows = unit(k_ref[:, key_head * DK : (key_head + 1) * DK])
            keys[key_head] = [unit_rows[block(p)] for p in range(blocks)]
            gram[key_head] = {
                (p, r): dot_transposed(keys[key_head][p], keys[key_head][r])
                for p in range(blocks)
                for r in range(p + 1)
            }
        lower = {}
        for head in heads:
            for p in range(blocks):
                at = columns[block(p), head : head + 1]
                weight = strengths[block(p), head : head + 1]
                for r in range(p + 1):
                    spread = at - rows[head : head + 1, block(r)]
                    if p == r:
                        damp = jnp.where(strict, jnp.exp(jnp.where(strict, spread, 0.0)), 0.0)
                    else:
                        damp = jnp.exp(spread)
                    lower[head, p, r] = weight * gram[head // repeat][p, r] * damp
        inverse = lower_inverses([lower[head, p, p] for head in heads for p in range(blocks)])
        inverse = {
            (head, p): inverse[i * blocks + p] for i, head in enumerate(heads) for p in range(blocks)
        }
        if first == 0:
            copies[3].wait()
        factors = {}
        for p in range(blocks):
            for head in heads:
                at = columns[block(p), head : head + 1]
                weight = strengths[block(p), head : head + 1]
                right = jnp.concatenate(
                    [
                        keys[head // repeat][p] * (-weight * jnp.exp(at)),
                        v_ref[block(p), head * DV : (head + 1) * DV] * weight,
                    ],
                    axis=1,
                )
                for r in range(p):
                    right = right - dot_parts(split(lower[head, p, r]), split(factors[head, r]))
                factors[head, p] = dot_parts(inverse[head, p], split(right))
                factor_ref[head, block(p), :] = factors[head, p]
        flipped = {key_head: [split(k.T) for k in keys[key_head]] for key_head in keys}
        for head in heads:
            last = rows[head : head + 1, tokens - 1 : tokens]
            total = jnp.exp(last) * eye
            for p in range(blocks):
                ending = jnp.exp(last - columns[block(p), head : head + 1])
                total = total + dot_parts(flipped[head // repeat][p], split(factors[head, p] * ending))
            summary_ref[head] = total
        group = pl.ds(first, len(heads))
        leaving.append(
            pltpu.make_async_copy(
                factor_ref.at[group], factor_hbm.at[group], out_sems.at[len(leaving)]
            )
        )
        leaving[-1].start()
    if swap:
        target = factor_hbm.at[value_heads, pl.ds(0, DK)]
        leaving.append(
            pltpu.make_async_copy(summary_ref.at[partner(0, swap)], target, out_sems.at[len(leaving)])
        )
        leaving[-1].start()
    for place, out_ref in enumerate(summaries):
        out_ref[...] = summary_ref[partner(place + 1 if swap else place, swap)]
    for copy in leaving:
        copy.wait()


def output_kernel(
    decay_hbm,
    q_hbm,
    k_hbm,
    factor_hbm,
    map_hbm,
    decay_ref,
    q_ref,
    k_ref,
    factor_ref,
    sems,
    map_ref,
    out_sems,
):
    repeat = factor_ref.shape[0] // (k_hbm.shape[1] // DK)
    groups = [pl.ds(head, repeat) for head in range(0, factor_ref.shape[0], repeat)]
    copies = fetch(
        [(decay_hbm, decay_ref), (q_hbm, q_ref), (k_hbm, k_ref)]
        + [(factor_hbm.at[group], factor_ref.at[group]) for group in groups],
        sems,
    )
    leaving = []
    for copy in copies[:3]:
        copy.wait()
    tokens = q_ref.shape[0]
    key_heads = q_ref.shape[1] // DK
    value_heads = factor_ref.shape[0]
    repeat = value_heads // key_heads
    blocks = tokens // BLOCK
    rows, columns = cumulative_logs(decay_ref[...])
    inclusive = iota((BLOCK, BLOCK), 0) >= iota((BLOCK, BLOCK), 1)
    for key_head in range(key_heads):
        lanes = slice(key_head * DK, (key_head + 1) * DK)
        queries = unit(q_ref[:, lanes]) * DK**-0.5
        keys = split(unit(k_ref[:, lanes]))
        heads = range(key_head * repeat, (key_head + 1) * repeat)
        parts = {}
        for p in range(blocks):
            query_parts = split(queries[block(p)])
            scores = [
                dot_parts_transposed(query_parts, tuple(part[block(r)] for part in keys))
                for r in range(p + 1)
            ]
            if p == 0:
                copies[3 + key_head].wait()
            for head in heads:
                at = columns[block(p), head : head + 1]
                parts[head, p] = split(factor_ref[head, block(p), :])
                total = jnp.concatenate(
                    [queries[block(p)] * jnp.exp(at), jnp.zeros((BLOCK, DV), jnp.float32)], axis=1
                )
                for r in range(p + 1):
                    spread = at - rows[head : head + 1, block(r)]
                    if p == r:
                        damp = jnp.where(inclusive, jnp.exp(jnp.where(inclusive, spread, 0.0)), 0.0)
                    else:
                        damp = jnp.exp(spread)
                    total = total + dot_parts(split(scores[r] * damp), parts[head, r])
                map_ref[head, block(p), :] = total
        group = groups[key_head]
        leaving.append(
            pltpu.make_async_copy(map_ref.at[group], map_hbm.at[group], out_sems.at[key_head])
        )
        leaving[-1].start()
    for copy in leaving:
        copy.wait()


def scan_kernel(held_ref, entry_ref):
    count, held, key_width, width = entry_ref.shape
    for head in range(held):
        state = jnp.zeros((key_width, width), jnp.float32)
        entry_ref[0, head] = state
        for source in range(count - 1):
            added = held_ref[source, head, :, key_width:]
            if source:
                added = added + dot(held_ref[source, head, :, :key_width], state)
            state = added
            entry_ref[source + 1, head] = state


def ordered_scan_kernel(factor_hbm, *rest):
    *arrays, held_ref, entry_ref, sems = rest
    count = entry_ref.shape[0]
    held, entries = arrays[: count - 1], arrays[count - 1 :]
    here = partner(0, True)
    own_summary = factor_hbm.at[factor_hbm.shape[0] - 1, pl.ds(0, DK)]
    own = pltpu.make_async_copy(own_summary, held_ref.at[here], sems.at[0])
    own.start()
    for i, summary in enumerate(held):
        held_ref[partner(i + 1, True)] = summary[...]
    own.wait()
    state = jnp.zeros(entry_ref.shape[1:], jnp.float32)
    entry_ref[0] = state
    for source in range(count - 1):
        added = held_ref[source, :, DK:]
        if source:
            added = added + dot(held_ref[source, :, :DK], state)
        state = added
        entry_ref[source + 1] = state
    for i, entry in enumerate(entries):
        entry[...] = entry_ref[partner(i, True)]


def projection_kernel(map_hbm, gate_hbm, gain_ref, weight_ref, *rest, pieces, split_here, swap):
    if split_here:
        *rest, whole_ref, weight_sems = rest
        parts_ref = rest.pop(-8)
    else:
        parts_ref = weight_ref
    *arrays, map_ref, gate_ref, state_ref, high_ref, low_ref, gate_sems, map_sems = rest
    outs = arrays[-len(pieces) :]
    states = arrays[: -len(pieces)]
    heads = state_ref.shape[0]
    rows = outs[0].shape[0]
    blocks = sorted({index for index, _ in pieces})
    places = []
    for i, index in enumerate(blocks):
        start = (lax.axis_index("tp") ^ index) * rows if swap.rows else index * rows
        places.append((pl.ds(pl.multiple_of(start, rows), rows), pl.ds(i * rows, rows)))
    gates = fetch([(gate_hbm.at[s, :], gate_ref.at[t, :]) for s, t in places], gate_sems)
    maps = fetch(
        [
            (map_hbm.at[head, s, :], map_ref.at[head, t, :])
            for head in range(heads)
            for s, t in places
        ],
        map_sems,
    )
    if split_here:
        bands = [pl.ds(row, WEIGHT_ROWS) for row in range(0, weight_ref.shape[0], WEIGHT_ROWS)]
        weights = fetch(
            [(weight_ref.at[band, :], whole_ref.at[band, :]) for band in bands], weight_sems
        )
    for i, state in enumerate(states):
        state_ref[partner(i, swap.heads)] = state[...]
    for copy in gates:
        copy.wait()
    gain = gain_ref[...]
    for head in range(heads):
        lanes = slice(head * DV, (head + 1) * DV)
        gate = gate_ref[:, lanes]
        factor = gate / (1.0 + jnp.exp(-gate)) * gain
        for copy in maps[head * len(blocks) : (head + 1) * len(blocks)]:
            copy.wait()
        core = map_ref[head, :, DK:] + dot(map_ref[head, :, :DK], state_ref[head])
        scale = lax.rsqrt(jnp.mean(core * core, axis=-1, keepdims=True) + EPS)
        high_ref[:, lanes], low_ref[:, lanes] = split(core * scale * factor)
    total = len(blocks) * rows
    depth, columns = parts_ref.shape[1:]
    step = WEIGHT_ROWS if split_here else depth
    for index, row in enumerate(range(0, depth, step)):
        band = slice(row, row + step)
        if split_here:
            weights[index].wait()
            parts_ref[0, band, :], parts_ref[1, band, :] = split(whole_ref[band, :])
        for column in range(0, columns, BAND):
            lanes = slice(column, column + BAND)
            both = jnp.concatenate([high_ref[:, band], low_ref[:, band]], axis=0)
            sums = jnp.dot(both, parts_ref[0, band, lanes], preferred_element_type=jnp.float32)
            last = jnp.dot(
                high_ref[:, band], parts_ref[1, band, lanes], preferred_element_type=jnp.float32
            )
            result = sums[:total] + (sums[total:] + last)
            for (piece, start), out_ref in zip(pieces, outs):
                if start <= column < start + out_ref.shape[1]:
                    at = blocks.index(piece) * rows
                    target = slice(column - start, column - start + BAND)
                    part = result[at : at + rows]
                    out_ref[:, target] = part if index == 0 else out_ref[:, target] + part


def forward_kernel(across_ref, end_ref, going_ref):
    going_ref[...] = across_ref[...] + end_ref[...]


def hand_on_kernel(_, __, ___):
    pass


def shape(*dims):
    return jax.ShapeDtypeStruct(dims, jnp.float32)


def params(mebibytes):
    return pltpu.CompilerParams(vmem_limit_bytes=int(mebibytes * 1024 * 1024))


def cost(flops, *arrays):
    return pl.CostEstimate(
        flops=flops, bytes_accessed=4 * sum(a.size for a in arrays), transcendentals=0
    )


def partners_swap(arrays, axis):
    count = len(arrays)
    return [arrays[0]] + [
        lax.ppermute(array, axis, [(d, d ^ i) for d in range(count)])
        for array, i in zip(arrays[1:], SWAP_ORDER)
    ]


class Swap(typing.NamedTuple):
    heads: bool
    rows: bool


def swap_is_possible(heads, count):
    return heads == count == 1 + len(SWAP_ORDER)


def entering_states(factors, summaries, swap, beside, after):
    heads = factors.shape[0] - 1
    count = lax.axis_size("ctx")
    if swap:
        held = partners_swap([factors, *summaries], "ctx")
        held, beside = lax.optimization_barrier((held, beside))
        entry = shape(DK, DV)
        entries = pl.pallas_call(
            ordered_scan_kernel,
            in_specs=[HBM] + [VMEM] * (count - 1),
            out_specs=[VMEM] * count,
            out_shape=[entry] * count,
            scratch_shapes=[
                pltpu.VMEM((count, DK, DK + DV), jnp.float32),
                pltpu.VMEM((count, DK, DV), jnp.float32),
                pltpu.SemaphoreType.DMA((1,)),
            ],
            compiler_params=params(SCAN_VMEM),
            name="state_scan",
        )(*held)
        entries, after = lax.optimization_barrier((entries, after))
        return partners_swap(entries, "ctx"), beside, after
    parts = max(1, count // heads)
    per_owner = max(1, heads // count)
    width = DV // parts
    groups = heads // per_owner
    summary = jnp.stack(summaries)
    maps = summary[:, :, :DK].reshape(groups, 1, per_owner, DK, DK)
    maps = jnp.broadcast_to(maps, (groups, parts, per_owner, DK, DK))
    adds = summary[:, :, DK:].reshape(groups, per_owner, DK, parts, width)
    payload = jnp.concatenate([maps, adds.transpose(0, 3, 1, 2, 4)], axis=-1)
    payload = payload.reshape(count, per_owner, DK, DK + width)
    held = lax.all_to_all(payload, "ctx", split_axis=0, concat_axis=0, tiled=True)
    entries = pl.pallas_call(
        scan_kernel,
        out_shape=shape(count, per_owner, DK, width),
        compiler_params=params(32),
        name="state_scan",
    )(held)
    back = lax.all_to_all(entries, "ctx", split_axis=0, concat_axis=0, tiled=True)
    back = back.reshape(groups, parts, per_owner, DK, width).transpose(0, 2, 3, 1, 4)
    back = back.reshape(heads, DK, DV)
    return [back[head] for head in range(heads)], beside, after


def project_and_sum(project, columns, axis):
    count = lax.axis_size(axis)
    if count != 4:
        *pieces, _ = project([(i, 0, columns) for i in range(count)], FIRST_VMEM)
        whole = jnp.concatenate(pieces, axis=0)
        return lax.psum_scatter(whole, axis, scatter_dimension=0, tiled=True)
    opposite, parts = project([(3, 0, columns)], FIRST_VMEM)
    from_end = lax.ppermute(opposite, axis, [(0, 1), (3, 2)])
    from_inner = lax.ppermute(opposite, axis, [(1, 2), (2, 1)])
    across, own, near = project([(i, 0, columns) for i in (2, 0, 1)], LATER_VMEM, parts)
    going = pl.pallas_call(
        forward_kernel,
        out_shape=shape(*own.shape),
        compiler_params=params(LATER_VMEM),
        name="forward",
    )(across, from_end)
    anywhere = pl.BlockSpec(memory_space=pl.ANY)
    near = pl.pallas_call(
        hand_on_kernel,
        in_specs=[anywhere] * 2,
        out_specs=anywhere,
        out_shape=shape(*near.shape),
        input_output_aliases={0: 0},
        compiler_params=params(LATER_VMEM),
        name="hand_on",
    )(near, going)
    from_near = lax.ppermute(near, axis, [(i, i ^ 1) for i in range(4)])
    from_across = lax.ppermute(going, axis, [(i, i ^ 2) for i in range(4)])
    return ((own + from_inner) + from_near) + from_across


def per_device(queries, key_vectors, values, decays, strengths, out_gate, norm_gain, out_weight):
    tokens = queries.shape[0]
    heads = values.shape[1] // DV
    key_heads = queries.shape[1] // DK
    depth, columns = out_weight.shape
    rows = tokens // lax.axis_size("tp")
    gain = norm_gain.reshape(1, DV)
    swap = Swap(
        heads=swap_is_possible(heads, lax.axis_size("ctx")), rows=lax.axis_size("tp") == 4
    )

    def buffers(*arrays):
        return [pltpu.VMEM(a.shape, a.dtype) for a in arrays] + [
            pltpu.SemaphoreType.DMA((len(arrays),))
        ]

    factor_shape = shape(heads, tokens, DK + DV)
    groups = pl.cdiv(heads, HEADS_AT_ONCE)
    sent = heads - 1 if swap.heads else heads
    factors, *summaries = pl.pallas_call(
        functools.partial(summary_kernel, swap=swap.heads),
        in_specs=[HBM] * 4,
        out_specs=[HBM] + [VMEM] * sent,
        out_shape=[shape(heads + 1, tokens, DK + DV)] + [shape(DK, DK + DV)] * sent,
        scratch_shapes=buffers(decays, strengths, key_vectors, values)
        + [pltpu.VMEM(factor_shape.shape, jnp.float32), pltpu.VMEM((heads, DK, DK + DV), jnp.float32)]
        + [pltpu.SemaphoreType.DMA((groups + 1,))],
        compiler_params=params(MOST_VMEM),
        name="state_summary",
    )(decays, strengths, key_vectors, values)
    maps = pl.pallas_call(
        output_kernel,
        in_specs=[HBM] * 4,
        out_specs=HBM,
        out_shape=shape(8 * heads, tokens, DK + DV),
        scratch_shapes=[pltpu.VMEM(a.shape, jnp.float32) for a in (decays, queries, key_vectors)]
        + [pltpu.VMEM(factor_shape.shape, jnp.float32), pltpu.SemaphoreType.DMA((3 + key_heads,))]
        + [pltpu.VMEM(factor_shape.shape, jnp.float32), pltpu.SemaphoreType.DMA((key_heads,))],
        compiler_params=params(MAP_VMEM),
        cost_estimate=cost(3 * 2 * heads * tokens * tokens * 384, factors, factors, queries),
        name="output_maps",
    )(decays, queries, key_vectors, factors)
    states, maps, weights = entering_states(factors, summaries, swap.heads, maps, out_weight)
    parts_shape = jax.ShapeDtypeStruct((2, depth, columns), jnp.bfloat16)

    fetched = [
        pltpu.VMEM(out_weight.shape, jnp.float32),
        pltpu.SemaphoreType.DMA((depth // WEIGHT_ROWS,)),
    ]

    def project(pieces, vmem, parts=None):
        total = len({piece[0] for piece in pieces}) * rows
        normed = pltpu.VMEM((total, depth), jnp.bfloat16)
        counts = (total // rows, heads * total // rows)
        return pl.pallas_call(
            functools.partial(
                projection_kernel,
                pieces=[(index, start) for index, start, _ in pieces],
                split_here=parts is None,
                swap=swap,
            ),
            in_specs=[HBM] * 2 + [VMEM, HBM if parts is None else VMEM] + [VMEM] * heads,
            out_shape=[shape(rows, width) for _, _, width in pieces]
            + [parts_shape] * (parts is None),
            scratch_shapes=[
                pltpu.VMEM((heads, total, DK + DV), jnp.float32),
                pltpu.VMEM((total, heads * DV), jnp.float32),
                pltpu.VMEM((heads, DK, DV), jnp.float32),
                normed,
                normed,
            ]
            + [pltpu.SemaphoreType.DMA((n,)) for n in counts]
            + fetched * (parts is None),
            compiler_params=params(vmem),
            cost_estimate=cost(3 * 2 * total * depth * columns, out_weight),
            name="projection",
        )(maps, out_gate, gain, weights if parts is None else parts, *states)

    return project_and_sum(project, columns, "tp")


def solution(mesh):
    return jax.shard_map(
        per_device,
        mesh=mesh,
        in_specs=(
            P("ctx", "tp"),
            P("ctx", "tp"),
            P("ctx", "tp"),
            P("tp", "ctx"),
            P("tp", "ctx"),
            P("ctx", "tp"),
            P(),
            P("tp", None),
        ),
        out_specs=P(("ctx", "tp"), None),
        check_vma=False,
    )
```

```python
import functools
import typing

import jax
import jax.numpy as jnp
from jax import lax
from jax.experimental import pallas as pl
from jax.experimental.pallas import tpu as pltpu
from jax.sharding import PartitionSpec as P

DK = 128
DV = 128
BLOCK = 128
SMALL = 32
BAND = 256
SWAP_ORDER = (7, 6, 5, 4, 3, 2, 1)
WEIGHT_ROWS = 256
MOST_VMEM = 56
MAP_VMEM = 56
SCAN_VMEM = 52.25
FIRST_VMEM = 40
LATER_VMEM = 32
HEADS_AT_ONCE = 8
EPS = 1e-06


HBM = pl.BlockSpec(memory_space=pltpu.HBM)
VMEM = pl.BlockSpec(memory_space=pltpu.VMEM)


def dot(left, right):
    return jnp.dot(left, right, precision=lax.Precision.HIGH, preferred_element_type=jnp.float32)


def dot_transposed(left, right):
    return lax.dot_general(
        left,
        right,
        (((1,), (1,)), ((), ())),
        precision=lax.Precision.HIGH,
        preferred_element_type=jnp.float32,
    )


def iota(shape, dim):
    return lax.broadcasted_iota(jnp.int32, shape, dim)


def unit(rows):
    return rows * lax.rsqrt(jnp.sum(rows * rows, axis=-1, keepdims=True) + EPS)


def cumulative_logs(decays):
    tokens = decays.shape[1]
    upto = jnp.where(iota((tokens, tokens), 0) <= iota((tokens, tokens), 1), 1.0, 0.0)
    rows = jnp.dot(
        jnp.log(decays), upto, precision=lax.Precision.HIGHEST, preferred_element_type=jnp.float32
    )
    return rows, rows.T


def split(value):
    high = value.astype(jnp.bfloat16)
    return high, (value - high.astype(jnp.float32)).astype(jnp.bfloat16)


def dot_parts(left, right):
    rows = left[0].shape[0]
    both = jnp.concatenate(left, axis=0)
    sums = jnp.dot(both, right[0], preferred_element_type=jnp.float32)
    rest = jnp.dot(left[0], right[1], preferred_element_type=jnp.float32)
    return sums[:rows] + (sums[rows:] + rest)


def dot_parts_transposed(left, right):
    rows = left[0].shape[0]
    dims = (((1,), (1,)), ((), ()))
    both = jnp.concatenate(left, axis=0)
    sums = lax.dot_general(both, right[0], dims, preferred_element_type=jnp.float32)
    rest = lax.dot_general(left[0], right[1], dims, preferred_element_type=jnp.float32)
    return sums[:rows] + (sums[rows:] + rest)


def stack_parts(*values):
    return tuple(jnp.concatenate(pieces, axis=0) for pieces in zip(*values))


def spread_parts(parts, masks):
    return tuple(jnp.concatenate([part * mask for mask in masks], axis=0) for part in parts)


def lower_inverses(lowers):
    row = iota((SMALL, BLOCK), 0)
    lane = iota((SMALL, BLOCK), 1)
    column = lane % SMALL
    place = lane // SMALL
    eye = jnp.where(row == column, 1.0, 0.0)
    in_8 = row // 8 == column // 8
    in_16 = row // 16 == column // 16
    odd = place % 2 == 1
    masks = [
        jnp.where(place == index, 1.0, 0.0).astype(jnp.bfloat16) for index in range(BLOCK // SMALL)
    ]
    packed = []
    for lower in lowers:
        blocks = jnp.zeros((SMALL, BLOCK), jnp.float32)
        for index in range(BLOCK // SMALL):
            blocks = jnp.where(place == index, lower[index * SMALL : (index + 1) * SMALL], blocks)
        packed.append(blocks)
    nil = [jnp.where(in_8, blocks, 0.0) for blocks in packed]
    parts = [split(n) for n in nil]
    nil_2 = [split(dot_parts(n, spread_parts(n, masks))) for n in parts]
    start = [eye - n for n in nil]
    pairs = [
        dot_parts(stack_parts(n, split(s)), spread_parts(n, masks)) for n, s in zip(nil_2, start)
    ]
    start = [s + pair[SMALL:] for s, pair in zip(start, pairs)]
    nil_4 = [spread_parts(split(pair[:SMALL]), masks) for pair in pairs]
    inv = [s + dot_parts(split(s), n) for s, n in zip(start, nil_4)]
    step_16 = [
        spread_parts(split(jnp.where(in_16 & ~in_8, blocks, 0.0)), masks) for blocks in packed
    ]
    half = [jnp.concatenate([d[8:16], d[24:32]], axis=0) for d in inv]
    half = [dot_parts(split(h), w) for h, w in zip(half, step_16)]
    half = [dot_parts(split(h), spread_parts(split(d), masks)) for h, d in zip(half, inv)]
    inv = [
        jnp.concatenate([d[:8], d[8:16] - h[:8], d[16:24], d[24:] - h[8:]], axis=0)
        for d, h in zip(inv, half)
    ]
    step_32 = [spread_parts(split(jnp.where(in_16, 0.0, blocks)), masks) for blocks in packed]
    half = [dot_parts(split(d[16:]), w) for d, w in zip(inv, step_32)]
    half = [dot_parts(split(h), spread_parts(split(d), masks)) for h, d in zip(half, inv)]
    inv = [jnp.concatenate([d[:16], d[16:] - h], axis=0) for d, h in zip(inv, half)]
    wide = [spread_parts(split(d), masks) for d in inv]
    low = [jnp.where(odd, d, 0.0) for d in inv]
    zeros = jnp.zeros((SMALL, BLOCK), jnp.bfloat16)
    step_64 = []
    for lower in lowers:
        below = jnp.where(place == 0, lower[32:64], jnp.where(place == 2, lower[96:128], 0.0))
        step_64.append(
            tuple(
                jnp.concatenate([zeros, part * masks[0], zeros, part * masks[2]], axis=0)
                for part in split(below)
            )
        )
    half = [dot_parts(split(l), w) for l, w in zip(low, step_64)]
    half = [dot_parts(split(h), w) for h, w in zip(half, wide)]
    inv = [
        jnp.concatenate([jnp.where(odd, 0.0, d), l - h], axis=0) for d, l, h in zip(inv, low, half)
    ]
    left = iota((64, BLOCK), 1) < 64
    low = [jnp.where(left, 0.0, d) for d in inv]
    wide = [jnp.concatenate([jnp.where(left, d, 0.0), l], axis=0) for d, l in zip(inv, low)]
    wide_parts = [split(w) for w in wide]
    zeros = jnp.zeros((64, BLOCK), jnp.bfloat16)
    step_128 = [
        tuple(
            jnp.concatenate([zeros, part], axis=0) for part in split(jnp.where(left, lower[64:], 0.0))
        )
        for lower in lowers
    ]
    half = [dot_parts(tuple(part[64:] for part in l), w) for l, w in zip(wide_parts, step_128)]
    half = [dot_parts(split(h), w) for h, w in zip(half, wide_parts)]
    return [
        tuple(
            jnp.concatenate([high, low], axis=0)
            for high, low in zip((part[:64] for part in parts), split(w[64:] - h))
        )
        for parts, w, h in zip(wide_parts, wide, half)
    ]


def block(index):
    return slice(index * BLOCK, (index + 1) * BLOCK)


def fetch(pairs, sems):
    copies = [pltpu.make_async_copy(src, dst, sems.at[i]) for i, (src, dst) in enumerate(pairs)]
    for copy in copies:
        copy.start()
    return copies


def partner(place, swap):
    return lax.axis_index("ctx") ^ (0, *SWAP_ORDER)[place] if swap else place


def summary_kernel(decay_hbm, strength_hbm, k_hbm, v_hbm, factor_hbm, *rest, swap):
    *summaries, decay_ref, strength_ref, k_ref, v_ref, sems, factor_ref, summary_ref, out_sems = rest
    copies = fetch(
        [(decay_hbm, decay_ref), (strength_hbm, strength_ref), (k_hbm, k_ref), (v_hbm, v_ref)], sems
    )
    tokens = k_ref.shape[0]
    key_heads = k_ref.shape[1] // DK
    value_heads = v_ref.shape[1] // DV
    repeat = value_heads // key_heads
    blocks = tokens // BLOCK
    for copy in copies[:2]:
        copy.wait()
    rows, columns = cumulative_logs(decay_ref[...])
    strengths = strength_ref[...].T
    strict = iota((BLOCK, BLOCK), 0) > iota((BLOCK, BLOCK), 1)
    eye = jnp.where(iota((BLOCK, DK + DV), 0) == iota((BLOCK, DK + DV), 1), 1.0, 0.0)
    copies[2].wait()
    leaving = []
    for first in range(0, value_heads, HEADS_AT_ONCE):
        heads = range(first, min(first + HEADS_AT_ONCE, value_heads))
        keys = {}
        gram = {}
        for key_head in sorted({head // repeat for head in heads}):
            unit_rows = unit(k_ref[:, key_head * DK : (key_head + 1) * DK])
            keys[key_head] = [unit_rows[block(p)] for p in range(blocks)]
            gram[key_head] = {
                (p, r): dot_transposed(keys[key_head][p], keys[key_head][r])
                for p in range(blocks)
                for r in range(p + 1)
            }
        lower = {}
        for head in heads:
            for p in range(blocks):
                at = columns[block(p), head : head + 1]
                weight = strengths[block(p), head : head + 1]
                for r in range(p + 1):
                    spread = at - rows[head : head + 1, block(r)]
                    if p == r:
                        damp = jnp.where(strict, jnp.exp(jnp.where(strict, spread, 0.0)), 0.0)
                    else:
                        damp = jnp.exp(spread)
                    lower[head, p, r] = weight * gram[head // repeat][p, r] * damp
        inverse = lower_inverses([lower[head, p, p] for head in heads for p in range(blocks)])
        inverse = {
            (head, p): inverse[i * blocks + p] for i, head in enumerate(heads) for p in range(blocks)
        }
        if first == 0:
            copies[3].wait()
        factors = {}
        for p in range(blocks):
            for head in heads:
                at = columns[block(p), head : head + 1]
                weight = strengths[block(p), head : head + 1]
                right = jnp.concatenate(
                    [
                        keys[head // repeat][p] * (-weight * jnp.exp(at)),
                        v_ref[block(p), head * DV : (head + 1) * DV] * weight,
                    ],
                    axis=1,
                )
                for r in range(p):
                    right = right - dot_parts(split(lower[head, p, r]), split(factors[head, r]))
                factors[head, p] = dot_parts(inverse[head, p], split(right))
                factor_ref[head, block(p), :] = factors[head, p]
        flipped = {key_head: [split(k.T) for k in keys[key_head]] for key_head in keys}
        for head in heads:
            last = rows[head : head + 1, tokens - 1 : tokens]
            total = jnp.exp(last) * eye
            for p in range(blocks):
                ending = jnp.exp(last - columns[block(p), head : head + 1])
                total = total + dot_parts(flipped[head // repeat][p], split(factors[head, p] * ending))
            summary_ref[head] = total
        group = pl.ds(first, len(heads))
        leaving.append(
            pltpu.make_async_copy(
                factor_ref.at[group], factor_hbm.at[group], out_sems.at[len(leaving)]
            )
        )
        leaving[-1].start()
    if swap:
        target = factor_hbm.at[value_heads, pl.ds(0, DK)]
        leaving.append(
            pltpu.make_async_copy(summary_ref.at[partner(0, swap)], target, out_sems.at[len(leaving)])
        )
        leaving[-1].start()
    for place, out_ref in enumerate(summaries):
        out_ref[...] = summary_ref[partner(place + 1 if swap else place, swap)]
    for copy in leaving:
        copy.wait()


def output_kernel(
    decay_hbm,
    q_hbm,
    k_hbm,
    factor_hbm,
    map_hbm,
    decay_ref,
    q_ref,
    k_ref,
    factor_ref,
    sems,
    map_ref,
    out_sems,
):
    repeat = factor_ref.shape[0] // (k_hbm.shape[1] // DK)
    groups = [pl.ds(head, repeat) for head in range(0, factor_ref.shape[0], repeat)]
    copies = fetch(
        [(decay_hbm, decay_ref), (q_hbm, q_ref), (k_hbm, k_ref)]
        + [(factor_hbm.at[group], factor_ref.at[group]) for group in groups],
        sems,
    )
    leaving = []
    tokens = q_ref.shape[0]
    key_heads = q_ref.shape[1] // DK
    value_heads = factor_ref.shape[0]
    repeat = value_heads // key_heads
    blocks = tokens // BLOCK
    copies[0].wait()
    rows, columns = cumulative_logs(decay_ref[...])
    for copy in copies[1:3]:
        copy.wait()
    inclusive = iota((BLOCK, BLOCK), 0) >= iota((BLOCK, BLOCK), 1)
    for key_head in range(key_heads):
        lanes = slice(key_head * DK, (key_head + 1) * DK)
        queries = unit(q_ref[:, lanes]) * DK**-0.5
        keys = split(unit(k_ref[:, lanes]))
        heads = range(key_head * repeat, (key_head + 1) * repeat)
        parts = {}
        for p in range(blocks):
            query_parts = split(queries[block(p)])
            scores = [
                dot_parts_transposed(query_parts, tuple(part[block(r)] for part in keys))
                for r in range(p + 1)
            ]
            if p == 0:
                copies[3 + key_head].wait()
            for head in heads:
                at = columns[block(p), head : head + 1]
                parts[head, p] = split(factor_ref[head, block(p), :])
                total = jnp.concatenate(
                    [queries[block(p)] * jnp.exp(at), jnp.zeros((BLOCK, DV), jnp.float32)], axis=1
                )
                for r in range(p + 1):
                    spread = at - rows[head : head + 1, block(r)]
                    if p == r:
                        damp = jnp.where(inclusive, jnp.exp(jnp.where(inclusive, spread, 0.0)), 0.0)
                    else:
                        damp = jnp.exp(spread)
                    total = total + dot_parts(split(scores[r] * damp), parts[head, r])
                map_ref[head, block(p), :] = total
        group = groups[key_head]
        leaving.append(
            pltpu.make_async_copy(map_ref.at[group], map_hbm.at[group], out_sems.at[key_head])
        )
        leaving[-1].start()
    for copy in leaving:
        copy.wait()


def scan_kernel(held_ref, entry_ref):
    count, held, key_width, width = entry_ref.shape
    for head in range(held):
        state = jnp.zeros((key_width, width), jnp.float32)
        entry_ref[0, head] = state
        for source in range(count - 1):
            added = held_ref[source, head, :, key_width:]
            if source:
                added = added + dot(held_ref[source, head, :, :key_width], state)
            state = added
            entry_ref[source + 1, head] = state


def ordered_scan_kernel(factor_hbm, *rest):
    *arrays, held_ref, entry_ref, sems = rest
    count = entry_ref.shape[0]
    held, entries = arrays[: count - 1], arrays[count - 1 :]
    here = partner(0, True)
    own_summary = factor_hbm.at[factor_hbm.shape[0] - 1, pl.ds(0, DK)]
    own = pltpu.make_async_copy(own_summary, held_ref.at[here], sems.at[0])
    own.start()
    for i, summary in enumerate(held):
        held_ref[partner(i + 1, True)] = summary[...]
    own.wait()
    maps = [split(held_ref[source, :, :DK]) for source in range(1, count - 1)]
    state = held_ref[0, :, DK:]
    entry_ref[0] = jnp.zeros_like(state)
    entry_ref[1] = state
    for source in range(1, count - 1):
        state = held_ref[source, :, DK:] + dot_parts(maps[source - 1], split(state))
        entry_ref[source + 1] = state
    for i, entry in enumerate(entries):
        entry[...] = entry_ref[partner(i, True)]


def projection_kernel(map_hbm, gate_hbm, gain_ref, weight_ref, *rest, pieces, split_here, swap):
    if split_here:
        *rest, whole_ref, weight_sems = rest
        parts_ref = rest.pop(-8)
    else:
        parts_ref = weight_ref
    *arrays, map_ref, gate_ref, state_ref, high_ref, low_ref, gate_sems, map_sems = rest
    outs = arrays[-len(pieces) :]
    states = arrays[: -len(pieces)]
    heads = state_ref.shape[0]
    rows = outs[0].shape[0]
    blocks = sorted({index for index, _ in pieces})
    places = []
    for i, index in enumerate(blocks):
        start = (lax.axis_index("tp") ^ index) * rows if swap.rows else index * rows
        places.append((pl.ds(pl.multiple_of(start, rows), rows), pl.ds(i * rows, rows)))
    gates = fetch([(gate_hbm.at[s, :], gate_ref.at[t, :]) for s, t in places], gate_sems)
    maps = fetch(
        [
            (map_hbm.at[head, s, :], map_ref.at[head, t, :])
            for head in range(heads)
            for s, t in places
        ],
        map_sems,
    )
    if split_here:
        bands = [pl.ds(row, WEIGHT_ROWS) for row in range(0, weight_ref.shape[0], WEIGHT_ROWS)]
        weights = fetch(
            [(weight_ref.at[band, :], whole_ref.at[band, :]) for band in bands], weight_sems
        )
    for i, state in enumerate(states):
        state_ref[partner(i, swap.heads)] = state[...]
    for copy in gates:
        copy.wait()
    gain = gain_ref[...]
    for head in range(heads):
        lanes = slice(head * DV, (head + 1) * DV)
        gate = gate_ref[:, lanes]
        factor = gate / (1.0 + jnp.exp(-gate)) * gain
        for copy in maps[head * len(blocks) : (head + 1) * len(blocks)]:
            copy.wait()
        core = map_ref[head, :, DK:] + dot(map_ref[head, :, :DK], state_ref[head])
        scale = lax.rsqrt(jnp.mean(core * core, axis=-1, keepdims=True) + EPS)
        high_ref[:, lanes], low_ref[:, lanes] = split(core * scale * factor)
    total = len(blocks) * rows
    depth, columns = parts_ref.shape[1:]
    step = WEIGHT_ROWS if split_here else depth
    for index, row in enumerate(range(0, depth, step)):
        band = slice(row, row + step)
        if split_here:
            weights[index].wait()
            parts_ref[0, band, :], parts_ref[1, band, :] = split(whole_ref[band, :])
        for column in range(0, columns, BAND):
            lanes = slice(column, column + BAND)
            both = jnp.concatenate([high_ref[:, band], low_ref[:, band]], axis=0)
            sums = jnp.dot(both, parts_ref[0, band, lanes], preferred_element_type=jnp.float32)
            last = jnp.dot(
                high_ref[:, band], parts_ref[1, band, lanes], preferred_element_type=jnp.float32
            )
            result = sums[:total] + (sums[total:] + last)
            for (piece, start), out_ref in zip(pieces, outs):
                if start <= column < start + out_ref.shape[1]:
                    at = blocks.index(piece) * rows
                    target = slice(column - start, column - start + BAND)
                    part = result[at : at + rows]
                    out_ref[:, target] = part if index == 0 else out_ref[:, target] + part


def forward_kernel(across_ref, end_ref, going_ref):
    going_ref[...] = across_ref[...] + end_ref[...]


def hand_on_kernel(_, __, ___):
    pass


def shape(*dims):
    return jax.ShapeDtypeStruct(dims, jnp.float32)


def params(mebibytes):
    return pltpu.CompilerParams(vmem_limit_bytes=int(mebibytes * 1024 * 1024))


def cost(flops, *arrays):
    return pl.CostEstimate(
        flops=flops, bytes_accessed=4 * sum(a.size for a in arrays), transcendentals=0
    )


def partners_swap(arrays, axis):
    count = len(arrays)
    return [arrays[0]] + [
        lax.ppermute(array, axis, [(d, d ^ i) for d in range(count)])
        for array, i in zip(arrays[1:], SWAP_ORDER)
    ]


class Swap(typing.NamedTuple):
    heads: bool
    rows: bool


def swap_is_possible(heads, count):
    return heads == count == 1 + len(SWAP_ORDER)


def entering_states(factors, summaries, swap, beside, after):
    heads = factors.shape[0] - 1
    count = lax.axis_size("ctx")
    if swap:
        held = partners_swap([factors, *summaries], "ctx")
        held, beside = lax.optimization_barrier((held, beside))
        entry = shape(DK, DV)
        entries = pl.pallas_call(
            ordered_scan_kernel,
            in_specs=[HBM] + [VMEM] * (count - 1),
            out_specs=[VMEM] * count,
            out_shape=[entry] * count,
            scratch_shapes=[
                pltpu.VMEM((count, DK, DK + DV), jnp.float32),
                pltpu.VMEM((count, DK, DV), jnp.float32),
                pltpu.SemaphoreType.DMA((1,)),
            ],
            compiler_params=params(SCAN_VMEM),
            name="state_scan",
        )(*held)
        entries, after = lax.optimization_barrier((entries, after))
        return partners_swap(entries, "ctx"), beside, after
    parts = max(1, count // heads)
    per_owner = max(1, heads // count)
    width = DV // parts
    groups = heads // per_owner
    summary = jnp.stack(summaries)
    maps = summary[:, :, :DK].reshape(groups, 1, per_owner, DK, DK)
    maps = jnp.broadcast_to(maps, (groups, parts, per_owner, DK, DK))
    adds = summary[:, :, DK:].reshape(groups, per_owner, DK, parts, width)
    payload = jnp.concatenate([maps, adds.transpose(0, 3, 1, 2, 4)], axis=-1)
    payload = payload.reshape(count, per_owner, DK, DK + width)
    held = lax.all_to_all(payload, "ctx", split_axis=0, concat_axis=0, tiled=True)
    entries = pl.pallas_call(
        scan_kernel,
        out_shape=shape(count, per_owner, DK, width),
        compiler_params=params(32),
        name="state_scan",
    )(held)
    back = lax.all_to_all(entries, "ctx", split_axis=0, concat_axis=0, tiled=True)
    back = back.reshape(groups, parts, per_owner, DK, width).transpose(0, 2, 3, 1, 4)
    back = back.reshape(heads, DK, DV)
    return [back[head] for head in range(heads)], beside, after


def project_and_sum(project, columns, axis):
    count = lax.axis_size(axis)
    if count != 4:
        *pieces, _ = project([(i, 0, columns) for i in range(count)], FIRST_VMEM)
        whole = jnp.concatenate(pieces, axis=0)
        return lax.psum_scatter(whole, axis, scatter_dimension=0, tiled=True)
    opposite, parts = project([(3, 0, columns)], FIRST_VMEM)
    from_end = lax.ppermute(opposite, axis, [(0, 1), (3, 2)])
    from_inner = lax.ppermute(opposite, axis, [(1, 2), (2, 1)])
    across, own, near = project([(i, 0, columns) for i in (2, 0, 1)], LATER_VMEM, parts)
    going = pl.pallas_call(
        forward_kernel,
        out_shape=shape(*own.shape),
        compiler_params=params(LATER_VMEM),
        name="forward",
    )(across, from_end)
    anywhere = pl.BlockSpec(memory_space=pl.ANY)
    near = pl.pallas_call(
        hand_on_kernel,
        in_specs=[anywhere] * 2,
        out_specs=anywhere,
        out_shape=shape(*near.shape),
        input_output_aliases={0: 0},
        compiler_params=params(LATER_VMEM),
        name="hand_on",
    )(near, going)
    from_near = lax.ppermute(near, axis, [(i, i ^ 1) for i in range(4)])
    from_across = lax.ppermute(going, axis, [(i, i ^ 2) for i in range(4)])
    return ((own + from_inner) + from_near) + from_across


def per_device(queries, key_vectors, values, decays, strengths, out_gate, norm_gain, out_weight):
    tokens = queries.shape[0]
    heads = values.shape[1] // DV
    key_heads = queries.shape[1] // DK
    depth, columns = out_weight.shape
    rows = tokens // lax.axis_size("tp")
    gain = norm_gain.reshape(1, DV)
    swap = Swap(
        heads=swap_is_possible(heads, lax.axis_size("ctx")), rows=lax.axis_size("tp") == 4
    )

    def buffers(*arrays):
        return [pltpu.VMEM(a.shape, a.dtype) for a in arrays] + [
            pltpu.SemaphoreType.DMA((len(arrays),))
        ]

    factor_shape = shape(heads, tokens, DK + DV)
    groups = pl.cdiv(heads, HEADS_AT_ONCE)
    sent = heads - 1 if swap.heads else heads
    factors, *summaries = pl.pallas_call(
        functools.partial(summary_kernel, swap=swap.heads),
        in_specs=[HBM] * 4,
        out_specs=[HBM] + [VMEM] * sent,
        out_shape=[shape(heads + 1, tokens, DK + DV)] + [shape(DK, DK + DV)] * sent,
        scratch_shapes=buffers(decays, strengths, key_vectors, values)
        + [pltpu.VMEM(factor_shape.shape, jnp.float32), pltpu.VMEM((heads, DK, DK + DV), jnp.float32)]
        + [pltpu.SemaphoreType.DMA((groups + 1,))],
        compiler_params=params(MOST_VMEM),
        name="state_summary",
    )(decays, strengths, key_vectors, values)
    maps = pl.pallas_call(
        output_kernel,
        in_specs=[HBM] * 4,
        out_specs=HBM,
        out_shape=shape(8 * heads, tokens, DK + DV),
        scratch_shapes=[pltpu.VMEM(a.shape, jnp.float32) for a in (decays, queries, key_vectors)]
        + [pltpu.VMEM(factor_shape.shape, jnp.float32), pltpu.SemaphoreType.DMA((3 + key_heads,))]
        + [pltpu.VMEM(factor_shape.shape, jnp.float32), pltpu.SemaphoreType.DMA((key_heads,))],
        compiler_params=params(MAP_VMEM),
        cost_estimate=cost(3 * 2 * heads * tokens * tokens * 384, factors, factors, queries),
        name="output_maps",
    )(decays, queries, key_vectors, factors)
    states, maps, weights = entering_states(factors, summaries, swap.heads, maps, out_weight)
    parts_shape = jax.ShapeDtypeStruct((2, depth, columns), jnp.bfloat16)

    fetched = [
        pltpu.VMEM(out_weight.shape, jnp.float32),
        pltpu.SemaphoreType.DMA((depth // WEIGHT_ROWS,)),
    ]

    def project(pieces, vmem, parts=None):
        total = len({piece[0] for piece in pieces}) * rows
        normed = pltpu.VMEM((total, depth), jnp.bfloat16)
        counts = (total // rows, heads * total // rows)
        return pl.pallas_call(
            functools.partial(
                projection_kernel,
                pieces=[(index, start) for index, start, _ in pieces],
                split_here=parts is None,
                swap=swap,
            ),
            in_specs=[HBM] * 2 + [VMEM, HBM if parts is None else VMEM] + [VMEM] * heads,
            out_shape=[shape(rows, width) for _, _, width in pieces]
            + [parts_shape] * (parts is None),
            scratch_shapes=[
                pltpu.VMEM((heads, total, DK + DV), jnp.float32),
                pltpu.VMEM((total, heads * DV), jnp.float32),
                pltpu.VMEM((heads, DK, DV), jnp.float32),
                normed,
                normed,
            ]
            + [pltpu.SemaphoreType.DMA((n,)) for n in counts]
            + fetched * (parts is None),
            compiler_params=params(vmem),
            cost_estimate=cost(3 * 2 * total * depth * columns, out_weight),
            name="projection",
        )(maps, out_gate, gain, weights if parts is None else parts, *states)

    return project_and_sum(project, columns, "tp")


def solution(mesh):
    return jax.shard_map(
        per_device,
        mesh=mesh,
        in_specs=(
            P("ctx", "tp"),
            P("ctx", "tp"),
            P("ctx", "tp"),
            P("tp", "ctx"),
            P("tp", "ctx"),
            P("ctx", "tp"),
            P(),
            P("tp", None),
        ),
        out_specs=P(("ctx", "tp"), None),
        check_vma=False,
    )
```

```python
import functools
import typing

import jax
import jax.numpy as jnp
from jax import lax
from jax.experimental import pallas as pl
from jax.experimental.pallas import tpu as pltpu
from jax.sharding import PartitionSpec as P

DK = 128
DV = 128
BLOCK = 128
SMALL = 32
BAND = 256
SWAP_ORDER = (7, 6, 5, 4, 3, 2, 1)
WEIGHT_ROWS = 256
MOST_VMEM = 56
MAP_VMEM = 53.75
SCAN_VMEM = 52.25
FIRST_VMEM = 40
LATER_VMEM = 32
HEADS_AT_ONCE = 4
EPS = 1e-06


HBM = pl.BlockSpec(memory_space=pltpu.HBM)
VMEM = pl.BlockSpec(memory_space=pltpu.VMEM)


def dot(left, right):
    return jnp.dot(left, right, precision=lax.Precision.HIGH, preferred_element_type=jnp.float32)


def dot_transposed(left, right):
    return lax.dot_general(
        left,
        right,
        (((1,), (1,)), ((), ())),
        precision=lax.Precision.HIGH,
        preferred_element_type=jnp.float32,
    )


def iota(shape, dim):
    return lax.broadcasted_iota(jnp.int32, shape, dim)


def unit(rows):
    return rows * lax.rsqrt(jnp.sum(rows * rows, axis=-1, keepdims=True) + EPS)


def cumulative_logs(decays):
    tokens = decays.shape[1]
    upto = jnp.where(iota((tokens, tokens), 0) <= iota((tokens, tokens), 1), 1.0, 0.0)
    rows = jnp.dot(
        jnp.log(decays), upto, precision=lax.Precision.HIGHEST, preferred_element_type=jnp.float32
    )
    return rows, rows.T


def split(value):
    high = value.astype(jnp.bfloat16)
    return high, (value - high.astype(jnp.float32)).astype(jnp.bfloat16)


def dot_parts(left, right):
    rows = left[0].shape[0]
    both = jnp.concatenate(left, axis=0)
    sums = jnp.dot(both, right[0], preferred_element_type=jnp.float32)
    rest = jnp.dot(left[0], right[1], preferred_element_type=jnp.float32)
    return sums[:rows] + (sums[rows:] + rest)


def dot_parts_transposed(left, right):
    rows = left[0].shape[0]
    dims = (((1,), (1,)), ((), ()))
    both = jnp.concatenate(left, axis=0)
    sums = lax.dot_general(both, right[0], dims, preferred_element_type=jnp.float32)
    rest = lax.dot_general(left[0], right[1], dims, preferred_element_type=jnp.float32)
    return sums[:rows] + (sums[rows:] + rest)


def stack_parts(*values):
    return tuple(jnp.concatenate(pieces, axis=0) for pieces in zip(*values))


def spread_parts(parts, masks):
    return tuple(jnp.concatenate([part * mask for mask in masks], axis=0) for part in parts)


def lower_inverses(lowers):
    row = iota((SMALL, BLOCK), 0)
    lane = iota((SMALL, BLOCK), 1)
    column = lane % SMALL
    place = lane // SMALL
    eye = jnp.where(row == column, 1.0, 0.0)
    in_8 = row // 8 == column // 8
    in_16 = row // 16 == column // 16
    odd = place % 2 == 1
    masks = [
        jnp.where(place == index, 1.0, 0.0).astype(jnp.bfloat16) for index in range(BLOCK // SMALL)
    ]
    packed = []
    for lower in lowers:
        blocks = jnp.zeros((SMALL, BLOCK), jnp.float32)
        for index in range(BLOCK // SMALL):
            blocks = jnp.where(place == index, lower[index * SMALL : (index + 1) * SMALL], blocks)
        packed.append(blocks)
    nil = [jnp.where(in_8, blocks, 0.0) for blocks in packed]
    parts = [split(n) for n in nil]
    nil_2 = [split(dot_parts(n, spread_parts(n, masks))) for n in parts]
    start = [eye - n for n in nil]
    pairs = [
        dot_parts(stack_parts(n, split(s)), spread_parts(n, masks)) for n, s in zip(nil_2, start)
    ]
    start = [s + pair[SMALL:] for s, pair in zip(start, pairs)]
    nil_4 = [spread_parts(split(pair[:SMALL]), masks) for pair in pairs]
    inv = [s + dot_parts(split(s), n) for s, n in zip(start, nil_4)]
    step_16 = [
        spread_parts(split(jnp.where(in_16 & ~in_8, blocks, 0.0)), masks) for blocks in packed
    ]
    half = [jnp.concatenate([d[8:16], d[24:32]], axis=0) for d in inv]
    half = [dot_parts(split(h), w) for h, w in zip(half, step_16)]
    half = [dot_parts(split(h), spread_parts(split(d), masks)) for h, d in zip(half, inv)]
    inv = [
        jnp.concatenate([d[:8], d[8:16] - h[:8], d[16:24], d[24:] - h[8:]], axis=0)
        for d, h in zip(inv, half)
    ]
    step_32 = [spread_parts(split(jnp.where(in_16, 0.0, blocks)), masks) for blocks in packed]
    half = [dot_parts(split(d[16:]), w) for d, w in zip(inv, step_32)]
    half = [dot_parts(split(h), spread_parts(split(d), masks)) for h, d in zip(half, inv)]
    inv = [jnp.concatenate([d[:16], d[16:] - h], axis=0) for d, h in zip(inv, half)]
    wide = [spread_parts(split(d), masks) for d in inv]
    low = [jnp.where(odd, d, 0.0) for d in inv]
    zeros = jnp.zeros((SMALL, BLOCK), jnp.bfloat16)
    step_64 = []
    for lower in lowers:
        below = jnp.where(place == 0, lower[32:64], jnp.where(place == 2, lower[96:128], 0.0))
        step_64.append(
            tuple(
                jnp.concatenate([zeros, part * masks[0], zeros, part * masks[2]], axis=0)
                for part in split(below)
            )
        )
    half = [dot_parts(split(l), w) for l, w in zip(low, step_64)]
    half = [dot_parts(split(h), w) for h, w in zip(half, wide)]
    inv = [
        jnp.concatenate([jnp.where(odd, 0.0, d), l - h], axis=0) for d, l, h in zip(inv, low, half)
    ]
    left = iota((64, BLOCK), 1) < 64
    low = [jnp.where(left, 0.0, d) for d in inv]
    wide = [jnp.concatenate([jnp.where(left, d, 0.0), l], axis=0) for d, l in zip(inv, low)]
    wide_parts = [split(w) for w in wide]
    zeros = jnp.zeros((64, BLOCK), jnp.bfloat16)
    step_128 = [
        tuple(
            jnp.concatenate([zeros, part], axis=0) for part in split(jnp.where(left, lower[64:], 0.0))
        )
        for lower in lowers
    ]
    half = [dot_parts(tuple(part[64:] for part in l), w) for l, w in zip(wide_parts, step_128)]
    half = [dot_parts(split(h), w) for h, w in zip(half, wide_parts)]
    return [
        tuple(
            jnp.concatenate([high, low], axis=0)
            for high, low in zip((part[:64] for part in parts), split(w[64:] - h))
        )
        for parts, w, h in zip(wide_parts, wide, half)
    ]


def block(index):
    return slice(index * BLOCK, (index + 1) * BLOCK)


def fetch(pairs, sems):
    copies = [pltpu.make_async_copy(src, dst, sems.at[i]) for i, (src, dst) in enumerate(pairs)]
    for copy in copies:
        copy.start()
    return copies


def partner(place, swap):
    return lax.axis_index("ctx") ^ (0, *SWAP_ORDER)[place] if swap else place


def summary_kernel(decay_hbm, strength_hbm, k_hbm, v_hbm, factor_hbm, *rest, swap):
    *summaries, decay_ref, strength_ref, k_ref, v_ref, sems = rest[:-4]
    factor_ref, summary_ref, log_ref, out_sems = rest[-4:]
    copies = fetch(
        [(decay_hbm, decay_ref), (strength_hbm, strength_ref), (k_hbm, k_ref), (v_hbm, v_ref)], sems
    )
    tokens = k_ref.shape[0]
    key_heads = k_ref.shape[1] // DK
    value_heads = v_ref.shape[1] // DV
    repeat = value_heads // key_heads
    blocks = tokens // BLOCK
    for copy in copies[:2]:
        copy.wait()
    rows, columns = cumulative_logs(decay_ref[...])
    strengths = strength_ref[...].T
    strict = iota((BLOCK, BLOCK), 0) > iota((BLOCK, BLOCK), 1)
    eye = jnp.where(iota((BLOCK, DK + DV), 0) == iota((BLOCK, DK + DV), 1), 1.0, 0.0)
    log_ref[:value_heads] = rows
    target = factor_hbm.at[value_heads, pl.ds(DK, log_ref.shape[0])]
    leaving = [pltpu.make_async_copy(log_ref, target, out_sems.at[0])]
    leaving[0].start()
    copies[2].wait()
    for first in range(0, value_heads, HEADS_AT_ONCE):
        heads = range(first, min(first + HEADS_AT_ONCE, value_heads))
        keys = {}
        gram = {}
        for key_head in sorted({head // repeat for head in heads}):
            unit_rows = unit(k_ref[:, key_head * DK : (key_head + 1) * DK])
            keys[key_head] = [unit_rows[block(p)] for p in range(blocks)]
            gram[key_head] = {
                (p, r): dot_transposed(keys[key_head][p], keys[key_head][r])
                for p in range(blocks)
                for r in range(p + 1)
            }
        lower = {}
        for head in heads:
            for p in range(blocks):
                at = columns[block(p), head : head + 1]
                weight = strengths[block(p), head : head + 1]
                for r in range(p + 1):
                    spread = at - rows[head : head + 1, block(r)]
                    if p == r:
                        damp = jnp.where(strict, jnp.exp(jnp.where(strict, spread, 0.0)), 0.0)
                    else:
                        damp = jnp.exp(spread)
                    lower[head, p, r] = weight * gram[head // repeat][p, r] * damp
        inverse = lower_inverses([lower[head, p, p] for head in heads for p in range(blocks)])
        inverse = {
            (head, p): inverse[i * blocks + p] for i, head in enumerate(heads) for p in range(blocks)
        }
        if first == 0:
            copies[3].wait()
        factors = {}
        for p in range(blocks):
            for head in heads:
                at = columns[block(p), head : head + 1]
                weight = strengths[block(p), head : head + 1]
                right = jnp.concatenate(
                    [
                        keys[head // repeat][p] * (-weight * jnp.exp(at)),
                        v_ref[block(p), head * DV : (head + 1) * DV] * weight,
                    ],
                    axis=1,
                )
                for r in range(p):
                    right = right - dot_parts(split(lower[head, p, r]), split(factors[head, r]))
                factors[head, p] = dot_parts(inverse[head, p], split(right))
                factor_ref[head, block(p), :] = factors[head, p]
        flipped = {key_head: [split(k.T) for k in keys[key_head]] for key_head in keys}
        for head in heads:
            last = rows[head : head + 1, tokens - 1 : tokens]
            total = jnp.exp(last) * eye
            for p in range(blocks):
                ending = jnp.exp(last - columns[block(p), head : head + 1])
                total = total + dot_parts(flipped[head // repeat][p], split(factors[head, p] * ending))
            summary_ref[head] = total
        group = pl.ds(first, len(heads))
        leaving.append(
            pltpu.make_async_copy(
                factor_ref.at[group], factor_hbm.at[group], out_sems.at[len(leaving)]
            )
        )
        leaving[-1].start()
    if swap:
        target = factor_hbm.at[value_heads, pl.ds(0, DK)]
        leaving.append(
            pltpu.make_async_copy(summary_ref.at[partner(0, swap)], target, out_sems.at[len(leaving)])
        )
        leaving[-1].start()
    for place, out_ref in enumerate(summaries):
        out_ref[...] = summary_ref[partner(place + 1 if swap else place, swap)]
    for copy in leaving:
        copy.wait()


def output_kernel(
    q_hbm,
    k_hbm,
    factor_hbm,
    map_hbm,
    own_ref,
    log_ref,
    q_ref,
    k_ref,
    factor_ref,
    sems,
    map_ref,
    out_sems,
):
    repeat = factor_ref.shape[0] // (k_hbm.shape[1] // DK)
    groups = [pl.ds(head, repeat) for head in range(0, factor_ref.shape[0], repeat)]
    copies = fetch(
        [(factor_hbm.at[factor_ref.shape[0], pl.ds(DK, log_ref.shape[0])], log_ref)]
        + [(q_hbm, q_ref), (k_hbm, k_ref)]
        + [(factor_hbm.at[group], factor_ref.at[group]) for group in groups]
        + [(factor_hbm.at[factor_ref.shape[0], pl.ds(0, DK)], own_ref)],
        sems,
    )
    leaving = [copies.pop()]
    tokens = q_ref.shape[0]
    key_heads = q_ref.shape[1] // DK
    value_heads = factor_ref.shape[0]
    repeat = value_heads // key_heads
    blocks = tokens // BLOCK
    for copy in copies[:3]:
        copy.wait()
    rows = log_ref[:value_heads]
    columns = log_ref[...].T
    inclusive = iota((BLOCK, BLOCK), 0) >= iota((BLOCK, BLOCK), 1)
    for key_head in range(key_heads):
        lanes = slice(key_head * DK, (key_head + 1) * DK)
        queries = unit(q_ref[:, lanes]) * DK**-0.5
        keys = split(unit(k_ref[:, lanes]))
        heads = range(key_head * repeat, (key_head + 1) * repeat)
        parts = {}
        for p in range(blocks):
            query_parts = split(queries[block(p)])
            scores = [
                dot_parts_transposed(query_parts, tuple(part[block(r)] for part in keys))
                for r in range(p + 1)
            ]
            if p == 0:
                copies[3 + key_head].wait()
            for head in heads:
                at = columns[block(p), head : head + 1]
                parts[head, p] = split(factor_ref[head, block(p), :])
                total = jnp.concatenate(
                    [queries[block(p)] * jnp.exp(at), jnp.zeros((BLOCK, DV), jnp.float32)], axis=1
                )
                for r in range(p + 1):
                    spread = at - rows[head : head + 1, block(r)]
                    if p == r:
                        damp = jnp.where(inclusive, jnp.exp(jnp.where(inclusive, spread, 0.0)), 0.0)
                    else:
                        damp = jnp.exp(spread)
                    total = total + dot_parts(split(scores[r] * damp), parts[head, r])
                map_ref[head, block(p), :] = total
        group = groups[key_head]
        leaving.append(
            pltpu.make_async_copy(map_ref.at[group], map_hbm.at[group], out_sems.at[key_head])
        )
        leaving[-1].start()
    for copy in leaving:
        copy.wait()


def scan_kernel(held_ref, entry_ref):
    count, held, key_width, width = entry_ref.shape
    for head in range(held):
        state = jnp.zeros((key_width, width), jnp.float32)
        entry_ref[0, head] = state
        for source in range(count - 1):
            added = held_ref[source, head, :, key_width:]
            if source:
                added = added + dot(held_ref[source, head, :, :key_width], state)
            state = added
            entry_ref[source + 1, head] = state


def ordered_scan_kernel(*rest):
    *arrays, held_ref, entry_ref = rest
    count = entry_ref.shape[0]
    held, entries = arrays[:count], arrays[count:]
    for i, summary in enumerate(held):
        held_ref[partner(i, True)] = summary[...]
    maps = [split(held_ref[source, :, :DK]) for source in range(1, count - 1)]
    state = held_ref[0, :, DK:]
    entry_ref[0] = jnp.zeros_like(state)
    entry_ref[1] = state
    for source in range(1, count - 1):
        state = held_ref[source, :, DK:] + dot_parts(maps[source - 1], split(state))
        entry_ref[source + 1] = state
    for i, entry in enumerate(entries):
        entry[...] = entry_ref[partner(i, True)]


def projection_kernel(map_hbm, gate_hbm, gain_ref, weight_ref, *rest, pieces, split_here, swap):
    if split_here:
        *rest, whole_ref, weight_sems = rest
        parts_ref = rest.pop(-8)
    else:
        parts_ref = weight_ref
    *arrays, map_ref, gate_ref, state_ref, high_ref, low_ref, gate_sems, map_sems = rest
    outs = arrays[-len(pieces) :]
    states = arrays[: -len(pieces)]
    heads = state_ref.shape[0]
    rows = outs[0].shape[0]
    blocks = sorted({index for index, _ in pieces})
    places = []
    for i, index in enumerate(blocks):
        start = (lax.axis_index("tp") ^ index) * rows if swap.rows else index * rows
        places.append((pl.ds(pl.multiple_of(start, rows), rows), pl.ds(i * rows, rows)))
    gates = fetch([(gate_hbm.at[s, :], gate_ref.at[t, :]) for s, t in places], gate_sems)
    maps = fetch(
        [
            (map_hbm.at[head, s, :], map_ref.at[head, t, :])
            for head in range(heads)
            for s, t in places
        ],
        map_sems,
    )
    if split_here:
        bands = [pl.ds(row, WEIGHT_ROWS) for row in range(0, weight_ref.shape[0], WEIGHT_ROWS)]
        weights = fetch(
            [(weight_ref.at[band, :], whole_ref.at[band, :]) for band in bands], weight_sems
        )
    for i, state in enumerate(states):
        state_ref[partner(i, swap.heads)] = state[...]
    for copy in gates:
        copy.wait()
    gain = gain_ref[...]
    for head in range(heads):
        lanes = slice(head * DV, (head + 1) * DV)
        gate = gate_ref[:, lanes]
        factor = gate / (1.0 + jnp.exp(-gate)) * gain
        for copy in maps[head * len(blocks) : (head + 1) * len(blocks)]:
            copy.wait()
        core = map_ref[head, :, DK:] + dot(map_ref[head, :, :DK], state_ref[head])
        scale = lax.rsqrt(jnp.mean(core * core, axis=-1, keepdims=True) + EPS)
        high_ref[:, lanes], low_ref[:, lanes] = split(core * scale * factor)
    total = len(blocks) * rows
    depth, columns = parts_ref.shape[1:]
    step = WEIGHT_ROWS if split_here else depth
    for index, row in enumerate(range(0, depth, step)):
        band = slice(row, row + step)
        if split_here:
            weights[index].wait()
            parts_ref[0, band, :], parts_ref[1, band, :] = split(whole_ref[band, :])
        for column in range(0, columns, BAND):
            lanes = slice(column, column + BAND)
            both = jnp.concatenate([high_ref[:, band], low_ref[:, band]], axis=0)
            sums = jnp.dot(both, parts_ref[0, band, lanes], preferred_element_type=jnp.float32)
            last = jnp.dot(
                high_ref[:, band], parts_ref[1, band, lanes], preferred_element_type=jnp.float32
            )
            result = sums[:total] + (sums[total:] + last)
            for (piece, start), out_ref in zip(pieces, outs):
                if start <= column < start + out_ref.shape[1]:
                    at = blocks.index(piece) * rows
                    target = slice(column - start, column - start + BAND)
                    part = result[at : at + rows]
                    out_ref[:, target] = part if index == 0 else out_ref[:, target] + part


def forward_kernel(across_ref, end_ref, going_ref):
    going_ref[...] = across_ref[...] + end_ref[...]


def hand_on_kernel(_, __, ___):
    pass


def shape(*dims):
    return jax.ShapeDtypeStruct(dims, jnp.float32)


def params(mebibytes):
    return pltpu.CompilerParams(vmem_limit_bytes=int(mebibytes * 1024 * 1024))


def cost(flops, *arrays):
    return pl.CostEstimate(
        flops=flops, bytes_accessed=4 * sum(a.size for a in arrays), transcendentals=0
    )


def partners_swap(arrays, axis):
    count = len(arrays)
    return [arrays[0]] + [
        lax.ppermute(array, axis, [(d, d ^ i) for d in range(count)])
        for array, i in zip(arrays[1:], SWAP_ORDER)
    ]


class Swap(typing.NamedTuple):
    heads: bool
    rows: bool


def swap_is_possible(heads, count):
    return heads == count == 1 + len(SWAP_ORDER)


def entering_states(own, summaries, swap, beside, after):
    heads = len(summaries) + swap
    count = lax.axis_size("ctx")
    if swap:
        held = partners_swap([own, *summaries], "ctx")
        held, beside = lax.optimization_barrier((held, beside))
        entry = shape(DK, DV)
        entries = pl.pallas_call(
            ordered_scan_kernel,
            in_specs=[VMEM] * count,
            out_specs=[VMEM] * count,
            out_shape=[entry] * count,
            scratch_shapes=[
                pltpu.VMEM((count, DK, DK + DV), jnp.float32),
                pltpu.VMEM((count, DK, DV), jnp.float32),
            ],
            compiler_params=params(SCAN_VMEM),
            name="state_scan",
        )(*held)
        entries, after = lax.optimization_barrier((entries, after))
        return partners_swap(entries, "ctx"), beside, after
    parts = max(1, count // heads)
    per_owner = max(1, heads // count)
    width = DV // parts
    groups = heads // per_owner
    summary = jnp.stack(summaries)
    maps = summary[:, :, :DK].reshape(groups, 1, per_owner, DK, DK)
    maps = jnp.broadcast_to(maps, (groups, parts, per_owner, DK, DK))
    adds = summary[:, :, DK:].reshape(groups, per_owner, DK, parts, width)
    payload = jnp.concatenate([maps, adds.transpose(0, 3, 1, 2, 4)], axis=-1)
    payload = payload.reshape(count, per_owner, DK, DK + width)
    held = lax.all_to_all(payload, "ctx", split_axis=0, concat_axis=0, tiled=True)
    entries = pl.pallas_call(
        scan_kernel,
        out_shape=shape(count, per_owner, DK, width),
        compiler_params=params(32),
        name="state_scan",
    )(held)
    back = lax.all_to_all(entries, "ctx", split_axis=0, concat_axis=0, tiled=True)
    back = back.reshape(groups, parts, per_owner, DK, width).transpose(0, 2, 3, 1, 4)
    back = back.reshape(heads, DK, DV)
    return [back[head] for head in range(heads)], beside, after


def project_and_sum(project, columns, axis):
    count = lax.axis_size(axis)
    if count != 4:
        *pieces, _ = project([(i, 0, columns) for i in range(count)], FIRST_VMEM)
        whole = jnp.concatenate(pieces, axis=0)
        return lax.psum_scatter(whole, axis, scatter_dimension=0, tiled=True)
    opposite, parts = project([(3, 0, columns)], FIRST_VMEM)
    from_end = lax.ppermute(opposite, axis, [(0, 1), (3, 2)])
    from_inner = lax.ppermute(opposite, axis, [(1, 2), (2, 1)])
    across, own, near = project([(i, 0, columns) for i in (2, 0, 1)], LATER_VMEM, parts)
    going = pl.pallas_call(
        forward_kernel,
        out_shape=shape(*own.shape),
        compiler_params=params(LATER_VMEM),
        name="forward",
    )(across, from_end)
    anywhere = pl.BlockSpec(memory_space=pl.ANY)
    near = pl.pallas_call(
        hand_on_kernel,
        in_specs=[anywhere] * 2,
        out_specs=anywhere,
        out_shape=shape(*near.shape),
        input_output_aliases={0: 0},
        compiler_params=params(LATER_VMEM),
        name="hand_on",
    )(near, going)
    from_near = lax.ppermute(near, axis, [(i, i ^ 1) for i in range(4)])
    from_across = lax.ppermute(going, axis, [(i, i ^ 2) for i in range(4)])
    return ((own + from_inner) + from_near) + from_across


def per_device(queries, key_vectors, values, decays, strengths, out_gate, norm_gain, out_weight):
    tokens = queries.shape[0]
    heads = values.shape[1] // DV
    key_heads = queries.shape[1] // DK
    depth, columns = out_weight.shape
    rows = tokens // lax.axis_size("tp")
    gain = norm_gain.reshape(1, DV)
    swap = Swap(
        heads=swap_is_possible(heads, lax.axis_size("ctx")), rows=lax.axis_size("tp") == 4
    )

    def buffers(*arrays):
        return [pltpu.VMEM(a.shape, a.dtype) for a in arrays] + [
            pltpu.SemaphoreType.DMA((len(arrays),))
        ]

    factor_shape = shape(heads, tokens, DK + DV)
    groups = pl.cdiv(heads, HEADS_AT_ONCE)
    sent = heads - 1 if swap.heads else heads
    log_shape = shape(8 * pl.cdiv(heads, 8), tokens)
    factors, *summaries = pl.pallas_call(
        functools.partial(summary_kernel, swap=swap.heads),
        in_specs=[HBM] * 4,
        out_specs=[HBM] + [VMEM] * sent,
        out_shape=[shape(heads + 1, tokens, DK + DV)] + [shape(DK, DK + DV)] * sent,
        scratch_shapes=buffers(decays, strengths, key_vectors, values)
        + [pltpu.VMEM(factor_shape.shape, jnp.float32), pltpu.VMEM((heads, DK, DK + DV), jnp.float32)]
        + [pltpu.VMEM(log_shape.shape, jnp.float32), pltpu.SemaphoreType.DMA((groups + 2,))],
        compiler_params=params(MOST_VMEM),
        name="state_summary",
    )(decays, strengths, key_vectors, values)
    maps, own = pl.pallas_call(
        output_kernel,
        in_specs=[HBM] * 3,
        out_specs=[HBM, VMEM],
        out_shape=[shape(8 * heads, tokens, DK + DV), shape(DK, DK + DV)],
        scratch_shapes=[pltpu.VMEM(a.shape, jnp.float32) for a in (log_shape, queries, key_vectors)]
        + [pltpu.VMEM(factor_shape.shape, jnp.float32), pltpu.SemaphoreType.DMA((4 + key_heads,))]
        + [pltpu.VMEM(factor_shape.shape, jnp.float32), pltpu.SemaphoreType.DMA((key_heads,))],
        compiler_params=params(MAP_VMEM),
        cost_estimate=cost(3 * 2 * heads * tokens * tokens * 384, factors, factors, queries),
        name="output_maps",
    )(queries, key_vectors, factors)
    states, maps, weights = entering_states(own, summaries, swap.heads, maps, out_weight)
    parts_shape = jax.ShapeDtypeStruct((2, depth, columns), jnp.bfloat16)

    fetched = [
        pltpu.VMEM(out_weight.shape, jnp.float32),
        pltpu.SemaphoreType.DMA((depth // WEIGHT_ROWS,)),
    ]

    def project(pieces, vmem, parts=None):
        total = len({piece[0] for piece in pieces}) * rows
        normed = pltpu.VMEM((total, depth), jnp.bfloat16)
        counts = (total // rows, heads * total // rows)
        return pl.pallas_call(
            functools.partial(
                projection_kernel,
                pieces=[(index, start) for index, start, _ in pieces],
                split_here=parts is None,
                swap=swap,
            ),
            in_specs=[HBM] * 2 + [VMEM, HBM if parts is None else VMEM] + [VMEM] * heads,
            out_shape=[shape(rows, width) for _, _, width in pieces]
            + [parts_shape] * (parts is None),
            scratch_shapes=[
                pltpu.VMEM((heads, total, DK + DV), jnp.float32),
                pltpu.VMEM((total, heads * DV), jnp.float32),
                pltpu.VMEM((heads, DK, DV), jnp.float32),
                normed,
                normed,
            ]
            + [pltpu.SemaphoreType.DMA((n,)) for n in counts]
            + fetched * (parts is None),
            compiler_params=params(vmem),
            cost_estimate=cost(3 * 2 * total * depth * columns, out_weight),
            name="projection",
        )(maps, out_gate, gain, weights if parts is None else parts, *states)

    return project_and_sum(project, columns, "tp")


def solution(mesh):
    return jax.shard_map(
        per_device,
        mesh=mesh,
        in_specs=(
            P("ctx", "tp"),
            P("ctx", "tp"),
            P("ctx", "tp"),
            P("tp", "ctx"),
            P("tp", "ctx"),
            P("ctx", "tp"),
            P(),
            P("tp", None),
        ),
        out_specs=P(("ctx", "tp"), None),
        check_vma=False,
    )
```

```python
import functools
import typing

import jax
import jax.numpy as jnp
from jax import lax
from jax.experimental import pallas as pl
from jax.experimental.pallas import tpu as pltpu
from jax.sharding import PartitionSpec as P

DK = 128
DV = 128
BLOCK = 128
SMALL = 32
BAND = 256
SWAP_ORDER = (7, 6, 5, 4, 3, 2, 1)
WEIGHT_ROWS = 256
MOST_VMEM = 56
MAP_VMEM = 53.75
SCAN_VMEM = 52.25
FIRST_VMEM = 40
LATER_VMEM = 32
HEADS_AT_ONCE = 8
EPS = 1e-06


HBM = pl.BlockSpec(memory_space=pltpu.HBM)
VMEM = pl.BlockSpec(memory_space=pltpu.VMEM)


def dot(left, right):
    return jnp.dot(left, right, precision=lax.Precision.HIGH, preferred_element_type=jnp.float32)


def dot_transposed(left, right):
    return lax.dot_general(
        left,
        right,
        (((1,), (1,)), ((), ())),
        precision=lax.Precision.HIGH,
        preferred_element_type=jnp.float32,
    )


def iota(shape, dim):
    return lax.broadcasted_iota(jnp.int32, shape, dim)


def unit(rows):
    return rows * lax.rsqrt(jnp.sum(rows * rows, axis=-1, keepdims=True) + EPS)


def cumulative_logs(decays):
    tokens = decays.shape[1]
    upto = jnp.where(iota((tokens, tokens), 0) <= iota((tokens, tokens), 1), 1.0, 0.0)
    rows = jnp.dot(
        jnp.log(decays), upto, precision=lax.Precision.HIGHEST, preferred_element_type=jnp.float32
    )
    return rows, rows.T


def split(value):
    high = value.astype(jnp.bfloat16)
    return high, (value - high.astype(jnp.float32)).astype(jnp.bfloat16)


def dot_parts(left, right):
    rows = left[0].shape[0]
    both = jnp.concatenate(left, axis=0)
    sums = jnp.dot(both, right[0], preferred_element_type=jnp.float32)
    rest = jnp.dot(left[0], right[1], preferred_element_type=jnp.float32)
    return sums[:rows] + (sums[rows:] + rest)


def dot_parts_transposed(left, right):
    rows = left[0].shape[0]
    dims = (((1,), (1,)), ((), ()))
    both = jnp.concatenate(left, axis=0)
    sums = lax.dot_general(both, right[0], dims, preferred_element_type=jnp.float32)
    rest = lax.dot_general(left[0], right[1], dims, preferred_element_type=jnp.float32)
    return sums[:rows] + (sums[rows:] + rest)


def stack_parts(*values):
    return tuple(jnp.concatenate(pieces, axis=0) for pieces in zip(*values))


def spread_parts(parts, masks):
    return tuple(jnp.concatenate([part * mask for mask in masks], axis=0) for part in parts)


def lower_inverses(lowers):
    row = iota((SMALL, BLOCK), 0)
    lane = iota((SMALL, BLOCK), 1)
    column = lane % SMALL
    place = lane // SMALL
    eye = jnp.where(row == column, 1.0, 0.0)
    in_8 = row // 8 == column // 8
    in_16 = row // 16 == column // 16
    odd = place % 2 == 1
    masks = [
        jnp.where(place == index, 1.0, 0.0).astype(jnp.bfloat16) for index in range(BLOCK // SMALL)
    ]
    packed = []
    for lower in lowers:
        blocks = jnp.zeros((SMALL, BLOCK), jnp.float32)
        for index in range(BLOCK // SMALL):
            blocks = jnp.where(place == index, lower[index * SMALL : (index + 1) * SMALL], blocks)
        packed.append(blocks)
    nil = [jnp.where(in_8, blocks, 0.0) for blocks in packed]
    parts = [split(n) for n in nil]
    nil_2 = [split(dot_parts(n, spread_parts(n, masks))) for n in parts]
    start = [eye - n for n in nil]
    pairs = [
        dot_parts(stack_parts(n, split(s)), spread_parts(n, masks)) for n, s in zip(nil_2, start)
    ]
    start = [s + pair[SMALL:] for s, pair in zip(start, pairs)]
    nil_4 = [spread_parts(split(pair[:SMALL]), masks) for pair in pairs]
    inv = [s + dot_parts(split(s), n) for s, n in zip(start, nil_4)]
    step_16 = [
        spread_parts(split(jnp.where(in_16 & ~in_8, blocks, 0.0)), masks) for blocks in packed
    ]
    half = [jnp.concatenate([d[8:16], d[24:32]], axis=0) for d in inv]
    half = [dot_parts(split(h), w) for h, w in zip(half, step_16)]
    half = [dot_parts(split(h), spread_parts(split(d), masks)) for h, d in zip(half, inv)]
    inv = [
        jnp.concatenate([d[:8], d[8:16] - h[:8], d[16:24], d[24:] - h[8:]], axis=0)
        for d, h in zip(inv, half)
    ]
    step_32 = [spread_parts(split(jnp.where(in_16, 0.0, blocks)), masks) for blocks in packed]
    half = [dot_parts(split(d[16:]), w) for d, w in zip(inv, step_32)]
    half = [dot_parts(split(h), spread_parts(split(d), masks)) for h, d in zip(half, inv)]
    inv = [jnp.concatenate([d[:16], d[16:] - h], axis=0) for d, h in zip(inv, half)]
    wide = [spread_parts(split(d), masks) for d in inv]
    low = [jnp.where(odd, d, 0.0) for d in inv]
    zeros = jnp.zeros((SMALL, BLOCK), jnp.bfloat16)
    step_64 = []
    for lower in lowers:
        below = jnp.where(place == 0, lower[32:64], jnp.where(place == 2, lower[96:128], 0.0))
        step_64.append(
            tuple(
                jnp.concatenate([zeros, part * masks[0], zeros, part * masks[2]], axis=0)
                for part in split(below)
            )
        )
    half = [dot_parts(split(l), w) for l, w in zip(low, step_64)]
    half = [dot_parts(split(h), w) for h, w in zip(half, wide)]
    inv = [
        jnp.concatenate([jnp.where(odd, 0.0, d), l - h], axis=0) for d, l, h in zip(inv, low, half)
    ]
    left = iota((64, BLOCK), 1) < 64
    low = [jnp.where(left, 0.0, d) for d in inv]
    wide = [jnp.concatenate([jnp.where(left, d, 0.0), l], axis=0) for d, l in zip(inv, low)]
    wide_parts = [split(w) for w in wide]
    zeros = jnp.zeros((64, BLOCK), jnp.bfloat16)
    step_128 = [
        tuple(
            jnp.concatenate([zeros, part], axis=0) for part in split(jnp.where(left, lower[64:], 0.0))
        )
        for lower in lowers
    ]
    half = [dot_parts(tuple(part[64:] for part in l), w) for l, w in zip(wide_parts, step_128)]
    half = [dot_parts(split(h), w) for h, w in zip(half, wide_parts)]
    return [
        tuple(
            jnp.concatenate([high, low], axis=0)
            for high, low in zip((part[:64] for part in parts), split(w[64:] - h))
        )
        for parts, w, h in zip(wide_parts, wide, half)
    ]


def block(index):
    return slice(index * BLOCK, (index + 1) * BLOCK)


def fetch(pairs, sems):
    copies = [pltpu.make_async_copy(src, dst, sems.at[i]) for i, (src, dst) in enumerate(pairs)]
    for copy in copies:
        copy.start()
    return copies


def partner(place, swap):
    return lax.axis_index("ctx") ^ (0, *SWAP_ORDER)[place] if swap else place


def summary_kernel(decay_hbm, strength_hbm, k_hbm, v_hbm, factor_hbm, *rest, swap):
    *summaries, decay_ref, strength_ref, k_ref, v_ref, sems = rest[:-4]
    factor_ref, summary_ref, log_ref, out_sems = rest[-4:]
    copies = fetch(
        [(decay_hbm, decay_ref), (strength_hbm, strength_ref), (k_hbm, k_ref), (v_hbm, v_ref)], sems
    )
    tokens = k_ref.shape[0]
    key_heads = k_ref.shape[1] // DK
    value_heads = v_ref.shape[1] // DV
    repeat = value_heads // key_heads
    blocks = tokens // BLOCK
    for copy in copies[:2]:
        copy.wait()
    rows, columns = cumulative_logs(decay_ref[...])
    strengths = strength_ref[...].T
    strict = iota((BLOCK, BLOCK), 0) > iota((BLOCK, BLOCK), 1)
    eye = jnp.where(iota((BLOCK, DK + DV), 0) == iota((BLOCK, DK + DV), 1), 1.0, 0.0)
    log_ref[:value_heads] = rows
    target = factor_hbm.at[value_heads, pl.ds(DK, log_ref.shape[0])]
    leaving = [pltpu.make_async_copy(log_ref, target, out_sems.at[0])]
    leaving[0].start()
    copies[2].wait()
    for first in range(0, value_heads, HEADS_AT_ONCE):
        heads = range(first, min(first + HEADS_AT_ONCE, value_heads))
        keys = {}
        gram = {}
        for key_head in sorted({head // repeat for head in heads}):
            unit_rows = unit(k_ref[:, key_head * DK : (key_head + 1) * DK])
            keys[key_head] = [unit_rows[block(p)] for p in range(blocks)]
            gram[key_head] = {
                (p, r): dot_transposed(keys[key_head][p], keys[key_head][r])
                for p in range(blocks)
                for r in range(p + 1)
            }
        lower = {}
        for head in heads:
            for p in range(blocks):
                at = columns[block(p), head : head + 1]
                weight = strengths[block(p), head : head + 1]
                for r in range(p + 1):
                    spread = at - rows[head : head + 1, block(r)]
                    if p == r:
                        damp = jnp.where(strict, jnp.exp(jnp.where(strict, spread, 0.0)), 0.0)
                    else:
                        damp = jnp.exp(spread)
                    lower[head, p, r] = weight * gram[head // repeat][p, r] * damp
        inverse = lower_inverses([lower[head, p, p] for head in heads for p in range(blocks)])
        inverse = {
            (head, p): inverse[i * blocks + p] for i, head in enumerate(heads) for p in range(blocks)
        }
        if first == 0:
            copies[3].wait()
        factors = {}
        for p in range(blocks):
            for head in heads:
                at = columns[block(p), head : head + 1]
                weight = strengths[block(p), head : head + 1]
                right = jnp.concatenate(
                    [
                        keys[head // repeat][p] * (-weight * jnp.exp(at)),
                        v_ref[block(p), head * DV : (head + 1) * DV] * weight,
                    ],
                    axis=1,
                )
                for r in range(p):
                    right = right - dot_parts(split(lower[head, p, r]), split(factors[head, r]))
                factors[head, p] = dot_parts(inverse[head, p], split(right))
                factor_ref[head, block(p), :] = factors[head, p]
        flipped = {key_head: [split(k.T) for k in keys[key_head]] for key_head in keys}
        for head in heads:
            last = rows[head : head + 1, tokens - 1 : tokens]
            total = jnp.exp(last) * eye
            for p in range(blocks):
                ending = jnp.exp(last - columns[block(p), head : head + 1])
                total = total + dot_parts(flipped[head // repeat][p], split(factors[head, p] * ending))
            summary_ref[head] = total
        group = pl.ds(first, len(heads))
        leaving.append(
            pltpu.make_async_copy(
                factor_ref.at[group], factor_hbm.at[group], out_sems.at[len(leaving)]
            )
        )
        leaving[-1].start()
    if swap:
        target = factor_hbm.at[value_heads, pl.ds(0, DK)]
        leaving.append(
            pltpu.make_async_copy(summary_ref.at[partner(0, swap)], target, out_sems.at[len(leaving)])
        )
        leaving[-1].start()
    for place, out_ref in enumerate(summaries):
        out_ref[...] = summary_ref[partner(place + 1 if swap else place, swap)]
    for copy in leaving:
        copy.wait()


def output_kernel(
    q_hbm,
    k_hbm,
    factor_hbm,
    map_hbm,
    own_ref,
    log_ref,
    q_ref,
    k_ref,
    factor_ref,
    sems,
    map_ref,
    out_sems,
):
    repeat = factor_ref.shape[0] // (k_hbm.shape[1] // DK)
    groups = [pl.ds(head, repeat) for head in range(0, factor_ref.shape[0], repeat)]
    copies = fetch(
        [(factor_hbm.at[factor_ref.shape[0], pl.ds(DK, log_ref.shape[0])], log_ref)]
        + [(q_hbm, q_ref), (k_hbm, k_ref)]
        + [(factor_hbm.at[group], factor_ref.at[group]) for group in groups]
        + [(factor_hbm.at[factor_ref.shape[0], pl.ds(0, DK)], own_ref)],
        sems,
    )
    leaving = [copies.pop()]
    tokens = q_ref.shape[0]
    key_heads = q_ref.shape[1] // DK
    value_heads = factor_ref.shape[0]
    repeat = value_heads // key_heads
    blocks = tokens // BLOCK
    for copy in copies[:3]:
        copy.wait()
    rows = log_ref[:value_heads]
    columns = log_ref[...].T
    inclusive = iota((BLOCK, BLOCK), 0) >= iota((BLOCK, BLOCK), 1)
    for key_head in range(key_heads):
        lanes = slice(key_head * DK, (key_head + 1) * DK)
        queries = unit(q_ref[:, lanes]) * DK**-0.5
        keys = split(unit(k_ref[:, lanes]))
        heads = range(key_head * repeat, (key_head + 1) * repeat)
        parts = {}
        for p in range(blocks):
            query_parts = split(queries[block(p)])
            scores = [
                dot_parts_transposed(query_parts, tuple(part[block(r)] for part in keys))
                for r in range(p + 1)
            ]
            if p == 0:
                copies[3 + key_head].wait()
            for head in heads:
                at = columns[block(p), head : head + 1]
                parts[head, p] = split(factor_ref[head, block(p), :])
                total = jnp.concatenate(
                    [queries[block(p)] * jnp.exp(at), jnp.zeros((BLOCK, DV), jnp.float32)], axis=1
                )
                for r in range(p + 1):
                    spread = at - rows[head : head + 1, block(r)]
                    if p == r:
                        damp = jnp.where(inclusive, jnp.exp(jnp.where(inclusive, spread, 0.0)), 0.0)
                    else:
                        damp = jnp.exp(spread)
                    total = total + dot_parts(split(scores[r] * damp), parts[head, r])
                map_ref[head, block(p), :] = total
        group = groups[key_head]
        leaving.append(
            pltpu.make_async_copy(map_ref.at[group], map_hbm.at[group], out_sems.at[key_head])
        )
        leaving[-1].start()
    for copy in leaving:
        copy.wait()


def scan_kernel(held_ref, entry_ref):
    count, held, key_width, width = entry_ref.shape
    for head in range(held):
        state = jnp.zeros((key_width, width), jnp.float32)
        entry_ref[0, head] = state
        for source in range(count - 1):
            added = held_ref[source, head, :, key_width:]
            if source:
                added = added + dot(held_ref[source, head, :, :key_width], state)
            state = added
            entry_ref[source + 1, head] = state


def ordered_scan_kernel(_, *rest):
    *arrays, held_ref, entry_ref = rest
    count = entry_ref.shape[0]
    held, entries = arrays[:count], arrays[count:]
    for i, summary in enumerate(held):
        held_ref[partner(i, True)] = summary[...]
    maps = [split(held_ref[source, :, :DK]) for source in range(1, count - 1)]
    state = held_ref[0, :, DK:]
    entry_ref[0] = jnp.zeros_like(state)
    entry_ref[1] = state
    for source in range(1, count - 1):
        state = held_ref[source, :, DK:] + dot_parts(maps[source - 1], split(state))
        entry_ref[source + 1] = state
    for i, entry in enumerate(entries):
        entry[...] = entry_ref[partner(i, True)]


def projection_kernel(map_hbm, gate_hbm, gain_ref, weight_ref, *rest, pieces, split_here, swap):
    if split_here:
        *rest, whole_ref, weight_sems = rest
        parts_ref = rest.pop(-8)
    else:
        parts_ref = weight_ref
    *arrays, map_ref, gate_ref, state_ref, high_ref, low_ref, gate_sems, map_sems = rest
    outs = arrays[-len(pieces) :]
    states = arrays[: -len(pieces)]
    heads = state_ref.shape[0]
    rows = outs[0].shape[0]
    blocks = sorted({index for index, _ in pieces})
    places = []
    for i, index in enumerate(blocks):
        start = (lax.axis_index("tp") ^ index) * rows if swap.rows else index * rows
        places.append((pl.ds(pl.multiple_of(start, rows), rows), pl.ds(i * rows, rows)))
    gates = fetch([(gate_hbm.at[s, :], gate_ref.at[t, :]) for s, t in places], gate_sems)
    maps = fetch(
        [
            (map_hbm.at[head, s, :], map_ref.at[head, t, :])
            for head in range(heads)
            for s, t in places
        ],
        map_sems,
    )
    if split_here:
        bands = [pl.ds(row, WEIGHT_ROWS) for row in range(0, weight_ref.shape[0], WEIGHT_ROWS)]
        weights = fetch(
            [(weight_ref.at[band, :], whole_ref.at[band, :]) for band in bands], weight_sems
        )
    for i, state in enumerate(states):
        state_ref[partner(i, swap.heads)] = state[...]
    for copy in gates:
        copy.wait()
    gain = gain_ref[...]
    for head in range(heads):
        lanes = slice(head * DV, (head + 1) * DV)
        gate = gate_ref[:, lanes]
        factor = gate / (1.0 + jnp.exp(-gate)) * gain
        for copy in maps[head * len(blocks) : (head + 1) * len(blocks)]:
            copy.wait()
        core = map_ref[head, :, DK:] + dot(map_ref[head, :, :DK], state_ref[head])
        scale = lax.rsqrt(jnp.mean(core * core, axis=-1, keepdims=True) + EPS)
        high_ref[:, lanes], low_ref[:, lanes] = split(core * scale * factor)
    total = len(blocks) * rows
    depth, columns = parts_ref.shape[1:]
    step = WEIGHT_ROWS if split_here else depth
    for index, row in enumerate(range(0, depth, step)):
        band = slice(row, row + step)
        if split_here:
            weights[index].wait()
            parts_ref[0, band, :], parts_ref[1, band, :] = split(whole_ref[band, :])
        for column in range(0, columns, BAND):
            lanes = slice(column, column + BAND)
            both = jnp.concatenate([high_ref[:, band], low_ref[:, band]], axis=0)
            sums = jnp.dot(both, parts_ref[0, band, lanes], preferred_element_type=jnp.float32)
            last = jnp.dot(
                high_ref[:, band], parts_ref[1, band, lanes], preferred_element_type=jnp.float32
            )
            result = sums[:total] + (sums[total:] + last)
            for (piece, start), out_ref in zip(pieces, outs):
                if start <= column < start + out_ref.shape[1]:
                    at = blocks.index(piece) * rows
                    target = slice(column - start, column - start + BAND)
                    part = result[at : at + rows]
                    out_ref[:, target] = part if index == 0 else out_ref[:, target] + part


def forward_kernel(across_ref, end_ref, going_ref):
    going_ref[...] = across_ref[...] + end_ref[...]


def hand_on_kernel(_, __, ___):
    pass


def shape(*dims):
    return jax.ShapeDtypeStruct(dims, jnp.float32)


def params(mebibytes):
    return pltpu.CompilerParams(vmem_limit_bytes=int(mebibytes * 1024 * 1024))


def cost(flops, *arrays):
    return pl.CostEstimate(
        flops=flops, bytes_accessed=4 * sum(a.size for a in arrays), transcendentals=0
    )


def partners_swap(arrays, axis):
    count = len(arrays)
    return [arrays[0]] + [
        lax.ppermute(array, axis, [(d, d ^ i) for d in range(count)])
        for array, i in zip(arrays[1:], SWAP_ORDER)
    ]


class Swap(typing.NamedTuple):
    heads: bool
    rows: bool


def swap_is_possible(heads, count):
    return heads == count == 1 + len(SWAP_ORDER)


def entering_states(own, summaries, swap, beside, after):
    heads = len(summaries) + swap
    count = lax.axis_size("ctx")
    if swap:
        held = partners_swap([own, *summaries], "ctx")
        held, beside = lax.optimization_barrier((held, beside))
        entry = shape(DK, DV)
        entries = pl.pallas_call(
            ordered_scan_kernel,
            in_specs=[HBM] + [VMEM] * count,
            out_specs=[VMEM] * count,
            out_shape=[entry] * count,
            scratch_shapes=[
                pltpu.VMEM((count, DK, DK + DV), jnp.float32),
                pltpu.VMEM((count, DK, DV), jnp.float32),
            ],
            compiler_params=params(SCAN_VMEM),
            name="state_scan",
        )(beside, *held)
        entries, after = lax.optimization_barrier((entries, after))
        return partners_swap(entries, "ctx"), beside, after
    parts = max(1, count // heads)
    per_owner = max(1, heads // count)
    width = DV // parts
    groups = heads // per_owner
    summary = jnp.stack(summaries)
    maps = summary[:, :, :DK].reshape(groups, 1, per_owner, DK, DK)
    maps = jnp.broadcast_to(maps, (groups, parts, per_owner, DK, DK))
    adds = summary[:, :, DK:].reshape(groups, per_owner, DK, parts, width)
    payload = jnp.concatenate([maps, adds.transpose(0, 3, 1, 2, 4)], axis=-1)
    payload = payload.reshape(count, per_owner, DK, DK + width)
    held = lax.all_to_all(payload, "ctx", split_axis=0, concat_axis=0, tiled=True)
    entries = pl.pallas_call(
        scan_kernel,
        out_shape=shape(count, per_owner, DK, width),
        compiler_params=params(32),
        name="state_scan",
    )(held)
    back = lax.all_to_all(entries, "ctx", split_axis=0, concat_axis=0, tiled=True)
    back = back.reshape(groups, parts, per_owner, DK, width).transpose(0, 2, 3, 1, 4)
    back = back.reshape(heads, DK, DV)
    return [back[head] for head in range(heads)], beside, after


def project_and_sum(project, columns, axis):
    count = lax.axis_size(axis)
    if count != 4:
        *pieces, _ = project([(i, 0, columns) for i in range(count)], FIRST_VMEM)
        whole = jnp.concatenate(pieces, axis=0)
        return lax.psum_scatter(whole, axis, scatter_dimension=0, tiled=True)
    opposite, parts = project([(3, 0, columns)], FIRST_VMEM)
    from_end = lax.ppermute(opposite, axis, [(0, 1), (3, 2)])
    from_inner = lax.ppermute(opposite, axis, [(1, 2), (2, 1)])
    across, own, near = project([(i, 0, columns) for i in (2, 0, 1)], LATER_VMEM, parts)
    going = pl.pallas_call(
        forward_kernel,
        out_shape=shape(*own.shape),
        compiler_params=params(LATER_VMEM),
        name="forward",
    )(across, from_end)
    anywhere = pl.BlockSpec(memory_space=pl.ANY)
    near = pl.pallas_call(
        hand_on_kernel,
        in_specs=[anywhere] * 2,
        out_specs=anywhere,
        out_shape=shape(*near.shape),
        input_output_aliases={0: 0},
        compiler_params=params(LATER_VMEM),
        name="hand_on",
    )(near, going)
    from_near = lax.ppermute(near, axis, [(i, i ^ 1) for i in range(4)])
    from_across = lax.ppermute(going, axis, [(i, i ^ 2) for i in range(4)])
    return ((own + from_inner) + from_near) + from_across


def per_device(queries, key_vectors, values, decays, strengths, out_gate, norm_gain, out_weight):
    tokens = queries.shape[0]
    heads = values.shape[1] // DV
    key_heads = queries.shape[1] // DK
    depth, columns = out_weight.shape
    rows = tokens // lax.axis_size("tp")
    gain = norm_gain.reshape(1, DV)
    swap = Swap(
        heads=swap_is_possible(heads, lax.axis_size("ctx")), rows=lax.axis_size("tp") == 4
    )

    def buffers(*arrays):
        return [pltpu.VMEM(a.shape, a.dtype) for a in arrays] + [
            pltpu.SemaphoreType.DMA((len(arrays),))
        ]

    factor_shape = shape(heads, tokens, DK + DV)
    groups = pl.cdiv(heads, HEADS_AT_ONCE)
    sent = heads - 1 if swap.heads else heads
    log_shape = shape(8 * pl.cdiv(heads, 8), tokens)
    factors, *summaries = pl.pallas_call(
        functools.partial(summary_kernel, swap=swap.heads),
        in_specs=[HBM] * 4,
        out_specs=[HBM] + [VMEM] * sent,
        out_shape=[shape(heads + 1, tokens, DK + DV)] + [shape(DK, DK + DV)] * sent,
        scratch_shapes=buffers(decays, strengths, key_vectors, values)
        + [pltpu.VMEM(factor_shape.shape, jnp.float32), pltpu.VMEM((heads, DK, DK + DV), jnp.float32)]
        + [pltpu.VMEM(log_shape.shape, jnp.float32), pltpu.SemaphoreType.DMA((groups + 2,))],
        compiler_params=params(MOST_VMEM),
        name="state_summary",
    )(decays, strengths, key_vectors, values)
    maps, own = pl.pallas_call(
        output_kernel,
        in_specs=[HBM] * 3,
        out_specs=[HBM, VMEM],
        out_shape=[shape(8 * heads, tokens, DK + DV), shape(DK, DK + DV)],
        scratch_shapes=[pltpu.VMEM(a.shape, jnp.float32) for a in (log_shape, queries, key_vectors)]
        + [pltpu.VMEM(factor_shape.shape, jnp.float32), pltpu.SemaphoreType.DMA((4 + key_heads,))]
        + [pltpu.VMEM(factor_shape.shape, jnp.float32), pltpu.SemaphoreType.DMA((key_heads,))],
        compiler_params=params(MAP_VMEM),
        cost_estimate=cost(3 * 2 * heads * tokens * tokens * 384, factors, factors, queries),
        name="output_maps",
    )(queries, key_vectors, factors)
    states, maps, weights = entering_states(own, summaries, swap.heads, maps, out_weight)
    parts_shape = jax.ShapeDtypeStruct((2, depth, columns), jnp.bfloat16)

    fetched = [
        pltpu.VMEM(out_weight.shape, jnp.float32),
        pltpu.SemaphoreType.DMA((depth // WEIGHT_ROWS,)),
    ]

    def project(pieces, vmem, parts=None):
        total = len({piece[0] for piece in pieces}) * rows
        normed = pltpu.VMEM((total, depth), jnp.bfloat16)
        counts = (total // rows, heads * total // rows)
        return pl.pallas_call(
            functools.partial(
                projection_kernel,
                pieces=[(index, start) for index, start, _ in pieces],
                split_here=parts is None,
                swap=swap,
            ),
            in_specs=[HBM] * 2 + [VMEM, HBM if parts is None else VMEM] + [VMEM] * heads,
            out_shape=[shape(rows, width) for _, _, width in pieces]
            + [parts_shape] * (parts is None),
            scratch_shapes=[
                pltpu.VMEM((heads, total, DK + DV), jnp.float32),
                pltpu.VMEM((total, heads * DV), jnp.float32),
                pltpu.VMEM((heads, DK, DV), jnp.float32),
                normed,
                normed,
            ]
            + [pltpu.SemaphoreType.DMA((n,)) for n in counts]
            + fetched * (parts is None),
            compiler_params=params(vmem),
            cost_estimate=cost(3 * 2 * total * depth * columns, out_weight),
            name="projection",
        )(maps, out_gate, gain, weights if parts is None else parts, *states)

    return project_and_sum(project, columns, "tp")


def solution(mesh):
    return jax.shard_map(
        per_device,
        mesh=mesh,
        in_specs=(
            P("ctx", "tp"),
            P("ctx", "tp"),
            P("ctx", "tp"),
            P("tp", "ctx"),
            P("tp", "ctx"),
            P("ctx", "tp"),
            P(),
            P("tp", None),
        ),
        out_specs=P(("ctx", "tp"), None),
        check_vma=False,
    )
```

```python
import functools
import typing

import jax
import jax.numpy as jnp
from jax import lax
from jax.experimental import pallas as pl
from jax.experimental.pallas import tpu as pltpu
from jax.sharding import PartitionSpec as P

DK = 128
DV = 128
BLOCK = 128
SMALL = 32
BAND = 512
SWAP_ORDER = (1, 7, 6, 5, 4, 3, 2)
WEIGHT_ROWS = 256
MOST_VMEM = 56
MAP_VMEM = 53.75
SCAN_VMEM = 52.25
FIRST_VMEM = 40
LATER_VMEM = 32
HEADS_AT_ONCE = 8
EPS = 1e-06


HBM = pl.BlockSpec(memory_space=pltpu.HBM)
VMEM = pl.BlockSpec(memory_space=pltpu.VMEM)


def dot(left, right):
    return jnp.dot(left, right, precision=lax.Precision.HIGH, preferred_element_type=jnp.float32)


def dot_transposed(left, right):
    return lax.dot_general(
        left,
        right,
        (((1,), (1,)), ((), ())),
        precision=lax.Precision.HIGH,
        preferred_element_type=jnp.float32,
    )


def iota(shape, dim):
    return lax.broadcasted_iota(jnp.int32, shape, dim)


def unit(rows):
    return rows * lax.rsqrt(jnp.sum(rows * rows, axis=-1, keepdims=True) + EPS)


def cumulative_logs(decays):
    tokens = decays.shape[1]
    upto = jnp.where(iota((tokens, tokens), 0) <= iota((tokens, tokens), 1), 1.0, 0.0)
    rows = jnp.dot(
        jnp.log(decays), upto, precision=lax.Precision.HIGHEST, preferred_element_type=jnp.float32
    )
    return rows, rows.T


def split(value):
    high = value.astype(jnp.bfloat16)
    return high, (value - high.astype(jnp.float32)).astype(jnp.bfloat16)


def dot_parts(left, right):
    rows = left[0].shape[0]
    both = jnp.concatenate(left, axis=0)
    sums = jnp.dot(both, right[0], preferred_element_type=jnp.float32)
    rest = jnp.dot(left[0], right[1], preferred_element_type=jnp.float32)
    return sums[:rows] + (sums[rows:] + rest)


def dot_parts_transposed(left, right):
    rows = left[0].shape[0]
    dims = (((1,), (1,)), ((), ()))
    both = jnp.concatenate(left, axis=0)
    sums = lax.dot_general(both, right[0], dims, preferred_element_type=jnp.float32)
    rest = lax.dot_general(left[0], right[1], dims, preferred_element_type=jnp.float32)
    return sums[:rows] + (sums[rows:] + rest)


def stack_parts(*values):
    return tuple(jnp.concatenate(pieces, axis=0) for pieces in zip(*values))


def spread_parts(parts, masks):
    return tuple(jnp.concatenate([part * mask for mask in masks], axis=0) for part in parts)


def lower_inverses(lowers):
    row = iota((SMALL, BLOCK), 0)
    lane = iota((SMALL, BLOCK), 1)
    column = lane % SMALL
    place = lane // SMALL
    eye = jnp.where(row == column, 1.0, 0.0)
    in_8 = row // 8 == column // 8
    in_16 = row // 16 == column // 16
    odd = place % 2 == 1
    masks = [
        jnp.where(place == index, 1.0, 0.0).astype(jnp.bfloat16) for index in range(BLOCK // SMALL)
    ]
    packed = []
    for lower in lowers:
        blocks = jnp.zeros((SMALL, BLOCK), jnp.float32)
        for index in range(BLOCK // SMALL):
            blocks = jnp.where(place == index, lower[index * SMALL : (index + 1) * SMALL], blocks)
        packed.append(blocks)
    nil = [jnp.where(in_8, blocks, 0.0) for blocks in packed]
    parts = [split(n) for n in nil]
    nil_2 = [split(dot_parts(n, spread_parts(n, masks))) for n in parts]
    start = [eye - n for n in nil]
    pairs = [
        dot_parts(stack_parts(n, split(s)), spread_parts(n, masks)) for n, s in zip(nil_2, start)
    ]
    start = [s + pair[SMALL:] for s, pair in zip(start, pairs)]
    nil_4 = [spread_parts(split(pair[:SMALL]), masks) for pair in pairs]
    inv = [s + dot_parts(split(s), n) for s, n in zip(start, nil_4)]
    step_16 = [
        spread_parts(split(jnp.where(in_16 & ~in_8, blocks, 0.0)), masks) for blocks in packed
    ]
    half = [jnp.concatenate([d[8:16], d[24:32]], axis=0) for d in inv]
    half = [dot_parts(split(h), w) for h, w in zip(half, step_16)]
    half = [dot_parts(split(h), spread_parts(split(d), masks)) for h, d in zip(half, inv)]
    inv = [
        jnp.concatenate([d[:8], d[8:16] - h[:8], d[16:24], d[24:] - h[8:]], axis=0)
        for d, h in zip(inv, half)
    ]
    step_32 = [spread_parts(split(jnp.where(in_16, 0.0, blocks)), masks) for blocks in packed]
    half = [dot_parts(split(d[16:]), w) for d, w in zip(inv, step_32)]
    half = [dot_parts(split(h), spread_parts(split(d), masks)) for h, d in zip(half, inv)]
    inv = [jnp.concatenate([d[:16], d[16:] - h], axis=0) for d, h in zip(inv, half)]
    wide = [spread_parts(split(d), masks) for d in inv]
    low = [jnp.where(odd, d, 0.0) for d in inv]
    zeros = jnp.zeros((SMALL, BLOCK), jnp.bfloat16)
    step_64 = []
    for lower in lowers:
        below = jnp.where(place == 0, lower[32:64], jnp.where(place == 2, lower[96:128], 0.0))
        step_64.append(
            tuple(
                jnp.concatenate([zeros, part * masks[0], zeros, part * masks[2]], axis=0)
                for part in split(below)
            )
        )
    half = [dot_parts(split(l), w) for l, w in zip(low, step_64)]
    half = [dot_parts(split(h), w) for h, w in zip(half, wide)]
    inv = [
        jnp.concatenate([jnp.where(odd, 0.0, d), l - h], axis=0) for d, l, h in zip(inv, low, half)
    ]
    left = iota((64, BLOCK), 1) < 64
    low = [jnp.where(left, 0.0, d) for d in inv]
    wide = [jnp.concatenate([jnp.where(left, d, 0.0), l], axis=0) for d, l in zip(inv, low)]
    wide_parts = [split(w) for w in wide]
    zeros = jnp.zeros((64, BLOCK), jnp.bfloat16)
    step_128 = [
        tuple(
            jnp.concatenate([zeros, part], axis=0) for part in split(jnp.where(left, lower[64:], 0.0))
        )
        for lower in lowers
    ]
    half = [dot_parts(tuple(part[64:] for part in l), w) for l, w in zip(wide_parts, step_128)]
    half = [dot_parts(split(h), w) for h, w in zip(half, wide_parts)]
    return [
        tuple(
            jnp.concatenate([high, low], axis=0)
            for high, low in zip((part[:64] for part in parts), split(w[64:] - h))
        )
        for parts, w, h in zip(wide_parts, wide, half)
    ]


def block(index):
    return slice(index * BLOCK, (index + 1) * BLOCK)


def fetch(pairs, sems):
    copies = [pltpu.make_async_copy(src, dst, sems.at[i]) for i, (src, dst) in enumerate(pairs)]
    for copy in copies:
        copy.start()
    return copies


def partner(place, swap):
    return lax.axis_index("ctx") ^ (0, *SWAP_ORDER)[place] if swap else place


def summary_kernel(decay_hbm, strength_hbm, k_hbm, v_hbm, factor_hbm, *rest, swap):
    *summaries, decay_ref, strength_ref, k_ref, v_ref, sems = rest[:-4]
    factor_ref, summary_ref, log_ref, out_sems = rest[-4:]
    copies = fetch(
        [(decay_hbm, decay_ref), (strength_hbm, strength_ref), (k_hbm, k_ref), (v_hbm, v_ref)], sems
    )
    tokens = k_ref.shape[0]
    key_heads = k_ref.shape[1] // DK
    value_heads = v_ref.shape[1] // DV
    repeat = value_heads // key_heads
    blocks = tokens // BLOCK
    for copy in copies[:2]:
        copy.wait()
    rows, columns = cumulative_logs(decay_ref[...])
    strengths = strength_ref[...].T
    strict = iota((BLOCK, BLOCK), 0) > iota((BLOCK, BLOCK), 1)
    eye = jnp.where(iota((BLOCK, DK + DV), 0) == iota((BLOCK, DK + DV), 1), 1.0, 0.0)
    log_ref[:value_heads] = rows
    target = factor_hbm.at[value_heads, pl.ds(DK, log_ref.shape[0])]
    leaving = [pltpu.make_async_copy(log_ref, target, out_sems.at[0])]
    leaving[0].start()
    copies[2].wait()
    for first in range(0, value_heads, HEADS_AT_ONCE):
        heads = range(first, min(first + HEADS_AT_ONCE, value_heads))
        keys = {}
        gram = {}
        for key_head in sorted({head // repeat for head in heads}):
            unit_rows = unit(k_ref[:, key_head * DK : (key_head + 1) * DK])
            keys[key_head] = [unit_rows[block(p)] for p in range(blocks)]
            gram[key_head] = {
                (p, r): dot_transposed(keys[key_head][p], keys[key_head][r])
                for p in range(blocks)
                for r in range(p + 1)
            }
        lower = {}
        for head in heads:
            for p in range(blocks):
                at = columns[block(p), head : head + 1]
                weight = strengths[block(p), head : head + 1]
                for r in range(p + 1):
                    spread = at - rows[head : head + 1, block(r)]
                    if p == r:
                        damp = jnp.where(strict, jnp.exp(jnp.where(strict, spread, 0.0)), 0.0)
                    else:
                        damp = jnp.exp(spread)
                    lower[head, p, r] = weight * gram[head // repeat][p, r] * damp
        inverse = lower_inverses([lower[head, p, p] for head in heads for p in range(blocks)])
        inverse = {
            (head, p): inverse[i * blocks + p] for i, head in enumerate(heads) for p in range(blocks)
        }
        if first == 0:
            copies[3].wait()
        factors = {}
        for p in range(blocks):
            for head in heads:
                at = columns[block(p), head : head + 1]
                weight = strengths[block(p), head : head + 1]
                right = jnp.concatenate(
                    [
                        keys[head // repeat][p] * (-weight * jnp.exp(at)),
                        v_ref[block(p), head * DV : (head + 1) * DV] * weight,
                    ],
                    axis=1,
                )
                for r in range(p):
                    right = right - dot_parts(split(lower[head, p, r]), split(factors[head, r]))
                factors[head, p] = dot_parts(inverse[head, p], split(right))
                factor_ref[head, block(p), :] = factors[head, p]
        flipped = {key_head: [split(k.T) for k in keys[key_head]] for key_head in keys}
        for head in heads:
            last = rows[head : head + 1, tokens - 1 : tokens]
            total = jnp.exp(last) * eye
            for p in range(blocks):
                ending = jnp.exp(last - columns[block(p), head : head + 1])
                total = total + dot_parts(flipped[head // repeat][p], split(factors[head, p] * ending))
            summary_ref[head] = total
        group = pl.ds(first, len(heads))
        leaving.append(
            pltpu.make_async_copy(
                factor_ref.at[group], factor_hbm.at[group], out_sems.at[len(leaving)]
            )
        )
        leaving[-1].start()
    if swap:
        target = factor_hbm.at[value_heads, pl.ds(0, DK)]
        leaving.append(
            pltpu.make_async_copy(summary_ref.at[partner(0, swap)], target, out_sems.at[len(leaving)])
        )
        leaving[-1].start()
    for place, out_ref in enumerate(summaries):
        out_ref[...] = summary_ref[partner(place + 1 if swap else place, swap)]
    for copy in leaving:
        copy.wait()


def output_kernel(
    q_hbm,
    k_hbm,
    factor_hbm,
    map_hbm,
    own_ref,
    log_ref,
    q_ref,
    k_ref,
    factor_ref,
    sems,
    map_ref,
    out_sems,
):
    repeat = factor_ref.shape[0] // (k_hbm.shape[1] // DK)
    groups = [pl.ds(head, repeat) for head in range(0, factor_ref.shape[0], repeat)]
    copies = fetch(
        [(factor_hbm.at[factor_ref.shape[0], pl.ds(DK, log_ref.shape[0])], log_ref)]
        + [(q_hbm, q_ref), (k_hbm, k_ref)]
        + [(factor_hbm.at[group], factor_ref.at[group]) for group in groups]
        + [(factor_hbm.at[factor_ref.shape[0], pl.ds(0, DK)], own_ref)],
        sems,
    )
    leaving = [copies.pop()]
    tokens = q_ref.shape[0]
    key_heads = q_ref.shape[1] // DK
    value_heads = factor_ref.shape[0]
    repeat = value_heads // key_heads
    blocks = tokens // BLOCK
    for copy in copies[:3]:
        copy.wait()
    rows = log_ref[:value_heads]
    columns = log_ref[...].T
    inclusive = iota((BLOCK, BLOCK), 0) >= iota((BLOCK, BLOCK), 1)
    for key_head in range(key_heads):
        lanes = slice(key_head * DK, (key_head + 1) * DK)
        queries = unit(q_ref[:, lanes]) * DK**-0.5
        keys = split(unit(k_ref[:, lanes]))
        heads = range(key_head * repeat, (key_head + 1) * repeat)
        parts = {}
        for p in range(blocks):
            query_parts = split(queries[block(p)])
            scores = [
                dot_parts_transposed(query_parts, tuple(part[block(r)] for part in keys))
                for r in range(p + 1)
            ]
            if p == 0:
                copies[3 + key_head].wait()
            for head in heads:
                at = columns[block(p), head : head + 1]
                parts[head, p] = split(factor_ref[head, block(p), :])
                total = jnp.concatenate(
                    [queries[block(p)] * jnp.exp(at), jnp.zeros((BLOCK, DV), jnp.float32)], axis=1
                )
                for r in range(p + 1):
                    spread = at - rows[head : head + 1, block(r)]
                    if p == r:
                        damp = jnp.where(inclusive, jnp.exp(jnp.where(inclusive, spread, 0.0)), 0.0)
                    else:
                        damp = jnp.exp(spread)
                    total = total + dot_parts(split(scores[r] * damp), parts[head, r])
                map_ref[head, block(p), :] = total
        group = groups[key_head]
        leaving.append(
            pltpu.make_async_copy(map_ref.at[group], map_hbm.at[group], out_sems.at[key_head])
        )
        leaving[-1].start()
    for copy in leaving:
        copy.wait()


def scan_kernel(held_ref, entry_ref):
    count, held, key_width, width = entry_ref.shape
    for head in range(held):
        state = jnp.zeros((key_width, width), jnp.float32)
        entry_ref[0, head] = state
        for source in range(count - 1):
            added = held_ref[source, head, :, key_width:]
            if source:
                added = added + dot(held_ref[source, head, :, :key_width], state)
            state = added
            entry_ref[source + 1, head] = state


def ordered_scan_kernel(_, *rest):
    *arrays, held_ref, entry_ref = rest
    count = entry_ref.shape[0]
    held, entries = arrays[:count], arrays[count:]
    for i, summary in enumerate(held):
        held_ref[partner(i, True)] = summary[...]
    maps = [split(held_ref[source, :, :DK]) for source in range(1, count - 1)]
    state = held_ref[0, :, DK:]
    entry_ref[0] = jnp.zeros_like(state)
    entry_ref[1] = state
    for source in range(1, count - 1):
        state = held_ref[source, :, DK:] + dot_parts(maps[source - 1], split(state))
        entry_ref[source + 1] = state
    for i, entry in enumerate(entries):
        entry[...] = entry_ref[partner(i, True)]


def projection_kernel(map_hbm, gate_hbm, gain_ref, weight_ref, *rest, pieces, split_here, swap):
    if split_here:
        *rest, whole_ref, weight_sems = rest
        parts_ref = rest.pop(-8)
    else:
        parts_ref = weight_ref
    *arrays, map_ref, gate_ref, state_ref, high_ref, low_ref, gate_sems, map_sems = rest
    outs = arrays[-len(pieces) :]
    states = arrays[: -len(pieces)]
    heads = state_ref.shape[0]
    rows = outs[0].shape[0]
    blocks = sorted({index for index, _ in pieces})
    places = []
    for i, index in enumerate(blocks):
        start = (lax.axis_index("tp") ^ index) * rows if swap.rows else index * rows
        places.append((pl.ds(pl.multiple_of(start, rows), rows), pl.ds(i * rows, rows)))
    gates = fetch([(gate_hbm.at[s, :], gate_ref.at[t, :]) for s, t in places], gate_sems)
    maps = fetch(
        [
            (map_hbm.at[head, s, :], map_ref.at[head, t, :])
            for head in range(heads)
            for s, t in places
        ],
        map_sems,
    )
    if split_here:
        bands = [pl.ds(row, WEIGHT_ROWS) for row in range(0, weight_ref.shape[0], WEIGHT_ROWS)]
        weights = fetch(
            [(weight_ref.at[band, :], whole_ref.at[band, :]) for band in bands], weight_sems
        )
    for i, state in enumerate(states):
        state_ref[partner(i, swap.heads)] = state[...]
    for copy in gates:
        copy.wait()
    gain = gain_ref[...]
    for head in range(heads):
        lanes = slice(head * DV, (head + 1) * DV)
        gate = gate_ref[:, lanes]
        factor = gate / (1.0 + jnp.exp(-gate)) * gain
        for copy in maps[head * len(blocks) : (head + 1) * len(blocks)]:
            copy.wait()
        core = map_ref[head, :, DK:] + dot(map_ref[head, :, :DK], state_ref[head])
        scale = lax.rsqrt(jnp.mean(core * core, axis=-1, keepdims=True) + EPS)
        high_ref[:, lanes], low_ref[:, lanes] = split(core * scale * factor)
    total = len(blocks) * rows
    depth, columns = parts_ref.shape[1:]
    step = WEIGHT_ROWS if split_here else depth
    for index, row in enumerate(range(0, depth, step)):
        band = slice(row, row + step)
        if split_here:
            weights[index].wait()
            parts_ref[0, band, :], parts_ref[1, band, :] = split(whole_ref[band, :])
        for column in range(0, columns, BAND):
            lanes = slice(column, column + BAND)
            both = jnp.concatenate([high_ref[:, band], low_ref[:, band]], axis=0)
            sums = jnp.dot(both, parts_ref[0, band, lanes], preferred_element_type=jnp.float32)
            last = jnp.dot(
                high_ref[:, band], parts_ref[1, band, lanes], preferred_element_type=jnp.float32
            )
            result = sums[:total] + (sums[total:] + last)
            for (piece, start), out_ref in zip(pieces, outs):
                if start <= column < start + out_ref.shape[1]:
                    at = blocks.index(piece) * rows
                    target = slice(column - start, column - start + BAND)
                    part = result[at : at + rows]
                    out_ref[:, target] = part if index == 0 else out_ref[:, target] + part


def forward_kernel(across_ref, end_ref, going_ref):
    going_ref[...] = across_ref[...] + end_ref[...]


def hand_on_kernel(_, __, ___):
    pass


def shape(*dims):
    return jax.ShapeDtypeStruct(dims, jnp.float32)


def params(mebibytes):
    return pltpu.CompilerParams(vmem_limit_bytes=int(mebibytes * 1024 * 1024))


def cost(flops, *arrays):
    return pl.CostEstimate(
        flops=flops, bytes_accessed=4 * sum(a.size for a in arrays), transcendentals=0
    )


def partners_swap(arrays, axis):
    count = len(arrays)
    return [arrays[0]] + [
        lax.ppermute(array, axis, [(d, d ^ i) for d in range(count)])
        for array, i in zip(arrays[1:], SWAP_ORDER)
    ]


class Swap(typing.NamedTuple):
    heads: bool
    rows: bool


def swap_is_possible(heads, count):
    return heads == count == 1 + len(SWAP_ORDER)


def entering_states(own, summaries, swap, beside, after):
    heads = len(summaries) + swap
    count = lax.axis_size("ctx")
    if swap:
        held = partners_swap([own, *summaries], "ctx")
        held, beside = lax.optimization_barrier((held, beside))
        entry = shape(DK, DV)
        entries = pl.pallas_call(
            ordered_scan_kernel,
            in_specs=[HBM] + [VMEM] * count,
            out_specs=[VMEM] * count,
            out_shape=[entry] * count,
            scratch_shapes=[
                pltpu.VMEM((count, DK, DK + DV), jnp.float32),
                pltpu.VMEM((count, DK, DV), jnp.float32),
            ],
            compiler_params=params(SCAN_VMEM),
            name="state_scan",
        )(beside, *held)
        entries, after = lax.optimization_barrier((entries, after))
        return partners_swap(entries, "ctx"), beside, after
    parts = max(1, count // heads)
    per_owner = max(1, heads // count)
    width = DV // parts
    groups = heads // per_owner
    summary = jnp.stack(summaries)
    maps = summary[:, :, :DK].reshape(groups, 1, per_owner, DK, DK)
    maps = jnp.broadcast_to(maps, (groups, parts, per_owner, DK, DK))
    adds = summary[:, :, DK:].reshape(groups, per_owner, DK, parts, width)
    payload = jnp.concatenate([maps, adds.transpose(0, 3, 1, 2, 4)], axis=-1)
    payload = payload.reshape(count, per_owner, DK, DK + width)
    held = lax.all_to_all(payload, "ctx", split_axis=0, concat_axis=0, tiled=True)
    entries = pl.pallas_call(
        scan_kernel,
        out_shape=shape(count, per_owner, DK, width),
        compiler_params=params(32),
        name="state_scan",
    )(held)
    back = lax.all_to_all(entries, "ctx", split_axis=0, concat_axis=0, tiled=True)
    back = back.reshape(groups, parts, per_owner, DK, width).transpose(0, 2, 3, 1, 4)
    back = back.reshape(heads, DK, DV)
    return [back[head] for head in range(heads)], beside, after


def project_and_sum(project, columns, axis):
    count = lax.axis_size(axis)
    if count != 4:
        *pieces, _ = project([(i, 0, columns) for i in range(count)], FIRST_VMEM)
        whole = jnp.concatenate(pieces, axis=0)
        return lax.psum_scatter(whole, axis, scatter_dimension=0, tiled=True)
    opposite, parts = project([(3, 0, columns)], FIRST_VMEM)
    from_end = lax.ppermute(opposite, axis, [(0, 1), (3, 2)])
    from_inner = lax.ppermute(opposite, axis, [(1, 2), (2, 1)])
    across, own, near = project([(i, 0, columns) for i in (2, 0, 1)], LATER_VMEM, parts)
    going = pl.pallas_call(
        forward_kernel,
        out_shape=shape(*own.shape),
        compiler_params=params(LATER_VMEM),
        name="forward",
    )(across, from_end)
    anywhere = pl.BlockSpec(memory_space=pl.ANY)
    near = pl.pallas_call(
        hand_on_kernel,
        in_specs=[anywhere] * 2,
        out_specs=anywhere,
        out_shape=shape(*near.shape),
        input_output_aliases={0: 0},
        compiler_params=params(LATER_VMEM),
        name="hand_on",
    )(near, going)
    from_near = lax.ppermute(near, axis, [(i, i ^ 1) for i in range(4)])
    from_across = lax.ppermute(going, axis, [(i, i ^ 2) for i in range(4)])
    return ((own + from_inner) + from_near) + from_across


def per_device(queries, key_vectors, values, decays, strengths, out_gate, norm_gain, out_weight):
    tokens = queries.shape[0]
    heads = values.shape[1] // DV
    key_heads = queries.shape[1] // DK
    depth, columns = out_weight.shape
    rows = tokens // lax.axis_size("tp")
    gain = norm_gain.reshape(1, DV)
    swap = Swap(
        heads=swap_is_possible(heads, lax.axis_size("ctx")), rows=lax.axis_size("tp") == 4
    )

    def buffers(*arrays):
        return [pltpu.VMEM(a.shape, a.dtype) for a in arrays] + [
            pltpu.SemaphoreType.DMA((len(arrays),))
        ]

    factor_shape = shape(heads, tokens, DK + DV)
    groups = pl.cdiv(heads, HEADS_AT_ONCE)
    sent = heads - 1 if swap.heads else heads
    log_shape = shape(8 * pl.cdiv(heads, 8), tokens)
    factors, *summaries = pl.pallas_call(
        functools.partial(summary_kernel, swap=swap.heads),
        in_specs=[HBM] * 4,
        out_specs=[HBM] + [VMEM] * sent,
        out_shape=[shape(heads + 1, tokens, DK + DV)] + [shape(DK, DK + DV)] * sent,
        scratch_shapes=buffers(decays, strengths, key_vectors, values)
        + [pltpu.VMEM(factor_shape.shape, jnp.float32), pltpu.VMEM((heads, DK, DK + DV), jnp.float32)]
        + [pltpu.VMEM(log_shape.shape, jnp.float32), pltpu.SemaphoreType.DMA((groups + 2,))],
        compiler_params=params(MOST_VMEM),
        name="state_summary",
    )(decays, strengths, key_vectors, values)
    maps, own = pl.pallas_call(
        output_kernel,
        in_specs=[HBM] * 3,
        out_specs=[HBM, VMEM],
        out_shape=[shape(8 * heads, tokens, DK + DV), shape(DK, DK + DV)],
        scratch_shapes=[pltpu.VMEM(a.shape, jnp.float32) for a in (log_shape, queries, key_vectors)]
        + [pltpu.VMEM(factor_shape.shape, jnp.float32), pltpu.SemaphoreType.DMA((4 + key_heads,))]
        + [pltpu.VMEM(factor_shape.shape, jnp.float32), pltpu.SemaphoreType.DMA((key_heads,))],
        compiler_params=params(MAP_VMEM),
        cost_estimate=cost(3 * 2 * heads * tokens * tokens * 384, factors, factors, queries),
        name="output_maps",
    )(queries, key_vectors, factors)
    states, maps, weights = entering_states(own, summaries, swap.heads, maps, out_weight)
    parts_shape = jax.ShapeDtypeStruct((2, depth, columns), jnp.bfloat16)

    fetched = [
        pltpu.VMEM(out_weight.shape, jnp.float32),
        pltpu.SemaphoreType.DMA((depth // WEIGHT_ROWS,)),
    ]

    def project(pieces, vmem, parts=None):
        total = len({piece[0] for piece in pieces}) * rows
        normed = pltpu.VMEM((total, depth), jnp.bfloat16)
        counts = (total // rows, heads * total // rows)
        return pl.pallas_call(
            functools.partial(
                projection_kernel,
                pieces=[(index, start) for index, start, _ in pieces],
                split_here=parts is None,
                swap=swap,
            ),
            in_specs=[HBM] * 2 + [VMEM, HBM if parts is None else VMEM] + [VMEM] * heads,
            out_shape=[shape(rows, width) for _, _, width in pieces]
            + [parts_shape] * (parts is None),
            scratch_shapes=[
                pltpu.VMEM((heads, total, DK + DV), jnp.float32),
                pltpu.VMEM((total, heads * DV), jnp.float32),
                pltpu.VMEM((heads, DK, DV), jnp.float32),
                normed,
                normed,
            ]
            + [pltpu.SemaphoreType.DMA((n,)) for n in counts]
            + fetched * (parts is None),
            compiler_params=params(vmem),
            cost_estimate=cost(3 * 2 * total * depth * columns, out_weight),
            name="projection",
        )(maps, out_gate, gain, weights if parts is None else parts, *states)

    return project_and_sum(project, columns, "tp")


def solution(mesh):
    return jax.shard_map(
        per_device,
        mesh=mesh,
        in_specs=(
            P("ctx", "tp"),
            P("ctx", "tp"),
            P("ctx", "tp"),
            P("tp", "ctx"),
            P("tp", "ctx"),
            P("ctx", "tp"),
            P(),
            P("tp", None),
        ),
        out_specs=P(("ctx", "tp"), None),
        check_vma=False,
    )
```
